128 devices in a mesh: block: 32 (over y, x, core), view: 4 (over z).
Axes of the slice: x: 4, y: 4, z: 4, core: 2. Of those that a mesh axis runs over, the one named last changes fastest.
Arguments:
- estimate: float32 [256, 256, 256], P('block'), may hold values from 0.5 to 2
- tiles: float32 [4, 1024, 2, 128, 128], P('view', 'block'), may hold values from 0.25 to 4
- tile_block: int32 [4, 1024, 1], P('view', 'block'), may hold values from 0 to 31; in each aligned block of 32 rows (0 to 31, 32 to 63, ..., all dimensions but the last counted through in order) at most 2 rows name the same one
- tile_view: int32 [4, 1024], P('view', 'block'), may hold values from 0 to 1
- tile_slot: int32 [4, 1024], P('view', 'block'), may hold values from 0 to 15
- widths: float32 [3, 8], P(None, 'view'), may hold values from 0.6 to 2
Outputs:
- deconvolved: float32 [256, 256, 256], P('block')
The draws below stay inside these ranges and needn't reach their ends.
Inputs may be any that keep to these rules, and one draw needn't show every extreme that they name: `tile_block`: among the 32 tiles of one device at most 2 lie in one slab, and some slab holds exactly 2 of them. tile_slot = 4 * zt + 2 * ty + tx with zt the depth position in units of 2 planes and ty, tx the lateral offsets in units of 128 voxels.
All inputs are finite; a program needn't handle non-finite values.
Results may differ from the reference program's by a relative error of at most 0.0003.
Values sent between devices are 32-bit elements; how exact they have to be, the bound alone decides.
No kernel may reach another device: no remote copies, remote signals or barrier semaphores. Data moves between devices by JAX's collectives and lax.ppermute only.
A program may use at most 128 MiB of HBM per device.

```python
import math
import jax
import jax.numpy as jnp
import numpy as np
from jax import lax

TZ = 2
TILE_DEV = 32
TYX = 128
RAD = 3
VIEW_DEV = 2
ITERS = 2
VIEWS = 8
NYX = 256
NZ = 256
ZT = 4
TILES = 1024
CAP = 2
N_BLOCK = 32
N_VIEW = 4


def place_ends(values, stream_key, least, largest):
    index_at = [jax.random.randint(jax.random.fold_in(stream_key, axis), (), 0, length) for axis, length in enumerate(values.shape)]
    longest = values.shape.index(max(values.shape))
    neighbour = index_at[:longest] + [(index_at[longest] + 1) % values.shape[longest]] + index_at[longest + 1:]
    return values.at[tuple(index_at)].set(least).at[tuple(neighbour)].set(largest)


def shard_levels(key, shape, shards, least, high):
    level, own = 1.0, jax.random.fold_in(key, 6)
    for position, blocks in shards:
        steps = jnp.exp(jax.random.uniform(jax.random.fold_in(own, position), (blocks,), jnp.float32, least / len(shards), high / len(shards)))
        level = level * jnp.repeat(steps, shape[position] // blocks).reshape([-1 if axis == position else 1 for axis in range(len(shape))])
    return level


def routed_block(rng, own, number, rows, number_of, top, limit, skew):
    order = jax.random.permutation(rng, number_of)
    heavy_load, common = load_shares(number_of, rows * top, limit, skew, True), load_shares(number_of, rows * top, limit, skew, False)
    places = jnp.arange(number_of)

    def named(sizes, offset_by):
        used = int((sizes > 0).sum())
        fixed = max(1, used // 4)
        shifted = fixed + (places - fixed + offset_by * (used - fixed)) % max(1, number_of - fixed)
        return jnp.zeros((number_of,), jnp.int32).at[order[jnp.where(places < fixed, places, shifted)]].set(jnp.asarray(sizes, jnp.int32))

    sizes = jnp.where(number % 4 == 0, named(heavy_load, number // 4), named(common, number - number // 4 - 1))
    mixed = jax.random.permutation(jax.random.fold_in(own, 3), number_of)
    donor, receiver = mixed[0:number_of // 2 * 2:2], mixed[1:number_of // 2 * 2:2]
    margin = jnp.minimum(sizes[donor] - 1, limit - sizes[receiver]) // 2
    margin = jnp.where((donor == order[0]) | (receiver == order[0]) | (sizes[receiver] == 0), 0, jnp.maximum(margin, 0))
    shifted = jax.random.randint(jax.random.fold_in(own, 4), (number_of // 2,), 0, 1 << 20) % (margin + 1)
    sizes = sizes.at[donor].add(-shifted).at[receiver].add(shifted)
    members = jnp.searchsorted(jnp.cumsum(sizes), jnp.arange(rows * top), side="right").astype(jnp.int32)
    listing = members.reshape(top, rows).T
    listing = listing[jax.random.permutation(jax.random.fold_in(own, 1), rows)]
    offset_by = jax.random.randint(jax.random.fold_in(own, 2), (rows, 1), 0, top)
    return jnp.take_along_axis(listing, (jnp.arange(top)[None, :] + offset_by) % top, axis=1)


def load_shares(amount, total, most, slope, full):
    portions = [(1 << 20) // math.isqrt(standing ** slope) + 1 for standing in range(1, amount + 1)]
    largest = most if full else min(most, max(-(-total // amount), total * portions[0] // sum(portions)))
    least = 1 if total - largest >= amount - 1 else 0
    given, rest = [largest] + [least] * (amount - 1), total - largest - least * (amount - 1)
    while rest > 0:
        candidates = [i for i in range(1, amount) if given[i] < largest] or [i for i in range(1, amount) if given[i] < most]
        mass, remaining = sum([portions[i] for i in candidates]), rest
        for i in candidates:
            addition = min(most - given[i], max(1, remaining * portions[i] // mass), rest)
            given[i] = given[i] + addition
            rest = rest - addition
    return np.array(given)


def setup_inputs(seed: int = 0) -> dict:
    key_list = jax.random.split(jax.random.key(seed), 7)
    estimate = jnp.clip(jnp.exp(math.log(2.0) - 1.3862944 * jax.random.uniform(key_list[0], (NZ, NYX, NYX), jnp.float32) ** shard_levels(key_list[0], (NZ, NYX, NYX), ((0, 32),), -0.2, 0.2)), 0.5, 2.0)
    tiles = jnp.clip(jnp.exp(math.log(4.0) - 2.7725887 * jax.random.uniform(key_list[1], (N_VIEW, TILES, TZ, TYX, TYX), jnp.float32) ** shard_levels(key_list[1], (N_VIEW, TILES, TZ, TYX, TYX), ((0, 4), (1, 32)), -0.2, 0.2)), 0.25, 4.0)
    tile_block_keys = jax.random.split(jax.random.fold_in(key_list[2], 1), N_VIEW * TILES // TILE_DEV)
    tile_block_turns = jax.random.permutation(jax.random.fold_in(key_list[2], 3), N_VIEW * TILES // TILE_DEV)
    tile_block = jax.vmap(lambda own, number: routed_block(jax.random.fold_in(key_list[2], 2), own, number, TILE_DEV, N_BLOCK, 1, CAP, 2))(tile_block_keys, tile_block_turns).reshape((N_VIEW, TILES, 1))
    tile_view = place_ends(jax.random.randint(key_list[3], (N_VIEW, TILES), 0, VIEW_DEV), jax.random.fold_in(key_list[3], 1), 0, VIEW_DEV - 1).astype(jnp.int32)
    tile_slot = place_ends(jax.random.randint(key_list[4], (N_VIEW, TILES), 0, 4 * ZT), jax.random.fold_in(key_list[4], 1), 0, (4 * ZT) - 1).astype(jnp.int32)
    widths = jnp.clip(jnp.exp(math.log(2.0) - 1.2039728 * jax.random.uniform(key_list[5], (3, VIEWS), jnp.float32) ** shard_levels(key_list[5], (3, VIEWS), ((1, 4),), -0.2, 0.2)), 0.6, 2.0)
    return {"estimate": estimate, "tiles": tiles, "tile_block": tile_block, "tile_view": tile_view, "tile_slot": tile_slot, "widths": widths}


highest = lax.Precision.HIGHEST


def kernel_taps(spread):
    offsets = jnp.arange(-RAD, RAD + 1).astype(jnp.float32)
    raw = jnp.exp(-offsets * offsets / (2.0 * spread * spread))
    return raw / jnp.sum(raw)


def band_matrix(spread, extent):
    row_ids = jnp.arange(extent)[:, None]
    col_ids = jnp.arange(extent)[None, :]
    apart = (col_ids - row_ids).astype(jnp.float32)
    offsets = jnp.arange(-RAD, RAD + 1).astype(jnp.float32)
    norm = jnp.sum(jnp.exp(-offsets * offsets / (2.0 * spread * spread)))
    inside = jnp.abs(col_ids - row_ids) <= RAD
    return jnp.where(inside, jnp.exp(-apart * apart / (2.0 * spread * spread)) / norm, 0.0)


def blur(padded, spreads, planes):
    taps = kernel_taps(spreads[0])
    along_depth = taps[0] * padded[0:planes]
    for offset in range(1, 2 * RAD + 1):
        along_depth = along_depth + taps[offset] * padded[offset:offset + planes]
    extent = padded.shape[1]
    across = jnp.einsum('zyx,yw->zwx', along_depth, band_matrix(spreads[1], extent), precision=highest)
    return jnp.einsum('zyx,xw->zyw', across, band_matrix(spreads[2], extent), precision=highest)


def rimmed(volume):
    return jnp.pad(volume, ((RAD, RAD), (0, 0), (0, 0)))


def reference(estimate, tiles, tile_block, tile_view, tile_slot, widths):
    flattened = tiles.reshape(N_VIEW * TILES, TZ * TYX * TYX)
    groups = jnp.arange(N_VIEW).astype(jnp.int32)[:, None]
    view_ids = groups * VIEW_DEV + tile_view
    segment_ids = ((view_ids * N_BLOCK + tile_block[:, :, 0]) * (4 * ZT) + tile_slot).reshape(-1).astype(jnp.int32)
    segments = VIEWS * N_BLOCK * 4 * ZT
    summed = jax.ops.segment_sum(flattened, segment_ids, num_segments=segments)
    counts = jax.ops.segment_sum(jnp.ones(segment_ids.shape, jnp.float32), segment_ids, num_segments=segments)
    placed = summed / jnp.maximum(counts, 1.0)[:, None]
    observed = placed.reshape(VIEWS, N_BLOCK, ZT, 2, 2, TZ, TYX, TYX)
    observed = observed.transpose(0, 1, 2, 5, 3, 6, 4, 7).reshape(VIEWS, NZ, NYX, NYX)
    coverage = jnp.zeros((NZ, NYX, NYX), jnp.float32)
    for view_id in range(VIEWS):
        seen_mask = (observed[view_id] > 0.0).astype(jnp.float32)
        coverage = coverage + blur(rimmed(seen_mask), widths[:, view_id], NZ)
    current = estimate
    for sweep in range(ITERS):
        totals = jnp.zeros((NZ, NYX, NYX), jnp.float32)
        for view_id in range(VIEWS):
            blurred = blur(rimmed(current), widths[:, view_id], NZ)
            ratios = observed[view_id] / blurred
            totals = totals + blur(rimmed(ratios), widths[:, view_id], NZ)
        current = current * (1.0 + totals) / (1.0 + coverage)
    return current
```

```python
import jax
import jax.numpy as jnp
import numpy as np
from jax import lax
from jax.experimental import pallas as pl
from jax.experimental.pallas import tpu as pltpu
from jax.sharding import PartitionSpec as P

RAD = 3
ITERS = 2
ALL = ("block", "view")
PR, PC = 16, 8
SR, SC = 8, 16
LAT = SR * SC
HALO_PAD = 256
EXT = LAT + HALO_PAD
LIMIT = 50 << 20
F32, BF16 = jnp.float32, jnp.bfloat16

DIRS = [(0, -1), (0, 1), (-1, 0), (1, 0), (-1, -1), (-1, 1), (1, -1), (1, 1)]


def part_range(step, size):
    if step < 0:
        return list(range(-RAD, 0))
    if step > 0:
        return list(range(size, size + RAD))
    return list(range(size))


PARTS = [[(dr, dc) for dr in part_range(er, SR) for dc in part_range(ec, SC)] for er, ec in DIRS]
SIZES = [len(part) for part in PARTS]
HALO_AT = [sum(SIZES[:n]) for n in range(8)]
EXT_POS = [(s, j) for s in range(SR) for j in range(SC)] + [pos for part in PARTS for pos in part]
EXT_POS = EXT_POS + [(1000, 1000)] * (EXT - len(EXT_POS))


def device_of(r, c):
    r, c = r % PR, c % PC
    return ((r // 4) * 8 + c) * 4 + r % 4


def towards(er, ec):
    return [(device_of(r, c), device_of(r + er, c + ec)) for r in range(PR) for c in range(PC)]


def lane_table():
    main = [[-1] * 128 for _ in range(4)]
    aux = [[[-1] * 128 for _ in range(6)] for _ in range(2)]
    for n in range(8):
        for lane in range(4 * SIZES[n]):
            if n < 4 and lane < 128:
                main[n][lane] = (n, lane)
            else:
                for p in range(2):
                    if n < 4:
                        aux[p][n - 2][p * 64 + lane - 128] = (n, lane)
                    else:
                        aux[p][n - 2][p * 36 + lane] = (n, lane)
    return [x for row in main for x in row] + [x for kind in aux for row in kind for x in row]


LANES = lane_table()
LANE_N = np.array([0 if x == -1 else x[0] for x in LANES])
LANE_Q = np.array([-100 if x == -1 else x[1] // SIZES[x[0]] for x in LANES])
LANE_HALO = np.array([0 if x == -1 else HALO_AT[x[0]] + x[1] % SIZES[x[0]] for x in LANES])
LANE_OWN = np.array(
    [
        -1
        if x == -1
        else (x[1] // SIZES[x[0]]) * LAT
        + (PARTS[x[0]][x[1] % SIZES[x[0]]][0] % SR) * SC
        + PARTS[x[0]][x[1] % SIZES[x[0]]][1] % SC
        for x in LANES
    ]
)
ER = np.array([d[0] for d in DIRS])[LANE_N]
EC = np.array([d[1] for d in DIRS])[LANE_N]
N_MAIN, N_AUX = 512, 768


def params(**kw):
    return pltpu.CompilerParams(vmem_limit_bytes=LIMIT, **kw)


def turn(rows):
    chunk = lax.broadcasted_iota(jnp.int32, rows[0].shape, 1) // SC
    for k in (4, 2, 1):
        low = (chunk & k) == 0
        after = list(rows)
        for a in range(8):
            if a & k == 0:
                x, y = rows[a], rows[a | k]
                after[a] = jnp.where(low, x, pltpu.roll(y, SC * k, 1))
                after[a | k] = jnp.where(low, pltpu.roll(x, 128 - SC * k, 1), y)
        rows = after
    return rows


def split(x):
    high = x.astype(BF16)
    return high, (x - high.astype(F32)).astype(BF16)


def dot(a, b):
    return jnp.dot(a, b, preferred_element_type=F32)


def dot_t(a, b):
    return lax.dot_general(a, b, (((1,), (1,)), ((), ())), preferred_element_type=F32)


def send_kernel(view_ref, tiles_ref, left_ref, right_ref, meta_ref, out_ref):
    tiles = tiles_ref.reshape(512, 128)
    for p in range(2):
        rows = turn([tiles[pl.ds(p * 8 + s, 32, stride=16), :] for s in range(8)])
        for c in range(8):
            out_ref[0, c, 0, p * 32 : p * 32 + 32, :] = rows[c]
    left, right = left_ref.reshape(32, 128), right_ref.reshape(32, 128)
    rows = turn(
        [
            jnp.concatenate([left[pl.ds(s, 4, stride=8), :], right[pl.ds(s, 4, stride=8), :]], axis=0)
            for s in range(8)
        ]
    )
    for c in range(8):
        out_ref[0, c, 0, 64:72, :] = rows[c]
        out_ref[0, c, 0, 72:80, :] = meta_ref[...]


def make_message(view, tiles, estimate, meta):
    out = pl.pallas_call(
        send_kernel,
        grid_spec=pltpu.PrefetchScalarGridSpec(
            num_scalar_prefetch=1,
            grid=(4, 4),
            in_specs=[
                pl.BlockSpec((32, 2, 8, 128), lambda y, z, v: (0, 0, y * 4 + z, 0)),
                pl.BlockSpec((2, 2, 1, 8, 128), lambda y, z, v: (v[0], 0, y * 4 + z, 0, 0)),
                pl.BlockSpec((2, 2, 1, 8, 128), lambda y, z, v: (v[0], 0, y * 4 + z, 0, 1)),
                pl.BlockSpec((8, 128), lambda y, z, v: (0, 0)),
            ],
            out_specs=pl.BlockSpec((1, 8, 1, 80, 128), lambda y, z, v: (y, 0, z, 0, 0)),
        ),
        out_shape=jax.ShapeDtypeStruct((4, 8, 4, 80, 128), F32),
        compiler_params=params(),
        name="make_message",
    )(view, tiles, estimate.reshape(8, 2, 16, 8, 256), estimate.reshape(8, 2, 16, 8, 256), meta)
    return out.reshape(128, 80, 128)


def pack_own(x, pick_ref, outs):
    high, low = split(x)
    main = dot(high, pick_ref[:, :N_MAIN]) + dot(low, pick_ref[:, :N_MAIN])
    aux = jnp.zeros((128, N_AUX), F32)
    for p in range(2):
        pick = pick_ref[:, N_MAIN + p * N_AUX : N_MAIN + (p + 1) * N_AUX]
        aux = aux + dot(high[p * 128 : p * 128 + 128], pick) + dot(low[p * 128 : p * 128 + 128], pick)
    put_messages(main, aux, outs)


def put_messages(main, aux, outs):
    for n in range(4):
        outs[n][0:256, :] = main[:, n * 128 : n * 128 + 128]
        if n >= 2:
            outs[n][256:384, :] = aux[:, (n - 2) * 128 : (n - 2) * 128 + 128]
    for n in range(4, 8):
        outs[n][...] = aux[:, (n - 2) * 128 : (n - 2) * 128 + 128]


def take_messages(parts):
    main = jnp.concatenate([parts[n][0:256, :] for n in range(4)], axis=1)
    aux = jnp.concatenate([parts[n][256:384, :] for n in (2, 3)] + [parts[n][...] for n in range(4, 8)], axis=1)
    return split(main), split(aux)


MESSAGES = [jax.ShapeDtypeStruct((rows, 128), F32) for rows in (256, 256, 384, 384, 128, 128, 128, 128)]


def add_messages(parts, pick_ref, base):
    (mh, ml), (ah, al) = take_messages(parts)
    out = []
    for p in range(2):
        rows = slice(p * 128, p * 128 + 128)
        pick = pick_ref[:, N_MAIN + p * N_AUX : N_MAIN + (p + 1) * N_AUX]
        term = dot_t(mh[rows], pick_ref[:, :N_MAIN]) + dot_t(ml[rows], pick_ref[:, :N_MAIN])
        term = term + dot_t(ah, pick) + dot_t(al, pick)
        out.append(term + jnp.concatenate([base[q, rows, :] for q in range(4)], axis=1))
    return out


def begin_kernel(got_ref, pick_ref, cur_ref, *outs):
    got = got_ref.reshape(128 * 16, 128)
    for q in range(4):
        for p in range(2):
            row = (q % 2) * 4 + p * 2 + q // 2
            cur_ref[q, p * 128 : p * 128 + 128, :] = got[pl.ds(row, 128, stride=16), :]
    pack_own(jnp.concatenate([cur_ref[q] for q in range(4)], axis=1), pick_ref, outs)


def begin(got, pick):
    return pl.pallas_call(
        begin_kernel,
        grid=(1,),
        in_specs=[
            pl.BlockSpec((128, 16, 128), lambda i: (0, 4, 0)),
            pl.BlockSpec((512, N_MAIN + 2 * N_AUX), lambda i: (0, 0)),
        ],
        out_specs=[pl.BlockSpec((4, 256, 128), lambda i: (0, 0, 0))]
        + [pl.BlockSpec(m.shape, lambda i: (0, 0)) for m in MESSAGES],
        out_shape=[jax.ShapeDtypeStruct((4, 256, 128), F32)] + MESSAGES,
        compiler_params=params(),
        name="begin",
    )(got, pick)


def weight_kernel(taps_ref, er_ref, ec_ref, bh_ref, bl_ref, wh_ref, wl_ref):
    def from_taps(apart, axis, w):
        far = jnp.abs(apart)
        out = jnp.zeros(apart.shape, F32)
        for k in range(RAD + 1):
            out = jnp.where(far == k, taps_ref[axis, w, k], out)
        return out

    def plane(dim):
        place = lax.broadcasted_iota(jnp.int32, (256, 256), dim)
        return 2 * (place % 128) + place // 128

    lanes = lax.broadcasted_iota(jnp.int32, (EXT, LAT), 1)
    down = er_ref[...] - lanes // SC
    across = ec_ref[...] - lanes % SC
    depth = plane(0) - plane(1)
    for w in range(8):
        bh_ref[w], bl_ref[w] = split(from_taps(depth, 0, w))
        high, low = split(from_taps(down, 1, w) * from_taps(across, 2, w))
        lanes_w = slice((w % 2) * LAT, (w % 2) * LAT + LAT)
        wh_ref[w // 2, :, lanes_w] = high
        wl_ref[w // 2, :, lanes_w] = low


def make_weights(taps):
    er = np.broadcast_to(np.array([d[0] for d in EXT_POS], np.int32)[:, None], (EXT, LAT))
    ec = np.broadcast_to(np.array([d[1] for d in EXT_POS], np.int32)[:, None], (EXT, LAT))
    whole = pl.BlockSpec(memory_space=pltpu.VMEM)
    return pl.pallas_call(
        weight_kernel,
        in_specs=[pl.BlockSpec(memory_space=pltpu.SMEM), whole, whole],
        out_specs=[whole] * 4,
        out_shape=[jax.ShapeDtypeStruct((8, 256, 256), BF16)] * 2
        + [jax.ShapeDtypeStruct((4, EXT, 2 * LAT), BF16)] * 2,
        compiler_params=params(),
        name="make_weights",
    )(taps, er, ec)


def observe_kernel(got_ref, place_ref, obs_ref):
    sides = []
    for p in range(2):
        sides.append(got_ref[:, 0, p * 32 : p * 32 + 32, :].reshape(1024, 128))
    high, low = split(jnp.concatenate(sides, axis=1))
    place = place_ref[0, 0:1, :]
    for half in range(4):
        rows = lax.broadcasted_iota(jnp.int32, (256, 1024), 0) + half * 256
        hot = (rows.astype(F32) == place).astype(F32)
        counts = jnp.sum(hot, axis=1, keepdims=True)
        hot = hot.astype(BF16)
        mean = (dot(hot, high) + dot(hot, low)) / jnp.maximum(counts, 1.0)
        for i in range(2):
            for p in range(2):
                obs_ref[half // 2, (half % 2) * 2 + i, p * 128 : p * 128 + 128, :] = mean[
                    i * 128 : i * 128 + 128, p * 128 : p * 128 + 128
                ]


def observe(got, places):
    return pl.pallas_call(
        observe_kernel,
        grid=(4,),
        in_specs=[
            pl.BlockSpec((32, 1, 64, 128), lambda g: (0, g, 0, 0)),
            pl.BlockSpec((1, 1, 1024), lambda g: (g, 0, 0)),
        ],
        out_specs=pl.BlockSpec((2, 4, 256, 128), lambda g: (g, 0, 0, 0)),
        out_shape=jax.ShapeDtypeStruct((8, 4, 256, 128), F32),
        compiler_params=params(),
        cost_estimate=pl.CostEstimate(flops=4 << 30, bytes_accessed=8 << 20, transcendentals=0),
        name="observe",
    )(got.reshape(32, 4, 80, 128), places)


def quads(x):
    return jnp.concatenate([x[q] for q in range(4)], axis=1)


def back_project(pair_of, bh_ref, bl_ref, wh_ref, wl_ref, total):
    def step(pair, carry):
        sides = []
        for i in range(2):
            w = 2 * pair + i
            x = pair_of(pair, i)
            if x.dtype == BF16:
                sides.append(dot(bh_ref[w], x) + dot(bl_ref[w], x))
            else:
                high, low = split(x)
                sides.append(dot(bh_ref[w], high) + dot(bh_ref[w], low) + dot(bl_ref[w], high))
        rows = []
        for q in range(4):
            lanes = slice(q * LAT, q * LAT + LAT)
            rows.append(jnp.concatenate([side[:, lanes] for side in sides], axis=1))
        high, low = split(jnp.concatenate(rows, axis=0))
        wh, wl = wh_ref[pair], wl_ref[pair]
        term = dot_t(high, wh) + dot_t(low, wh) + dot_t(high, wl)

        @pl.when(pair == 0)
        def _():
            total[...] = term

        @pl.when(pair > 0)
        def _():
            total[...] += term

        return carry

    lax.fori_loop(0, 4, step, 0)


def finish_back(total, place_ref, own_ref, outs):
    for q in range(4):
        own_ref[q] = total[q * 256 : q * 256 + 256, :LAT]
    high, low = split(jnp.concatenate([total[q * 256 : q * 256 + 256, LAT:] for q in range(4)], axis=1))
    main_at = place_ref[0:N_MAIN, :]
    main = dot_t(high, main_at) + dot_t(low, main_at)
    aux = jnp.zeros((128, N_AUX), F32)
    for p in range(2):
        at = place_ref[N_MAIN + p * N_AUX : N_MAIN + (p + 1) * N_AUX, :]
        rows = slice(p * 128, p * 128 + 128)
        aux = aux + dot_t(high[rows], at) + dot_t(low[rows], at)
    put_messages(main, aux, outs)


def cover_kernel(obs_ref, bh_ref, bl_ref, wh_ref, wl_ref, place_ref, own_ref, *rest):
    outs, total = rest[:8], rest[8]

    def seen(pair, i):
        return (quads(obs_ref[2 * pair + i]) > 0.0).astype(F32).astype(BF16)

    back_project(seen, bh_ref, bl_ref, wh_ref, wl_ref, total)
    finish_back(total, place_ref, own_ref, outs)


def cover(obs, weights, place):
    whole = pl.BlockSpec(memory_space=pltpu.VMEM)
    return pl.pallas_call(
        cover_kernel,
        in_specs=[whole] * 6,
        out_specs=[whole] * 9,
        out_shape=[jax.ShapeDtypeStruct((4, 256, LAT), F32)] + MESSAGES,
        scratch_shapes=[pltpu.VMEM((1024, EXT), F32)],
        compiler_params=params(),
        cost_estimate=pl.CostEstimate(flops=6 << 30, bytes_accessed=8 << 20, transcendentals=0),
        name="cover",
    )(obs, *weights, place)


def sweep_kernel(*refs):
    obs_ref, bh_ref, bl_ref, wh_ref, wl_ref, place_ref, cur_ref = refs[:7]
    parts, own_ref, outs = refs[7:15], refs[15], refs[16:24]
    total, high_ref, low_ref = refs[24:]
    (mh, ml), (ah, al) = take_messages(parts)
    for p in range(2):
        rows = slice(p * 128, p * 128 + 128)
        at = place_ref[N_MAIN + p * N_AUX : N_MAIN + (p + 1) * N_AUX, :]
        main_at = place_ref[0:N_MAIN, :]
        halo = dot(mh[rows], main_at) + dot(ml[rows], main_at) + dot(ah, at) + dot(al, at)
        for q in range(4):
            high, low = split(halo[:, q * HALO_PAD : (q + 1) * HALO_PAD])
            to = slice(q * 256 + p * 128, q * 256 + p * 128 + 128)
            high_ref[to, LAT:], low_ref[to, LAT:] = high, low
    for q in range(4):
        high_ref[q * 256 : q * 256 + 256, :LAT], low_ref[q * 256 : q * 256 + 256, :LAT] = split(cur_ref[q])
    blurred = total

    def ratios(pair, i):
        if i == 0:
            wh, wl = wh_ref[pair], wl_ref[pair]
            high, low = high_ref[...], low_ref[...]
            ratios.side = dot(high, wh) + dot(low, wh) + dot(high, wl)
        side = ratios.side[:, i * LAT : i * LAT + LAT]
        high, low = split(jnp.concatenate([side[q * 256 : q * 256 + 256] for q in range(4)], axis=1))
        w = 2 * pair + i
        blur = dot(bh_ref[w], high) + dot(bh_ref[w], low) + dot(bl_ref[w], high)
        return quads(obs_ref[w]) / blur

    back_project(ratios, bh_ref, bl_ref, wh_ref, wl_ref, total)
    finish_back(total, place_ref, own_ref, outs)


def sweep(obs, weights, place, cur, parts):
    whole = pl.BlockSpec(memory_space=pltpu.VMEM)
    return pl.pallas_call(
        sweep_kernel,
        in_specs=[whole] * 15,
        out_specs=[whole] * 9,
        out_shape=[jax.ShapeDtypeStruct((4, 256, LAT), F32)] + MESSAGES,
        scratch_shapes=[
            pltpu.VMEM((1024, EXT), F32),
            pltpu.VMEM((1024, EXT), BF16),
            pltpu.VMEM((1024, EXT), BF16),
        ],
        compiler_params=params(),
        cost_estimate=pl.CostEstimate(flops=12 << 30, bytes_accessed=12 << 20, transcendentals=0),
        name="sweep",
    )(obs, *weights, place, cur, *parts)


def update_kernel(*refs):
    cur_ref, pick_ref, total_ref, cover_ref = refs[:4]
    totals, covers = refs[4:12], refs[12:20]
    cur_out, below_out, outs = refs[20], refs[21], refs[22:30]
    total = add_messages(totals, pick_ref, total_ref)
    cover = add_messages(covers, pick_ref, cover_ref)
    sides = []
    for p in range(2):
        rows = slice(p * 128, p * 128 + 128)
        below = 1.0 + cover[p]
        cur = jnp.concatenate([cur_ref[q, rows, :] for q in range(4)], axis=1)
        cur = cur * (1.0 + total[p]) / below
        for q in range(4):
            cur_out[q, rows, :] = cur[:, q * LAT : q * LAT + LAT]
            below_out[q, rows, :] = below[:, q * LAT : q * LAT + LAT]
        sides.append(cur)
    pack_own(jnp.concatenate(sides, axis=0), pick_ref, outs)


def update(cur, pick, total, cover):
    whole = pl.BlockSpec(memory_space=pltpu.VMEM)
    return pl.pallas_call(
        update_kernel,
        in_specs=[whole] * 20,
        out_specs=[whole] * 10,
        out_shape=[jax.ShapeDtypeStruct((4, 256, LAT), F32)] * 2 + MESSAGES,
        compiler_params=params(),
        name="update",
    )(cur, pick, total[0], cover[0], *total[1:], *cover[1:])


def last_kernel(*refs):
    cur_ref, pick_ref, total_ref, below_ref = refs[:4]
    totals, out_ref, rows_ref = refs[4:12], refs[12], refs[13]
    total = add_messages(totals, pick_ref, total_ref)
    for p in range(2):
        rows = slice(p * 128, p * 128 + 128)
        for q in range(4):
            mine = total[p][:, q * LAT : q * LAT + LAT]
            rows_ref[pl.ds(p * 4 + q, 128, stride=8), :] = (
                cur_ref[q, rows, :] * (1.0 + mine) / below_ref[q, rows, :]
            )
    done = rows_ref[...].reshape(32, 32, 128)
    for v in range(4):
        out_ref[:, v] = done


def last_update(cur, pick, total, below):
    whole = pl.BlockSpec(memory_space=pltpu.VMEM)
    out = pl.pallas_call(
        last_kernel,
        in_specs=[whole] * 12,
        out_specs=whole,
        out_shape=jax.ShapeDtypeStruct((32, 4, 32, 128), F32),
        scratch_shapes=[pltpu.VMEM((1024, 128), F32)],
        compiler_params=params(),
        name="last_update",
    )(cur, pick, total[0], below, *total[1:])
    return out.reshape(128, 32, 128)


def place_kernel(got_ref, out_ref, side_ref):
    got = got_ref.reshape(8 * 32, 128)
    for tx in range(2):
        rows = turn([got[pl.ds(c * 32 + tx, 16, stride=2), :] for c in range(8)])
        for s in range(8):
            side_ref[pl.ds(tx * 128 + s, 16, stride=8), :] = rows[s]
        lanes = slice(tx * 128, tx * 128 + 128)
        out_ref[:, :, 0, :, lanes] = side_ref[tx * 128 : tx * 128 + 128, :].reshape(8, 2, 8, 128)


def place_output(got):
    out = pl.pallas_call(
        place_kernel,
        grid=(4, 4),
        in_specs=[pl.BlockSpec((1, 8, 1, 32, 128), lambda y, z: (y, 0, z, 0, 0))],
        out_specs=pl.BlockSpec((8, 2, 1, 8, 256), lambda y, z: (0, 0, y * 4 + z, 0, 0)),
        out_shape=jax.ShapeDtypeStruct((8, 2, 16, 8, 256), F32),
        scratch_shapes=[pltpu.VMEM((256, 128), F32)],
        compiler_params=params(),
        name="place_output",
    )(got.reshape(4, 8, 4, 32, 128))
    return out.reshape(8, 256, 256)


def gather_parts(parts):
    return [lax.ppermute(x, ALL, towards(-er, -ec)) for x, (er, ec) in zip(parts, DIRS, strict=True)]


def reduce_parts(parts):
    return [lax.ppermute(x, ALL, towards(er, ec)) for x, (er, ec) in zip(parts, DIRS, strict=True)]


def on_device(estimate, tiles, tile_block, tile_view, tile_slot, widths):
    block, view = lax.axis_index("block"), lax.axis_index("view")
    r = (block // 8) * 4 + view
    c = block % 8
    slot = tile_slot[0]
    place = tile_view[0] * 512 + (slot % 4) * 128 + tile_block[0, :, 0] * 4 + slot // 4
    meta = jnp.concatenate([place.astype(F32), widths.reshape(6), jnp.zeros((90,), F32)])
    meta = jnp.broadcast_to(meta[None], (8, 128))
    message = make_message(view.reshape(1), tiles[0], estimate, meta)
    got = lax.all_to_all(message, ALL, split_axis=0, concat_axis=0, tiled=True)

    pick = (np.arange(4 * LAT)[:, None] == LANE_OWN[None, :]).astype(BF16)
    wrap_r = ((r + ER < 0) | (r + ER >= PR)).astype(jnp.int32) * ER
    wrap_c = ((c + EC < 0) | (c + EC >= PC)).astype(jnp.int32) * EC
    ty, tx = LANE_Q // 2 - wrap_r, LANE_Q % 2 - wrap_c
    inside = (LANE_Q >= 0) & (ty >= 0) & (ty < 2) & (tx >= 0) & (tx < 2)
    target = jnp.where(inside, (ty * 2 + tx) * HALO_PAD + LANE_HALO, -1)
    placed = (target[:, None] == jnp.arange(4 * HALO_PAD)[None, :]).astype(BF16)

    cur, *sent = begin(got, pick)
    parts = gather_parts(sent)
    row = got[:, 72, :]
    places = row[:, :32].reshape(32, 4, 32).transpose(1, 0, 2).reshape(4, 1, 1024)
    spread = row[0:4, 32:38].reshape(4, 3, 2).transpose(1, 0, 2).reshape(3, 8, 1)
    steps = jnp.arange(RAD + 1).astype(F32)
    raw = jnp.exp(-steps * steps / (2.0 * spread * spread))
    taps = raw / (2.0 * jnp.sum(raw, axis=2, keepdims=True) - raw[:, :, 0:1])
    weights = make_weights(taps)
    obs = observe(got, places)
    own, *sent = cover(obs, weights, placed)
    covered = [own] + reduce_parts(sent)
    own, *sent = sweep(obs, weights, placed, cur, parts)
    total = [own] + reduce_parts(sent)
    cur, below, *sent = update(cur, pick, total, covered)
    parts = gather_parts(sent)
    own, *sent = sweep(obs, weights, placed, cur, parts)
    total = [own] + reduce_parts(sent)
    out = last_update(cur, pick, total, below)
    out = lax.all_to_all(out, ALL, split_axis=0, concat_axis=0, tiled=True)
    return place_output(out)


def solution(mesh):
    placed = (
        P("block", None, None),
        P("view", "block", None, None, None),
        P("view", "block", None),
        P("view", "block"),
        P("view", "block"),
        P(None, "view"),
    )
    return jax.shard_map(
        on_device, mesh=mesh, in_specs=placed, out_specs=P("block", None, None), check_vma=False
    )
```

```python
import jax
import jax.numpy as jnp
import numpy as np
from jax import lax
from jax.experimental import pallas as pl
from jax.experimental.pallas import tpu as pltpu
from jax.sharding import PartitionSpec as P

RAD = 3
ITERS = 2
ALL = ("block", "view")
PR, PC = 16, 8
SR, SC = 8, 16
LAT = SR * SC
HALO_PAD = 256
EXT = LAT + HALO_PAD
F32, BF16 = jnp.float32, jnp.bfloat16

DIRS = [(0, -1), (0, 1), (-1, 0), (1, 0), (-1, -1), (-1, 1), (1, -1), (1, 1)]


def part_range(step, size):
    if step < 0:
        return list(range(-RAD, 0))
    if step > 0:
        return list(range(size, size + RAD))
    return list(range(size))


PARTS = [[(dr, dc) for dr in part_range(er, SR) for dc in part_range(ec, SC)] for er, ec in DIRS]
SIZES = [len(part) for part in PARTS]
HALO_AT = [sum(SIZES[:n]) for n in range(8)]
EXT_POS = [(s, j) for s in range(SR) for j in range(SC)] + [pos for part in PARTS for pos in part]
EXT_POS = EXT_POS + [(1000, 1000)] * (EXT - len(EXT_POS))


def device_of(r, c):
    r, c = r % PR, c % PC
    y, k = r // 4, r % 4
    return (y * 8 + c) * 4 + (k if y % 2 == 0 else 3 - k)


def towards(er, ec):
    return [(device_of(r, c), device_of(r + er, c + ec)) for r in range(PR) for c in range(PC)]


def lane_table():
    main = [[-1] * 128 for _ in range(4)]
    aux = [[[-1] * 128 for _ in range(6)] for _ in range(2)]
    for n in range(8):
        for lane in range(4 * SIZES[n]):
            if n < 4 and lane < 128:
                main[n][lane] = (n, lane)
            else:
                for p in range(2):
                    if n < 4:
                        aux[p][n - 2][p * 64 + lane - 128] = (n, lane)
                    else:
                        aux[p][n - 2][p * 36 + lane] = (n, lane)
    return [x for row in main for x in row] + [x for kind in aux for row in kind for x in row]


LANES = lane_table()
LANE_N = np.array([0 if x == -1 else x[0] for x in LANES])
LANE_Q = np.array([-100 if x == -1 else x[1] // SIZES[x[0]] for x in LANES])
LANE_HALO = np.array([0 if x == -1 else HALO_AT[x[0]] + x[1] % SIZES[x[0]] for x in LANES])
LANE_OWN = np.array(
    [
        -1
        if x == -1
        else (x[1] // SIZES[x[0]]) * LAT
        + (PARTS[x[0]][x[1] % SIZES[x[0]]][0] % SR) * SC
        + PARTS[x[0]][x[1] % SIZES[x[0]]][1] % SC
        for x in LANES
    ]
)
ER = np.array([d[0] for d in DIRS])[LANE_N]
EC = np.array([d[1] for d in DIRS])[LANE_N]
N_MAIN, N_AUX = 512, 768


def params(mib):
    return pltpu.CompilerParams(vmem_limit_bytes=mib << 20)


def turn(rows):
    chunk = lax.broadcasted_iota(jnp.int32, rows[0].shape, 1) // SC
    for k in (4, 2, 1):
        low = (chunk & k) == 0
        after = list(rows)
        for a in range(8):
            if a & k == 0:
                x, y = rows[a], rows[a | k]
                after[a] = jnp.where(low, x, pltpu.roll(y, SC * k, 1))
                after[a | k] = jnp.where(low, pltpu.roll(x, 128 - SC * k, 1), y)
        rows = after
    return rows


def split(x):
    high = x.astype(BF16)
    return high, (x - high.astype(F32)).astype(BF16)


def dot(a, b):
    return jnp.dot(a, b, preferred_element_type=F32)


def send_kernel(view_ref, tiles_ref, left_ref, right_ref, meta_ref, out_ref):
    tiles = tiles_ref.reshape(2048, 128)
    left, right = left_ref.reshape(128, 128), right_ref.reshape(128, 128)
    odd = pl.program_id(0) % 2
    for k in range(4):
        z = jnp.where(odd == 0, k, 3 - k)
        for p in range(2):
            rows = turn([tiles[pl.ds(p * 32 + k * 8 + s, 32, stride=64), :] for s in range(8)])
            for c in range(8):
                out_ref[0, c, z, p * 32 : p * 32 + 32, :] = rows[c]
        rows = []
        for s in range(8):
            at = pl.ds(k * 8 + s, 4, stride=32)
            rows.append(jnp.concatenate([left[at, :], right[at, :]], axis=0))
        rows = turn(rows)
        for c in range(8):
            out_ref[0, c, z, 64:72, :] = rows[c]
            out_ref[0, c, z, 72:80, :] = meta_ref[...]


def make_message(view, tiles, estimate, meta):
    estimate = estimate.reshape(8, 2, 4, 32, 256)
    out = pl.pallas_call(
        send_kernel,
        grid_spec=pltpu.PrefetchScalarGridSpec(
            num_scalar_prefetch=1,
            grid=(4,),
            in_specs=[
                pl.BlockSpec((32, 2, 32, 128), lambda y, v: (0, 0, y, 0)),
                pl.BlockSpec((2, 2, 1, 32, 128), lambda y, v: (v[0], 0, y, 0, 0)),
                pl.BlockSpec((2, 2, 1, 32, 128), lambda y, v: (v[0], 0, y, 0, 1)),
                pl.BlockSpec((8, 128), lambda y, v: (0, 0)),
            ],
            out_specs=pl.BlockSpec((1, 8, 4, 80, 128), lambda y, v: (y, 0, 0, 0, 0)),
        ),
        out_shape=jax.ShapeDtypeStruct((4, 8, 4, 80, 128), F32),
        compiler_params=params(56),
        name="make_message",
    )(view, tiles, estimate, estimate, meta)
    return out.reshape(128, 80, 128)


def stacked(x):
    return jnp.concatenate(split(x), axis=0)


def dot_halves(x, table):
    out = dot(x, table)
    rows = out.shape[0] // 2
    return out[:rows] + out[rows:]


def aux_at(p):
    return slice(N_MAIN + p * N_AUX, N_MAIN + (p + 1) * N_AUX)


def to_messages(x, table_ref, outs):
    main = dot_halves(stacked(x), table_ref[:, :N_MAIN])
    aux = dot_halves(stacked(x[:128]), table_ref[:, aux_at(0)]) + dot_halves(stacked(x[128:]), table_ref[:, aux_at(1)])
    put_messages(main, aux, outs)


def from_messages(parts, table_ref):
    main = jnp.concatenate([parts[n][0:256, :] for n in range(4)], axis=1)
    aux = jnp.concatenate([parts[n][256:384, :] for n in (2, 3)] + [parts[n][...] for n in range(4, 8)], axis=1)
    main = dot_halves(stacked(main), table_ref[:N_MAIN, :])
    aux = stacked(aux)
    return [main[p * 128 : p * 128 + 128] + dot_halves(aux, table_ref[aux_at(p), :]) for p in range(2)]


def put_messages(main, aux, outs):
    for n in range(4):
        outs[n][0:256, :] = main[:, n * 128 : n * 128 + 128]
        if n >= 2:
            outs[n][256:384, :] = aux[:, (n - 2) * 128 : (n - 2) * 128 + 128]
    for n in range(4, 8):
        outs[n][...] = aux[:, (n - 2) * 128 : (n - 2) * 128 + 128]


MESSAGES = [jax.ShapeDtypeStruct((rows, 128), F32) for rows in (256, 256, 384, 384, 128, 128, 128, 128)]


def add_messages(parts, table_ref, base):
    out = []
    for p, term in enumerate(from_messages(parts, table_ref)):
        out.append(term + jnp.concatenate([base[q, p * 128 : p * 128 + 128, :] for q in range(4)], axis=1))
    return out


def quads(x):
    return jnp.concatenate([x[q] for q in range(4)], axis=1)


def begin_kernel(got_ref, pick_ref, cur_ref, *outs):
    got = got_ref.reshape(128 * 16, 128)
    for q in range(4):
        for p in range(2):
            row = (q % 2) * 4 + p * 2 + q // 2
            for m in range(16):
                at = p * 128 + m * 8
                cur_ref[q, at : at + 8, :] = got[pl.ds(m * 16 + row, 8, stride=256), :]
    to_messages(quads(cur_ref), pick_ref, outs)


def begin(got, pick):
    return pl.pallas_call(
        begin_kernel,
        grid=(1,),
        in_specs=[
            pl.BlockSpec((128, 16, 128), lambda i: (0, 4, 0)),
            pl.BlockSpec((512, N_MAIN + 2 * N_AUX), lambda i: (0, 0)),
        ],
        out_specs=[pl.BlockSpec((4, 256, 128), lambda i: (0, 0, 0))]
        + [pl.BlockSpec(m.shape, lambda i: (0, 0)) for m in MESSAGES],
        out_shape=[jax.ShapeDtypeStruct((4, 256, 128), F32)] + MESSAGES,
        compiler_params=params(16),
        name="begin",
    )(got, pick)


def weight_kernel(taps_ref, er_ref, ec_ref, ert_ref, ect_ref, fore_ref, back_ref):
    def from_taps(apart, axis, w):
        far = jnp.abs(apart)
        out = jnp.zeros(apart.shape, F32)
        for k in range(RAD + 1):
            out = jnp.where(far == k, taps_ref[axis, w, k], out)
        return out

    lanes = lax.broadcasted_iota(jnp.int32, (EXT, LAT), 1)
    down, across = er_ref[...] - lanes // SC, ec_ref[...] - lanes % SC
    rows = lax.broadcasted_iota(jnp.int32, (LAT, EXT), 0)
    down_t, across_t = ert_ref[...] - rows // SC, ect_ref[...] - rows % SC
    for w in range(8):
        pair, at = w // 2, slice((w % 2) * LAT, (w % 2) * LAT + LAT)
        high, low = split(from_taps(down, 1, w) * from_taps(across, 2, w))
        for i, x in enumerate((high, high, low)):
            fore_ref[pair, i * EXT : i * EXT + EXT, at] = x
        high, low = split(from_taps(down_t, 1, w) * from_taps(across_t, 2, w))
        for i, x in enumerate((high, high, low)):
            start = i * 2 * LAT + (w % 2) * LAT
            back_ref[pair, start : start + LAT, :] = x


def make_weights(taps):
    ext = np.array(EXT_POS, np.int32)
    tall = [np.broadcast_to(ext[:, i][:, None], (EXT, LAT)) for i in range(2)]
    wide = [np.broadcast_to(ext[:, i][None, :], (LAT, EXT)) for i in range(2)]
    whole = pl.BlockSpec(memory_space=pltpu.VMEM)
    return pl.pallas_call(
        weight_kernel,
        in_specs=[pl.BlockSpec(memory_space=pltpu.SMEM)] + [whole] * 4,
        out_specs=[whole] * 2,
        out_shape=[
            jax.ShapeDtypeStruct((4, 3 * EXT, 2 * LAT), BF16),
            jax.ShapeDtypeStruct((4, 6 * LAT, EXT), BF16),
        ],
        compiler_params=params(20),
        name="make_weights",
    )(taps, *tall, *wide)


def observe_kernel(got_ref, meta_ref, obs_ref):
    sides = []
    for p in range(2):
        sides.append(got_ref[:, 0, p * 32 : p * 32 + 32, :].reshape(1024, 128))
    high, low = split(jnp.concatenate(sides, axis=1))
    lanes = []
    for i in range(0, 32, 4):
        lanes.append(sum(meta_ref[i + k, 0, 0:1, :] for k in range(1, 4)) + meta_ref[i, 0, 0:1, :])
    place = jnp.concatenate(lanes, axis=1)
    for half in range(4):
        rows = lax.broadcasted_iota(jnp.int32, (256, 1024), 0) + half * 256
        hot = (rows.astype(F32) == place).astype(F32)
        counts = jnp.sum(hot, axis=1, keepdims=True)
        hot = hot.astype(BF16)
        mean = (dot(hot, high) + dot(hot, low)) / jnp.maximum(counts, 1.0)
        for i in range(2):
            for p in range(2):
                obs_ref[half // 2, (half % 2) * 2 + i, p * 128 : p * 128 + 128, :] = mean[
                    i * 128 : i * 128 + 128, p * 128 : p * 128 + 128
                ]


def observe(got):
    got = got.reshape(32, 4, 80, 128)
    return pl.pallas_call(
        observe_kernel,
        grid=(4,),
        in_specs=[
            pl.BlockSpec((32, 1, 64, 128), lambda g: (0, g, 0, 0)),
            pl.BlockSpec((32, 1, 8, 128), lambda g: (0, g, 9, 0)),
        ],
        out_specs=pl.BlockSpec((2, 4, 256, 128), lambda g: (g, 0, 0, 0)),
        out_shape=jax.ShapeDtypeStruct((8, 4, 256, 128), F32),
        compiler_params=params(20),
        cost_estimate=pl.CostEstimate(flops=4 << 30, bytes_accessed=8 << 20, transcendentals=0),
        name="observe",
    )(got, got)


def depth_blur(x, taps):
    rows = [None] * 32
    for p in range(2):
        for m in range(16):
            rows[2 * m + p] = x[p * 128 + m * 8 : p * 128 + m * 8 + 8]
    layer = lax.broadcasted_iota(jnp.int32, rows[0].shape, 0)
    before = [jnp.where(layer == 0, 0.0, pltpu.roll(rows[32 - k], 1, 0)) for k in (3, 2, 1)]
    after = [jnp.where(layer == 7, 0.0, pltpu.roll(rows[k], 7, 0)) for k in (0, 1, 2)]
    e = before + rows + after
    out = [
        taps[0] * e[z + 3]
        + taps[1] * (e[z + 2] + e[z + 4])
        + (taps[2] * (e[z + 1] + e[z + 5]) + taps[3] * (e[z] + e[z + 6]))
        for z in range(32)
    ]
    return jnp.concatenate([out[2 * m + p] for p in range(2) for m in range(16)], axis=0)


def back_project(blurred, back_ref, total):
    total[...] = jnp.zeros_like(total)

    def step(pair, carry):
        rows = []
        for x in blurred(pair):
            halves = [split(side) for side in x]
            high = [h for h, _ in halves]
            low = [l for _, l in halves]
            rows.append(jnp.concatenate(high + low + high, axis=1))
        total[...] += dot(jnp.concatenate(rows, axis=0), back_ref[pair])
        return carry

    lax.fori_loop(0, 4, step, 0, unroll=True)


def finish_back(total, out_ref, own_ref, outs):
    for q in range(4):
        own_ref[q] = total[q * 256 : q * 256 + 256, :LAT]
    halo = jnp.concatenate([total[q * 256 : q * 256 + 256, LAT:] for q in range(4)], axis=1)
    to_messages(halo, out_ref, outs)


def cover_kernel(taps_ref, obs_ref, back_ref, out_ref, own_ref, *rest):
    outs, total = rest[:8], rest[8]

    def blurred(pair):
        for q in range(4):
            sides = []
            for i in range(2):
                taps = [taps_ref[0, 2 * pair + i, k] for k in range(RAD + 1)]
                sides.append(depth_blur((obs_ref[2 * pair + i, q] > 0.0).astype(F32), taps))
            yield sides

    back_project(blurred, back_ref, total)
    finish_back(total, out_ref, own_ref, outs)


def cover(taps, obs, back, leave):
    whole = pl.BlockSpec(memory_space=pltpu.VMEM)
    return pl.pallas_call(
        cover_kernel,
        in_specs=[pl.BlockSpec(memory_space=pltpu.SMEM)] + [whole] * 3,
        out_specs=[whole] * 9,
        out_shape=[jax.ShapeDtypeStruct((4, 256, LAT), F32)] + MESSAGES,
        scratch_shapes=[pltpu.VMEM((1024, EXT), F32)],
        compiler_params=params(20),
        cost_estimate=pl.CostEstimate(flops=6 << 30, bytes_accessed=8 << 20, transcendentals=0),
        name="cover",
    )(taps, obs, back, leave)


def sweep_kernel(taps_ref, obs_ref, fore_ref, back_ref, enter_ref, leave_ref, cur_ref, *refs):
    parts, own_ref, outs = refs[:8], refs[8], refs[9:17]
    total, ext = refs[17:]

    def put(rows, at, x):
        high, low = split(x)
        for i, half in enumerate((high, low, high)):
            ext[rows, i * EXT + at : i * EXT + at + x.shape[1]] = half

    for q in range(4):
        put(slice(q * 256, q * 256 + 256), 0, cur_ref[q])
    for p, halo in enumerate(from_messages(parts, enter_ref)):
        for q in range(4):
            start = q * 256 + p * 128
            put(slice(start, start + 128), LAT, halo[:, q * HALO_PAD : (q + 1) * HALO_PAD])

    def blurred(pair):
        across = dot(ext[...], fore_ref[pair])
        for q in range(4):
            sides = []
            for i in range(2):
                w = 2 * pair + i
                taps = [taps_ref[0, w, k] for k in range(RAD + 1)]
                blur = depth_blur(across[q * 256 : q * 256 + 256, i * LAT : i * LAT + LAT], taps)
                near = pl.reciprocal(blur, approx=True)
                near = near * (2.0 - blur * near)
                sides.append(depth_blur(obs_ref[w, q] * near, taps))
            yield sides

    back_project(blurred, back_ref, total)
    finish_back(total, leave_ref, own_ref, outs)


def sweep(taps, obs, weights, enter, leave, cur, parts):
    whole = pl.BlockSpec(memory_space=pltpu.VMEM)
    return pl.pallas_call(
        sweep_kernel,
        in_specs=[pl.BlockSpec(memory_space=pltpu.SMEM)] + [whole] * 14,
        out_specs=[whole] * 9,
        out_shape=[jax.ShapeDtypeStruct((4, 256, LAT), F32)] + MESSAGES,
        scratch_shapes=[pltpu.VMEM((1024, EXT), F32), pltpu.VMEM((1024, 3 * EXT), BF16)],
        compiler_params=params(26),
        cost_estimate=pl.CostEstimate(flops=12 << 30, bytes_accessed=12 << 20, transcendentals=0),
        name="sweep",
    )(taps, obs, *weights, enter, leave, cur, *parts)


def below_kernel(add_ref, cover_ref, *refs):
    covers, out_ref = refs[:8], refs[8]
    for p, cover in enumerate(add_messages(covers, add_ref, cover_ref)):
        for q in range(4):
            out_ref[q, p * 128 : p * 128 + 128, :] = 1.0 + cover[:, q * LAT : q * LAT + LAT]


def sum_below(add, cover):
    whole = pl.BlockSpec(memory_space=pltpu.VMEM)
    return pl.pallas_call(
        below_kernel,
        in_specs=[whole] * 10,
        out_specs=whole,
        out_shape=jax.ShapeDtypeStruct((4, 256, LAT), F32),
        compiler_params=params(12),
        name="sum_below",
    )(add, *cover)


def update_kernel(pick_ref, add_ref, cur_ref, below_ref, total_ref, *refs):
    totals, cur_out, outs = refs[:8], refs[8], refs[9:17]
    total = add_messages(totals, add_ref, total_ref)
    for p in range(2):
        rows = slice(p * 128, p * 128 + 128)
        for q in range(4):
            mine = total[p][:, q * LAT : q * LAT + LAT]
            cur_out[q, rows, :] = cur_ref[q, rows, :] * (1.0 + mine) / below_ref[q, rows, :]
    to_messages(quads(cur_out), pick_ref, outs)


def update(pick, add, cur, below, total):
    whole = pl.BlockSpec(memory_space=pltpu.VMEM)
    return pl.pallas_call(
        update_kernel,
        in_specs=[whole] * 13,
        out_specs=[whole] * 9,
        out_shape=[jax.ShapeDtypeStruct((4, 256, LAT), F32)] + MESSAGES,
        compiler_params=params(14),
        name="update",
    )(pick, add, cur, below, *total)


def last_kernel(add_ref, cur_ref, below_ref, total_ref, *refs):
    totals, out_ref, rows_ref = refs[:8], refs[8], refs[9]
    total = add_messages(totals, add_ref, total_ref)
    for p in range(2):
        rows = slice(p * 128, p * 128 + 128)
        for q in range(4):
            mine = total[p][:, q * LAT : q * LAT + LAT]
            done = cur_ref[q, rows, :] * (1.0 + mine) / below_ref[q, rows, :]
            for m in range(16):
                rows_ref[pl.ds(m * 8 + p * 4 + q, 8, stride=128), :] = done[m * 8 : m * 8 + 8]
    done = rows_ref[...].reshape(32, 32, 128)
    for v in range(4):
        out_ref[:, v] = done


def last_update(add, cur, below, total):
    whole = pl.BlockSpec(memory_space=pltpu.VMEM)
    out = pl.pallas_call(
        last_kernel,
        in_specs=[whole] * 12,
        out_specs=whole,
        out_shape=jax.ShapeDtypeStruct((32, 4, 32, 128), F32),
        scratch_shapes=[pltpu.VMEM((1024, 128), F32)],
        compiler_params=params(14),
        name="last_update",
    )(add, cur, below, *total)
    return out.reshape(128, 32, 128)


def place_kernel(got_ref, out_ref, side_ref):
    got = got_ref.reshape(1024, 128)
    odd = pl.program_id(0) % 2
    for k in range(4):
        z = jnp.where(odd == 0, k, 3 - k)
        for tx in range(2):
            rows = turn([got[pl.ds(c * 128 + z * 32 + tx, 16, stride=2), :] for c in range(8)])
            side = side_ref.at[k * 2 + tx]
            for s in range(8):
                side[pl.ds(s, 16, stride=8), :] = rows[s]
            lanes = slice(tx * 128, tx * 128 + 128)
            out_ref[:, :, 0, k * 8 : k * 8 + 8, lanes] = side[...].reshape(8, 2, 8, 128)


def place_output(got):
    out = pl.pallas_call(
        place_kernel,
        grid=(4,),
        in_specs=[pl.BlockSpec((1, 8, 4, 32, 128), lambda y: (y, 0, 0, 0, 0))],
        out_specs=pl.BlockSpec((8, 2, 1, 32, 256), lambda y: (0, 0, y, 0, 0)),
        out_shape=jax.ShapeDtypeStruct((8, 2, 4, 32, 256), F32),
        scratch_shapes=[pltpu.VMEM((8, 128, 128), F32)],
        compiler_params=params(20),
        name="place_output",
    )(got.reshape(4, 8, 4, 32, 128))
    return out.reshape(8, 256, 256)


def gather_parts(parts):
    return [lax.ppermute(x, ALL, towards(-er, -ec)) for x, (er, ec) in zip(parts, DIRS, strict=True)]


def reduce_parts(parts):
    return [lax.ppermute(x, ALL, towards(er, ec)) for x, (er, ec) in zip(parts, DIRS, strict=True)]


def on_device(estimate, tiles, tile_block, tile_view, tile_slot, widths):
    block, view = lax.axis_index("block"), lax.axis_index("view")
    y = block // 8
    r = y * 4 + jnp.where(y % 2 == 0, view, 3 - view)
    c = block % 8
    slot = tile_slot[0]
    deep = tile_block[0, :, 0] * 4 + slot // 4
    place = tile_view[0] * 512 + (slot % 4) * 128 + (deep % 16) * 8 + deep // 16
    place = jnp.where(jnp.arange(128) // 32 == block % 4, jnp.tile(place.astype(F32), 4), 0.0)
    own_widths = jnp.pad(widths.reshape(1, 6), ((1, 6), (0, 122)))
    meta = jnp.where(jnp.arange(8)[:, None] == 0, place[None, :], own_widths)
    message = make_message(view.reshape(1), tiles[0], estimate, meta)
    got = lax.all_to_all(message, ALL, split_axis=0, concat_axis=0, tiled=True)

    add = (LANE_OWN[:, None] == np.arange(4 * LAT)[None, :]).astype(BF16)
    pick = (np.arange(4 * LAT)[:, None] == LANE_OWN[None, :]).astype(BF16)
    wrap_r = ((r + ER < 0) | (r + ER >= PR)).astype(jnp.int32) * ER
    wrap_c = ((c + EC < 0) | (c + EC >= PC)).astype(jnp.int32) * EC
    ty, tx = LANE_Q // 2 - wrap_r, LANE_Q % 2 - wrap_c
    inside = (LANE_Q >= 0) & (ty >= 0) & (ty < 2) & (tx >= 0) & (tx < 2)
    target = jnp.where(inside, (ty * 2 + tx) * HALO_PAD + LANE_HALO, -1)
    enter = (target[:, None] == jnp.arange(4 * HALO_PAD)[None, :]).astype(BF16)
    leave = (jnp.arange(4 * HALO_PAD)[:, None] == target[None, :]).astype(BF16)

    cur, *sent = begin(got, pick)
    got, sent = lax.optimization_barrier((got, sent))
    parts = gather_parts(sent)
    spread = got[0:4, 73, 0:6].reshape(4, 3, 2).transpose(1, 0, 2).reshape(3, 8, 1)
    steps = jnp.arange(RAD + 1).astype(F32)
    raw = jnp.exp(-steps * steps / (2.0 * spread * spread))
    taps = raw / (2.0 * jnp.sum(raw, axis=2, keepdims=True) - raw[:, :, 0:1])
    weights = make_weights(taps)
    obs = observe(got)
    own, *sent = cover(taps, obs, weights[1], leave)
    covered = [own] + reduce_parts(sent)
    own, *sent = sweep(taps, obs, weights, enter, leave, cur, parts)
    total = [own] + reduce_parts(sent)
    below = sum_below(add, covered)
    cur, *sent = update(pick, add, cur, below, total)
    parts = gather_parts(sent)
    own, *sent = sweep(taps, obs, weights, enter, leave, cur, parts)
    total = [own] + reduce_parts(sent)
    out = last_update(add, cur, below, total)
    out = lax.all_to_all(out, ALL, split_axis=0, concat_axis=0, tiled=True)
    return place_output(out)


def solution(mesh):
    placed = (
        P("block", None, None),
        P("view", "block", None, None, None),
        P("view", "block", None),
        P("view", "block"),
        P("view", "block"),
        P(None, "view"),
    )
    return jax.shard_map(
        on_device, mesh=mesh, in_specs=placed, out_specs=P("block", None, None), check_vma=False
    )
```

```python
import jax
import jax.numpy as jnp
import numpy as np
from jax import lax
from jax.experimental import pallas as pl
from jax.experimental.pallas import tpu as pltpu
from jax.sharding import PartitionSpec as P

RAD = 3
ITERS = 2
ALL = ("block", "view")
PR, PC = 16, 8
SR, SC = 8, 16
LAT = SR * SC
HALO_PAD = 256
EXT = LAT + HALO_PAD
F32, BF16 = jnp.float32, jnp.bfloat16

DIRS = [(0, -1), (0, 1), (-1, 0), (1, 0), (-1, -1), (-1, 1), (1, -1), (1, 1)]


def part_range(step, size):
    if step < 0:
        return list(range(-RAD, 0))
    if step > 0:
        return list(range(size, size + RAD))
    return list(range(size))


PARTS = [[(dr, dc) for dr in part_range(er, SR) for dc in part_range(ec, SC)] for er, ec in DIRS]
SIZES = [len(part) for part in PARTS]
HALO_AT = [sum(SIZES[:n]) for n in range(8)]
EXT_POS = [(s, j) for s in range(SR) for j in range(SC)] + [pos for part in PARTS for pos in part]
EXT_POS = EXT_POS + [(1000, 1000)] * (EXT - len(EXT_POS))


def device_of(r, c):
    r, c = r % PR, c % PC
    y, k = r // 4, r % 4
    return (y * 8 + c) * 4 + (k if y % 2 == 0 else 3 - k)


def towards(er, ec):
    return [(device_of(r, c), device_of(r + er, c + ec)) for r in range(PR) for c in range(PC)]


def lane_table():
    main = [[-1] * 128 for _ in range(4)]
    aux = [[[-1] * 128 for _ in range(6)] for _ in range(2)]
    for n in range(8):
        for lane in range(4 * SIZES[n]):
            if n < 4 and lane < 128:
                main[n][lane] = (n, lane)
            else:
                for p in range(2):
                    if n < 4:
                        aux[p][n - 2][p * 64 + lane - 128] = (n, lane)
                    else:
                        aux[p][n - 2][p * 36 + lane] = (n, lane)
    return [x for row in main for x in row] + [x for kind in aux for row in kind for x in row]


LANES = lane_table()
LANE_N = np.array([0 if x == -1 else x[0] for x in LANES])
LANE_Q = np.array([-100 if x == -1 else x[1] // SIZES[x[0]] for x in LANES])
LANE_HALO = np.array([0 if x == -1 else HALO_AT[x[0]] + x[1] % SIZES[x[0]] for x in LANES])
LANE_OWN = np.array(
    [
        -1
        if x == -1
        else (x[1] // SIZES[x[0]]) * LAT
        + (PARTS[x[0]][x[1] % SIZES[x[0]]][0] % SR) * SC
        + PARTS[x[0]][x[1] % SIZES[x[0]]][1] % SC
        for x in LANES
    ]
)
ER = np.array([d[0] for d in DIRS])[LANE_N]
EC = np.array([d[1] for d in DIRS])[LANE_N]
N_MAIN, N_AUX = 512, 768


def params(mib):
    return pltpu.CompilerParams(vmem_limit_bytes=mib << 20)


def turn(rows):
    chunk = lax.broadcasted_iota(jnp.int32, rows[0].shape, 1) // SC
    for k in (4, 2, 1):
        low = (chunk & k) == 0
        after = list(rows)
        for a in range(8):
            if a & k == 0:
                x, y = rows[a], rows[a | k]
                after[a] = jnp.where(low, x, pltpu.roll(y, SC * k, 1))
                after[a | k] = jnp.where(low, pltpu.roll(x, 128 - SC * k, 1), y)
        rows = after
    return rows


def split(x):
    high = x.astype(BF16)
    return high, (x - high.astype(F32)).astype(BF16)


def dot(a, b):
    return jnp.dot(a, b, preferred_element_type=F32)


def send_small_kernel(view_ref, left_ref, right_ref, meta_ref, out_ref):
    left, right = left_ref.reshape(128, 128), right_ref.reshape(128, 128)
    odd = pl.program_id(0) % 2
    for k in range(4):
        z = jnp.where(odd == 0, k, 3 - k)
        rows = []
        for s in range(8):
            at = pl.ds(k * 8 + s, 4, stride=32)
            rows.append(jnp.concatenate([left[at, :], right[at, :]], axis=0))
        rows = turn(rows)
        for c in range(8):
            out_ref[0, c, z, 0:8, :] = rows[c]
            out_ref[0, c, z, 8:16, :] = meta_ref[...]


def small_message(view, estimate, meta):
    estimate = estimate.reshape(8, 2, 4, 32, 256)
    out = pl.pallas_call(
        send_small_kernel,
        grid_spec=pltpu.PrefetchScalarGridSpec(
            num_scalar_prefetch=1,
            grid=(4,),
            in_specs=[
                pl.BlockSpec((2, 2, 1, 32, 128), lambda y, v: (v[0], 0, y, 0, 0)),
                pl.BlockSpec((2, 2, 1, 32, 128), lambda y, v: (v[0], 0, y, 0, 1)),
                pl.BlockSpec((8, 128), lambda y, v: (0, 0)),
            ],
            out_specs=pl.BlockSpec((1, 8, 4, 16, 128), lambda y, v: (y, 0, 0, 0, 0)),
        ),
        out_shape=jax.ShapeDtypeStruct((4, 8, 4, 16, 128), F32),
        compiler_params=params(56),
        name="small_message",
    )(view, estimate, estimate, meta)
    return out.reshape(128, 16, 128)


def send_tiles_kernel(view_ref, tiles_ref, out_ref):
    tiles = tiles_ref.reshape(2048, 128)
    odd = pl.program_id(0) % 2
    for k in range(4):
        z = jnp.where(odd == 0, k, 3 - k)
        for p in range(2):
            rows = turn([tiles[pl.ds(p * 32 + k * 8 + s, 32, stride=64), :] for s in range(8)])
            for c in range(8):
                out_ref[0, c, z, p * 32 : p * 32 + 32, :] = rows[c]


def tile_message(view, tiles):
    out = pl.pallas_call(
        send_tiles_kernel,
        grid_spec=pltpu.PrefetchScalarGridSpec(
            num_scalar_prefetch=1,
            grid=(4,),
            in_specs=[pl.BlockSpec((32, 2, 32, 128), lambda y, v: (0, 0, y, 0))],
            out_specs=pl.BlockSpec((1, 8, 4, 64, 128), lambda y, v: (y, 0, 0, 0, 0)),
        ),
        out_shape=jax.ShapeDtypeStruct((4, 8, 4, 64, 128), F32),
        compiler_params=params(56),
        cost_estimate=pl.CostEstimate(flops=1 << 20, bytes_accessed=24 << 20, transcendentals=0),
        name="tile_message",
    )(view, tiles)
    return out.reshape(128, 64, 128)


def stacked(x):
    return jnp.concatenate(split(x), axis=0)


def dot_halves(x, table):
    out = dot(x, table)
    rows = out.shape[0] // 2
    return out[:rows] + out[rows:]


def aux_at(p):
    return slice(N_MAIN + p * N_AUX, N_MAIN + (p + 1) * N_AUX)


def to_messages(x, table_ref, outs):
    main = dot_halves(stacked(x), table_ref[:, :N_MAIN])
    aux = dot_halves(stacked(x[:128]), table_ref[:, aux_at(0)]) + dot_halves(stacked(x[128:]), table_ref[:, aux_at(1)])
    put_messages(main, aux, outs)


def from_messages(parts, table_ref):
    main = jnp.concatenate([parts[n][0:256, :] for n in range(4)], axis=1)
    aux = jnp.concatenate([parts[n][256:384, :] for n in (2, 3)] + [parts[n][...] for n in range(4, 8)], axis=1)
    main = dot_halves(stacked(main), table_ref[:N_MAIN, :])
    aux = stacked(aux)
    return [main[p * 128 : p * 128 + 128] + dot_halves(aux, table_ref[aux_at(p), :]) for p in range(2)]


def put_messages(main, aux, outs):
    for n in range(4):
        outs[n][0:256, :] = main[:, n * 128 : n * 128 + 128]
        if n >= 2:
            outs[n][256:384, :] = aux[:, (n - 2) * 128 : (n - 2) * 128 + 128]
    for n in range(4, 8):
        outs[n][...] = aux[:, (n - 2) * 128 : (n - 2) * 128 + 128]


MESSAGES = [jax.ShapeDtypeStruct((rows, 128), F32) for rows in (256, 256, 384, 384, 128, 128, 128, 128)]


def add_messages(parts, table_ref, base):
    out = []
    for p, term in enumerate(from_messages(parts, table_ref)):
        out.append(term + jnp.concatenate([base[q, p * 128 : p * 128 + 128, :] for q in range(4)], axis=1))
    return out


def quads(x):
    return jnp.concatenate([x[q] for q in range(4)], axis=1)


def begin_kernel(got_ref, pick_ref, cur_ref, *outs):
    got = got_ref.reshape(128 * 16, 128)
    for q in range(4):
        for p in range(2):
            row = (q % 2) * 4 + p * 2 + q // 2
            for m in range(16):
                at = p * 128 + m * 8
                cur_ref[q, at : at + 8, :] = got[pl.ds(m * 16 + row, 8, stride=256), :]
    to_messages(quads(cur_ref), pick_ref, outs)


def begin(got, pick):
    return pl.pallas_call(
        begin_kernel,
        grid=(1,),
        in_specs=[
            pl.BlockSpec((128, 16, 128), lambda i: (0, 0, 0)),
            pl.BlockSpec((512, N_MAIN + 2 * N_AUX), lambda i: (0, 0)),
        ],
        out_specs=[pl.BlockSpec((4, 256, 128), lambda i: (0, 0, 0))]
        + [pl.BlockSpec(m.shape, lambda i: (0, 0)) for m in MESSAGES],
        out_shape=[jax.ShapeDtypeStruct((4, 256, 128), F32)] + MESSAGES,
        compiler_params=params(16),
        name="begin",
    )(got, pick)


def weight_kernel(taps_ref, er_ref, ec_ref, ert_ref, ect_ref, fore_ref, back_ref):
    def from_taps(apart, axis, w):
        far = jnp.abs(apart)
        out = jnp.zeros(apart.shape, F32)
        for k in range(RAD + 1):
            out = jnp.where(far == k, taps_ref[axis, w, k], out)
        return out

    lanes = lax.broadcasted_iota(jnp.int32, (EXT, LAT), 1)
    down, across = er_ref[...] - lanes // SC, ec_ref[...] - lanes % SC
    rows = lax.broadcasted_iota(jnp.int32, (LAT, EXT), 0)
    down_t, across_t = ert_ref[...] - rows // SC, ect_ref[...] - rows % SC
    for w in range(8):
        pair, at = w // 2, slice((w % 2) * LAT, (w % 2) * LAT + LAT)
        high, low = split(from_taps(down, 1, w) * from_taps(across, 2, w))
        for i, x in enumerate((high, high, low)):
            fore_ref[pair, i * EXT : i * EXT + EXT, at] = x
        high, low = split(from_taps(down_t, 1, w) * from_taps(across_t, 2, w))
        for i, x in enumerate((high, high, low)):
            start = i * 2 * LAT + (w % 2) * LAT
            back_ref[pair, start : start + LAT, :] = x


def make_weights(taps):
    ext = np.array(EXT_POS, np.int32)
    tall = [np.broadcast_to(ext[:, i][:, None], (EXT, LAT)) for i in range(2)]
    wide = [np.broadcast_to(ext[:, i][None, :], (LAT, EXT)) for i in range(2)]
    whole = pl.BlockSpec(memory_space=pltpu.VMEM)
    return pl.pallas_call(
        weight_kernel,
        in_specs=[pl.BlockSpec(memory_space=pltpu.SMEM)] + [whole] * 4,
        out_specs=[whole] * 2,
        out_shape=[
            jax.ShapeDtypeStruct((4, 3 * EXT, 2 * LAT), BF16),
            jax.ShapeDtypeStruct((4, 6 * LAT, EXT), BF16),
        ],
        compiler_params=params(20),
        name="make_weights",
    )(taps, *tall, *wide)


def observe_kernel(got_ref, meta_ref, obs_ref):
    sides = []
    for p in range(2):
        sides.append(got_ref[:, 0, p * 32 : p * 32 + 32, :].reshape(1024, 128))
    high, low = split(jnp.concatenate(sides, axis=1))
    lanes = []
    for i in range(0, 32, 4):
        lanes.append(sum(meta_ref[i + k, 0, 0:1, :] for k in range(1, 4)) + meta_ref[i, 0, 0:1, :])
    place = jnp.concatenate(lanes, axis=1)
    for half in range(4):
        rows = lax.broadcasted_iota(jnp.int32, (256, 1024), 0) + half * 256
        hot = (rows.astype(F32) == place).astype(F32)
        counts = jnp.sum(hot, axis=1, keepdims=True)
        hot = hot.astype(BF16)
        mean = (dot(hot, high) + dot(hot, low)) / jnp.maximum(counts, 1.0)
        for i in range(2):
            for p in range(2):
                obs_ref[half // 2, (half % 2) * 2 + i, p * 128 : p * 128 + 128, :] = mean[
                    i * 128 : i * 128 + 128, p * 128 : p * 128 + 128
                ]


def observe(got, small):
    got = got.reshape(32, 4, 64, 128)
    small = small.reshape(32, 4, 16, 128)
    return pl.pallas_call(
        observe_kernel,
        grid=(4,),
        in_specs=[
            pl.BlockSpec((32, 1, 64, 128), lambda g: (0, g, 0, 0)),
            pl.BlockSpec((32, 1, 8, 128), lambda g: (0, g, 1, 0)),
        ],
        out_specs=pl.BlockSpec((2, 4, 256, 128), lambda g: (g, 0, 0, 0)),
        out_shape=jax.ShapeDtypeStruct((8, 4, 256, 128), F32),
        compiler_params=params(20),
        cost_estimate=pl.CostEstimate(flops=4 << 30, bytes_accessed=8 << 20, transcendentals=0),
        name="observe",
    )(got, small)


def depth_blur(x, taps):
    rows = [None] * 32
    for p in range(2):
        for m in range(16):
            rows[2 * m + p] = x[p * 128 + m * 8 : p * 128 + m * 8 + 8]
    layer = lax.broadcasted_iota(jnp.int32, rows[0].shape, 0)
    before = [jnp.where(layer == 0, 0.0, pltpu.roll(rows[32 - k], 1, 0)) for k in (3, 2, 1)]
    after = [jnp.where(layer == 7, 0.0, pltpu.roll(rows[k], 7, 0)) for k in (0, 1, 2)]
    e = before + rows + after
    out = [
        taps[0] * e[z + 3]
        + taps[1] * (e[z + 2] + e[z + 4])
        + (taps[2] * (e[z + 1] + e[z + 5]) + taps[3] * (e[z] + e[z + 6]))
        for z in range(32)
    ]
    return jnp.concatenate([out[2 * m + p] for p in range(2) for m in range(16)], axis=0)


def back_project(blurred, back_ref, total):
    total[...] = jnp.zeros_like(total)

    def step(pair, carry):
        rows = []
        for x in blurred(pair):
            halves = [split(side) for side in x]
            high = [h for h, _ in halves]
            low = [l for _, l in halves]
            rows.append(jnp.concatenate(high + low + high, axis=1))
        total[...] += dot(jnp.concatenate(rows, axis=0), back_ref[pair])
        return carry

    lax.fori_loop(0, 4, step, 0, unroll=True)


def finish_back(total, out_ref, own_ref, outs):
    for q in range(4):
        own_ref[q] = total[q * 256 : q * 256 + 256, :LAT]
    halo = jnp.concatenate([total[q * 256 : q * 256 + 256, LAT:] for q in range(4)], axis=1)
    to_messages(halo, out_ref, outs)


def cover_kernel(taps_ref, obs_ref, back_ref, out_ref, own_ref, *rest):
    outs, total = rest[:8], rest[8]

    def blurred(pair):
        for q in range(4):
            sides = []
            for i in range(2):
                taps = [taps_ref[0, 2 * pair + i, k] for k in range(RAD + 1)]
                sides.append(depth_blur((obs_ref[2 * pair + i, q] > 0.0).astype(F32), taps))
            yield sides

    back_project(blurred, back_ref, total)
    finish_back(total, out_ref, own_ref, outs)


def cover(taps, obs, back, leave):
    whole = pl.BlockSpec(memory_space=pltpu.VMEM)
    return pl.pallas_call(
        cover_kernel,
        in_specs=[pl.BlockSpec(memory_space=pltpu.SMEM)] + [whole] * 3,
        out_specs=[whole] * 9,
        out_shape=[jax.ShapeDtypeStruct((4, 256, LAT), F32)] + MESSAGES,
        scratch_shapes=[pltpu.VMEM((1024, EXT), F32)],
        compiler_params=params(20),
        cost_estimate=pl.CostEstimate(flops=6 << 30, bytes_accessed=8 << 20, transcendentals=0),
        name="cover",
    )(taps, obs, back, leave)


def sweep_kernel(taps_ref, obs_ref, fore_ref, back_ref, enter_ref, leave_ref, cur_ref, *refs):
    parts, own_ref, outs = refs[:8], refs[8], refs[9:17]
    total, ext = refs[17:]

    def put(rows, at, x):
        high, low = split(x)
        for i, half in enumerate((high, low, high)):
            ext[rows, i * EXT + at : i * EXT + at + x.shape[1]] = half

    for q in range(4):
        put(slice(q * 256, q * 256 + 256), 0, cur_ref[q])
    for p, halo in enumerate(from_messages(parts, enter_ref)):
        for q in range(4):
            start = q * 256 + p * 128
            put(slice(start, start + 128), LAT, halo[:, q * HALO_PAD : (q + 1) * HALO_PAD])

    def blurred(pair):
        across = dot(ext[...], fore_ref[pair])
        for q in range(4):
            sides = []
            for i in range(2):
                w = 2 * pair + i
                taps = [taps_ref[0, w, k] for k in range(RAD + 1)]
                blur = depth_blur(across[q * 256 : q * 256 + 256, i * LAT : i * LAT + LAT], taps)
                near = pl.reciprocal(blur, approx=True)
                near = near * (2.0 - blur * near)
                sides.append(depth_blur(obs_ref[w, q] * near, taps))
            yield sides

    back_project(blurred, back_ref, total)
    finish_back(total, leave_ref, own_ref, outs)


def sweep(taps, obs, weights, enter, leave, cur, parts):
    whole = pl.BlockSpec(memory_space=pltpu.VMEM)
    return pl.pallas_call(
        sweep_kernel,
        in_specs=[pl.BlockSpec(memory_space=pltpu.SMEM)] + [whole] * 14,
        out_specs=[whole] * 9,
        out_shape=[jax.ShapeDtypeStruct((4, 256, LAT), F32)] + MESSAGES,
        scratch_shapes=[pltpu.VMEM((1024, EXT), F32), pltpu.VMEM((1024, 3 * EXT), BF16)],
        compiler_params=params(26),
        cost_estimate=pl.CostEstimate(flops=12 << 30, bytes_accessed=12 << 20, transcendentals=0),
        name="sweep",
    )(taps, obs, *weights, enter, leave, cur, *parts)


def below_kernel(add_ref, cover_ref, *refs):
    covers, out_ref = refs[:8], refs[8]
    for p, cover in enumerate(add_messages(covers, add_ref, cover_ref)):
        for q in range(4):
            out_ref[q, p * 128 : p * 128 + 128, :] = 1.0 + cover[:, q * LAT : q * LAT + LAT]


def sum_below(add, cover):
    whole = pl.BlockSpec(memory_space=pltpu.VMEM)
    return pl.pallas_call(
        below_kernel,
        in_specs=[whole] * 10,
        out_specs=whole,
        out_shape=jax.ShapeDtypeStruct((4, 256, LAT), F32),
        compiler_params=params(12),
        name="sum_below",
    )(add, *cover)


def update_kernel(pick_ref, add_ref, cur_ref, below_ref, total_ref, *refs):
    totals, cur_out, outs = refs[:8], refs[8], refs[9:17]
    total = add_messages(totals, add_ref, total_ref)
    for p in range(2):
        rows = slice(p * 128, p * 128 + 128)
        for q in range(4):
            mine = total[p][:, q * LAT : q * LAT + LAT]
            cur_out[q, rows, :] = cur_ref[q, rows, :] * (1.0 + mine) / below_ref[q, rows, :]
    to_messages(quads(cur_out), pick_ref, outs)


def update(pick, add, cur, below, total):
    whole = pl.BlockSpec(memory_space=pltpu.VMEM)
    return pl.pallas_call(
        update_kernel,
        in_specs=[whole] * 13,
        out_specs=[whole] * 9,
        out_shape=[jax.ShapeDtypeStruct((4, 256, LAT), F32)] + MESSAGES,
        compiler_params=params(14),
        name="update",
    )(pick, add, cur, below, *total)


def last_kernel(add_ref, cur_ref, below_ref, total_ref, *refs):
    totals, out_ref, rows_ref = refs[:8], refs[8], refs[9]
    total = add_messages(totals, add_ref, total_ref)
    for p in range(2):
        rows = slice(p * 128, p * 128 + 128)
        for q in range(4):
            mine = total[p][:, q * LAT : q * LAT + LAT]
            done = cur_ref[q, rows, :] * (1.0 + mine) / below_ref[q, rows, :]
            for m in range(16):
                rows_ref[pl.ds(m * 8 + p * 4 + q, 8, stride=128), :] = done[m * 8 : m * 8 + 8]
    done = rows_ref[...].reshape(32, 32, 128)
    for v in range(4):
        out_ref[:, v] = done


def last_update(add, cur, below, total):
    whole = pl.BlockSpec(memory_space=pltpu.VMEM)
    out = pl.pallas_call(
        last_kernel,
        in_specs=[whole] * 12,
        out_specs=whole,
        out_shape=jax.ShapeDtypeStruct((32, 4, 32, 128), F32),
        scratch_shapes=[pltpu.VMEM((1024, 128), F32)],
        compiler_params=params(14),
        name="last_update",
    )(add, cur, below, *total)
    return out.reshape(128, 32, 128)


def place_kernel(got_ref, out_ref, side_ref):
    got = got_ref.reshape(1024, 128)
    odd = pl.program_id(0) % 2
    for k in range(4):
        z = jnp.where(odd == 0, k, 3 - k)
        for tx in range(2):
            rows = turn([got[pl.ds(c * 128 + z * 32 + tx, 16, stride=2), :] for c in range(8)])
            side = side_ref.at[k * 2 + tx]
            for s in range(8):
                side[pl.ds(s, 16, stride=8), :] = rows[s]
            lanes = slice(tx * 128, tx * 128 + 128)
            out_ref[:, :, 0, k * 8 : k * 8 + 8, lanes] = side[...].reshape(8, 2, 8, 128)


def place_output(got):
    out = pl.pallas_call(
        place_kernel,
        grid=(4,),
        in_specs=[pl.BlockSpec((1, 8, 4, 32, 128), lambda y: (y, 0, 0, 0, 0))],
        out_specs=pl.BlockSpec((8, 2, 1, 32, 256), lambda y: (0, 0, y, 0, 0)),
        out_shape=jax.ShapeDtypeStruct((8, 2, 4, 32, 256), F32),
        scratch_shapes=[pltpu.VMEM((8, 128, 128), F32)],
        compiler_params=params(20),
        name="place_output",
    )(got.reshape(4, 8, 4, 32, 128))
    return out.reshape(8, 256, 256)


def gather_parts(parts):
    return [lax.ppermute(x, ALL, towards(-er, -ec)) for x, (er, ec) in zip(parts, DIRS, strict=True)]


def reduce_parts(parts):
    return [lax.ppermute(x, ALL, towards(er, ec)) for x, (er, ec) in zip(parts, DIRS, strict=True)]


def on_device(estimate, tiles, tile_block, tile_view, tile_slot, widths):
    block, view = lax.axis_index("block"), lax.axis_index("view")
    y = block // 8
    r = y * 4 + jnp.where(y % 2 == 0, view, 3 - view)
    c = block % 8
    slot = tile_slot[0]
    deep = tile_block[0, :, 0] * 4 + slot // 4
    place = tile_view[0] * 512 + (slot % 4) * 128 + (deep % 16) * 8 + deep // 16
    place = jnp.where(jnp.arange(128) // 32 == block % 4, jnp.tile(place.astype(F32), 4), 0.0)
    own_widths = jnp.pad(widths.reshape(1, 6), ((1, 6), (0, 122)))
    meta = jnp.where(jnp.arange(8)[:, None] == 0, place[None, :], own_widths)
    send = small_message(view.reshape(1), estimate, meta)
    order, send = lax.optimization_barrier((view.reshape(1), send))
    small = lax.all_to_all(send, ALL, split_axis=0, concat_axis=0, tiled=True)
    send = tile_message(order, tiles[0])
    send, small = lax.optimization_barrier((send, small))
    got = lax.all_to_all(send, ALL, split_axis=0, concat_axis=0, tiled=True)

    add = (LANE_OWN[:, None] == np.arange(4 * LAT)[None, :]).astype(BF16)
    pick = (np.arange(4 * LAT)[:, None] == LANE_OWN[None, :]).astype(BF16)
    wrap_r = ((r + ER < 0) | (r + ER >= PR)).astype(jnp.int32) * ER
    wrap_c = ((c + EC < 0) | (c + EC >= PC)).astype(jnp.int32) * EC
    ty, tx = LANE_Q // 2 - wrap_r, LANE_Q % 2 - wrap_c
    inside = (LANE_Q >= 0) & (ty >= 0) & (ty < 2) & (tx >= 0) & (tx < 2)
    target = jnp.where(inside, (ty * 2 + tx) * HALO_PAD + LANE_HALO, -1)
    enter = (target[:, None] == jnp.arange(4 * HALO_PAD)[None, :]).astype(BF16)
    leave = (jnp.arange(4 * HALO_PAD)[:, None] == target[None, :]).astype(BF16)

    cur, *sent = begin(small, pick)
    parts = gather_parts(sent)
    spread = small[0:4, 9, 0:6].reshape(4, 3, 2).transpose(1, 0, 2).reshape(3, 8, 1)
    steps = jnp.arange(RAD + 1).astype(F32)
    raw = jnp.exp(-steps * steps / (2.0 * spread * spread))
    taps = raw / (2.0 * jnp.sum(raw, axis=2, keepdims=True) - raw[:, :, 0:1])
    weights = make_weights(taps)
    got, weights, taps = lax.optimization_barrier((got, weights, taps))
    obs = observe(got, small)
    obs, corners = lax.optimization_barrier((obs, parts[4:]))
    own, *sent = cover(taps, obs, weights[1], leave)
    parts = parts[:4] + list(corners)
    sent, parts = lax.optimization_barrier((sent, parts))
    covered = [own] + reduce_parts(sent)
    covered[4], covered[5], cur = lax.optimization_barrier((covered[4], covered[5], cur))
    own, *sent = sweep(taps, obs, weights, enter, leave, cur, parts)
    total = [own] + reduce_parts(sent)
    below = sum_below(add, covered)
    cur, *sent = update(pick, add, cur, below, total)
    parts = gather_parts(sent)
    own, *sent = sweep(taps, obs, weights, enter, leave, cur, parts)
    total = [own] + reduce_parts(sent)
    out = last_update(add, cur, below, total)
    out = lax.all_to_all(out, ALL, split_axis=0, concat_axis=0, tiled=True)
    return place_output(out)


def solution(mesh):
    placed = (
        P("block", None, None),
        P("view", "block", None, None, None),
        P("view", "block", None),
        P("view", "block"),
        P("view", "block"),
        P(None, "view"),
    )
    return jax.shard_map(
        on_device, mesh=mesh, in_specs=placed, out_specs=P("block", None, None), check_vma=False
    )
```

```python
import jax
import jax.numpy as jnp
import numpy as np
from jax import lax
from jax.experimental import pallas as pl
from jax.experimental.pallas import tpu as pltpu
from jax.sharding import PartitionSpec as P

RAD = 3
ITERS = 2
ALL = ("block", "view")
PR, PC = 16, 8
SR, SC = 8, 16
LAT = SR * SC
HALO_PAD = 256
EXT = LAT + HALO_PAD
F32, BF16 = jnp.float32, jnp.bfloat16

DIRS = [(0, -1), (0, 1), (-1, 0), (1, 0), (-1, -1), (-1, 1), (1, -1), (1, 1)]


def part_range(step, size):
    if step < 0:
        return list(range(-RAD, 0))
    if step > 0:
        return list(range(size, size + RAD))
    return list(range(size))


PARTS = [[(dr, dc) for dr in part_range(er, SR) for dc in part_range(ec, SC)] for er, ec in DIRS]
SIZES = [len(part) for part in PARTS]
HALO_AT = [sum(SIZES[:n]) for n in range(8)]
EXT_POS = [(s, j) for s in range(SR) for j in range(SC)] + [pos for part in PARTS for pos in part]
EXT_POS = EXT_POS + [(1000, 1000)] * (EXT - len(EXT_POS))


def row_place(r):
    y, k = r // 3, r % 3
    turned = y % 2
    z = 1 + k + turned * (2 - 2 * k)
    home = r // 12
    return y + home * (15 - r - y), z - home * z


def column_place(c):
    core = c // 4
    return (c % 4 + core * (3 - 2 * (c % 4))) * 2 + core


def device_of(r, c):
    y, z = row_place(r % PR)
    return (y * 8 + column_place(c % PC)) * 4 + z


def towards(er, ec):
    return [(device_of(r, c), device_of(r + er, c + ec)) for r in range(PR) for c in range(PC)]


def lane_table():
    main = [[-1] * 128 for _ in range(4)]
    aux = [[[-1] * 128 for _ in range(6)] for _ in range(2)]
    for n in range(8):
        for lane in range(4 * SIZES[n]):
            if n < 4 and lane < 128:
                main[n][lane] = (n, lane)
            else:
                for p in range(2):
                    if n < 4:
                        aux[p][n - 2][p * 64 + lane - 128] = (n, lane)
                    else:
                        aux[p][n - 2][p * 36 + lane] = (n, lane)
    return [x for row in main for x in row] + [x for kind in aux for row in kind for x in row]


LANES = lane_table()
LANE_N = np.array([0 if x == -1 else x[0] for x in LANES])
LANE_Q = np.array([-100 if x == -1 else x[1] // SIZES[x[0]] for x in LANES])
LANE_HALO = np.array([0 if x == -1 else HALO_AT[x[0]] + x[1] % SIZES[x[0]] for x in LANES])
LANE_OWN = np.array(
    [
        -1
        if x == -1
        else (x[1] // SIZES[x[0]]) * LAT
        + (PARTS[x[0]][x[1] % SIZES[x[0]]][0] % SR) * SC
        + PARTS[x[0]][x[1] % SIZES[x[0]]][1] % SC
        for x in LANES
    ]
)
ER = np.array([d[0] for d in DIRS])[LANE_N]
EC = np.array([d[1] for d in DIRS])[LANE_N]
N_MAIN, N_AUX = 512, 768


def params(mib):
    return pltpu.CompilerParams(vmem_limit_bytes=mib << 20)


def turn(rows):
    chunk = lax.broadcasted_iota(jnp.int32, rows[0].shape, 1) // SC
    for k in (4, 2, 1):
        low = (chunk & k) == 0
        after = list(rows)
        for a in range(8):
            if a & k == 0:
                x, y = rows[a], rows[a | k]
                after[a] = jnp.where(low, x, pltpu.roll(y, SC * k, 1))
                after[a | k] = jnp.where(low, pltpu.roll(x, 128 - SC * k, 1), y)
        rows = after
    return rows


def split(x):
    high = x.astype(BF16)
    return high, (x - high.astype(F32)).astype(BF16)


def dot(a, b):
    return jnp.dot(a, b, preferred_element_type=F32)


def send_small_kernel(view_ref, left_ref, right_ref, meta_ref, out_ref):
    left, right = left_ref.reshape(128, 128), right_ref.reshape(128, 128)
    for k in range(4):
        y, z = row_place(pl.program_id(0) * 4 + k)
        rows = []
        for s in range(8):
            at = pl.ds(k * 8 + s, 4, stride=32)
            rows.append(jnp.concatenate([left[at, :], right[at, :]], axis=0))
        rows = turn(rows)
        for c in range(8):
            out_ref[y, column_place(c), z, 0:8, :] = rows[c]
            out_ref[y, column_place(c), z, 8:16, :] = meta_ref[...]


def small_message(view, estimate, meta):
    estimate = estimate.reshape(8, 2, 4, 32, 256)
    out = pl.pallas_call(
        send_small_kernel,
        grid_spec=pltpu.PrefetchScalarGridSpec(
            num_scalar_prefetch=1,
            grid=(4,),
            in_specs=[
                pl.BlockSpec((2, 2, 1, 32, 128), lambda y, v: (v[0], 0, y, 0, 0)),
                pl.BlockSpec((2, 2, 1, 32, 128), lambda y, v: (v[0], 0, y, 0, 1)),
                pl.BlockSpec((8, 128), lambda y, v: (0, 0)),
            ],
            out_specs=pl.BlockSpec((4, 8, 4, 16, 128), lambda y, v: (0, 0, 0, 0, 0)),
        ),
        out_shape=jax.ShapeDtypeStruct((4, 8, 4, 16, 128), F32),
        compiler_params=params(56),
        name="small_message",
    )(view, estimate, estimate, meta)
    return out.reshape(128, 16, 128)


def send_tiles_kernel(view_ref, tiles_ref, out_ref):
    tiles = tiles_ref.reshape(2048, 128)
    for k in range(4):
        y, z = row_place(pl.program_id(0) * 4 + k)
        for p in range(2):
            rows = turn([tiles[pl.ds(p * 32 + k * 8 + s, 32, stride=64), :] for s in range(8)])
            for c in range(8):
                out_ref[y, column_place(c), z, p * 32 : p * 32 + 32, :] = rows[c]


def tile_message(view, tiles):
    out = pl.pallas_call(
        send_tiles_kernel,
        grid_spec=pltpu.PrefetchScalarGridSpec(
            num_scalar_prefetch=1,
            grid=(4,),
            in_specs=[pl.BlockSpec((32, 2, 32, 128), lambda y, v: (0, 0, y, 0))],
            out_specs=pl.BlockSpec((4, 8, 4, 64, 128), lambda y, v: (0, 0, 0, 0, 0)),
        ),
        out_shape=jax.ShapeDtypeStruct((4, 8, 4, 64, 128), F32),
        compiler_params=params(56),
        cost_estimate=pl.CostEstimate(flops=1 << 20, bytes_accessed=24 << 20, transcendentals=0),
        name="tile_message",
    )(view, tiles)
    return out.reshape(128, 64, 128)


def stacked(x):
    return jnp.concatenate(split(x), axis=0)


def dot_halves(x, table):
    out = dot(x, table)
    rows = out.shape[0] // 2
    return out[:rows] + out[rows:]


def aux_at(p):
    return slice(N_MAIN + p * N_AUX, N_MAIN + (p + 1) * N_AUX)


def to_messages(x, table_ref, outs):
    main = dot_halves(stacked(x), table_ref[:, :N_MAIN])
    aux = dot_halves(stacked(x[:128]), table_ref[:, aux_at(0)]) + dot_halves(stacked(x[128:]), table_ref[:, aux_at(1)])
    put_messages(main, aux, outs)


def from_messages(parts, table_ref):
    main = jnp.concatenate([parts[n][0:256, :] for n in range(4)], axis=1)
    aux = jnp.concatenate([parts[n][256:384, :] for n in (2, 3)] + [parts[n][0:128, :] for n in range(4, 8)], axis=1)
    main = dot_halves(stacked(main), table_ref[:N_MAIN, :])
    aux = stacked(aux)
    return [main[p * 128 : p * 128 + 128] + dot_halves(aux, table_ref[aux_at(p), :]) for p in range(2)]


def put_messages(main, aux, outs):
    for n in range(4):
        outs[n][0:256, :] = main[:, n * 128 : n * 128 + 128]
        if n >= 2:
            outs[n][256:384, :] = aux[:, (n - 2) * 128 : (n - 2) * 128 + 128]
    for n in range(4, 8):
        outs[n][0:128, :] = aux[:, (n - 2) * 128 : (n - 2) * 128 + 128]


MESSAGES = [jax.ShapeDtypeStruct((rows, 128), F32) for rows in (256, 256, 384, 384, 128, 128, 128, 128)]


def add_messages(parts, table_ref, base):
    out = []
    for p, term in enumerate(from_messages(parts, table_ref)):
        out.append(term + jnp.concatenate([base[q, p * 128 : p * 128 + 128, :] for q in range(4)], axis=1))
    return out


def quads(x):
    return jnp.concatenate([x[q] for q in range(4)], axis=1)


def begin_kernel(got_ref, pick_ref, cur_ref, *outs):
    got = got_ref.reshape(128 * 16, 128)
    for q in range(4):
        for p in range(2):
            row = (q % 2) * 4 + p * 2 + q // 2
            for m in range(16):
                at = p * 128 + m * 8
                cur_ref[q, at : at + 8, :] = got[pl.ds(m * 16 + row, 8, stride=256), :]
    to_messages(quads(cur_ref), pick_ref, outs)


def begin(got, pick):
    return pl.pallas_call(
        begin_kernel,
        grid=(1,),
        in_specs=[
            pl.BlockSpec((128, 16, 128), lambda i: (0, 0, 0)),
            pl.BlockSpec((512, N_MAIN + 2 * N_AUX), lambda i: (0, 0)),
        ],
        out_specs=[pl.BlockSpec((4, 256, 128), lambda i: (0, 0, 0))]
        + [pl.BlockSpec(m.shape, lambda i: (0, 0)) for m in MESSAGES],
        out_shape=[jax.ShapeDtypeStruct((4, 256, 128), F32)] + MESSAGES,
        compiler_params=params(16),
        name="begin",
    )(got, pick)


def weight_kernel(taps_ref, er_ref, ec_ref, ert_ref, ect_ref, fore_ref, back_ref):
    def from_taps(apart, axis, w):
        far = jnp.abs(apart)
        out = jnp.zeros(apart.shape, F32)
        for k in range(RAD + 1):
            out = jnp.where(far == k, taps_ref[axis, w, k], out)
        return out

    lanes = lax.broadcasted_iota(jnp.int32, (EXT, LAT), 1)
    down, across = er_ref[...] - lanes // SC, ec_ref[...] - lanes % SC
    rows = lax.broadcasted_iota(jnp.int32, (LAT, EXT), 0)
    down_t, across_t = ert_ref[...] - rows // SC, ect_ref[...] - rows % SC
    for w in range(8):
        pair, at = w // 2, slice((w % 2) * LAT, (w % 2) * LAT + LAT)
        high, low = split(from_taps(down, 1, w) * from_taps(across, 2, w))
        for i, x in enumerate((high, high, low)):
            fore_ref[pair, i * EXT : i * EXT + EXT, at] = x
        high, low = split(from_taps(down_t, 1, w) * from_taps(across_t, 2, w))
        for i, x in enumerate((high, high, low)):
            start = i * 2 * LAT + (w % 2) * LAT
            back_ref[pair, start : start + LAT, :] = x


def make_weights(taps):
    ext = np.array(EXT_POS, np.int32)
    tall = [np.broadcast_to(ext[:, i][:, None], (EXT, LAT)) for i in range(2)]
    wide = [np.broadcast_to(ext[:, i][None, :], (LAT, EXT)) for i in range(2)]
    whole = pl.BlockSpec(memory_space=pltpu.VMEM)
    return pl.pallas_call(
        weight_kernel,
        in_specs=[pl.BlockSpec(memory_space=pltpu.SMEM)] + [whole] * 4,
        out_specs=[whole] * 2,
        out_shape=[
            jax.ShapeDtypeStruct((4, 3 * EXT, 2 * LAT), BF16),
            jax.ShapeDtypeStruct((4, 6 * LAT, EXT), BF16),
        ],
        compiler_params=params(20),
        name="make_weights",
    )(taps, *tall, *wide)


def observe_kernel(got_ref, meta_ref, obs_ref):
    sides = []
    for p in range(2):
        sides.append(got_ref[:, 0, p * 32 : p * 32 + 32, :].reshape(1024, 128))
    high, low = split(jnp.concatenate(sides, axis=1))
    lanes = []
    for i in range(0, 32, 4):
        lanes.append(sum(meta_ref[i + k, 0, 0:1, :] for k in range(1, 4)) + meta_ref[i, 0, 0:1, :])
    place = jnp.concatenate(lanes, axis=1)
    for half in range(4):
        rows = lax.broadcasted_iota(jnp.int32, (256, 1024), 0) + half * 256
        hot = (rows.astype(F32) == place).astype(F32)
        counts = jnp.sum(hot, axis=1, keepdims=True)
        hot = hot.astype(BF16)
        mean = (dot(hot, high) + dot(hot, low)) / jnp.maximum(counts, 1.0)
        for i in range(2):
            for p in range(2):
                obs_ref[half // 2, (half % 2) * 2 + i, p * 128 : p * 128 + 128, :] = mean[
                    i * 128 : i * 128 + 128, p * 128 : p * 128 + 128
                ]


def observe(got, small):
    got = got.reshape(32, 4, 64, 128)
    small = small.reshape(32, 4, 16, 128)
    return pl.pallas_call(
        observe_kernel,
        grid=(4,),
        in_specs=[
            pl.BlockSpec((32, 1, 64, 128), lambda g: (0, g, 0, 0)),
            pl.BlockSpec((32, 1, 8, 128), lambda g: (0, g, 1, 0)),
        ],
        out_specs=pl.BlockSpec((2, 4, 256, 128), lambda g: (g, 0, 0, 0)),
        out_shape=jax.ShapeDtypeStruct((8, 4, 256, 128), F32),
        compiler_params=params(20),
        cost_estimate=pl.CostEstimate(flops=4 << 30, bytes_accessed=8 << 20, transcendentals=0),
        name="observe",
    )(got, small)


def depth_blur(x, taps):
    rows = [None] * 32
    for p in range(2):
        for m in range(16):
            rows[2 * m + p] = x[p * 128 + m * 8 : p * 128 + m * 8 + 8]
    layer = lax.broadcasted_iota(jnp.int32, rows[0].shape, 0)
    before = [jnp.where(layer == 0, 0.0, pltpu.roll(rows[32 - k], 1, 0)) for k in (3, 2, 1)]
    after = [jnp.where(layer == 7, 0.0, pltpu.roll(rows[k], 7, 0)) for k in (0, 1, 2)]
    e = before + rows + after
    out = [
        taps[0] * e[z + 3]
        + taps[1] * (e[z + 2] + e[z + 4])
        + (taps[2] * (e[z + 1] + e[z + 5]) + taps[3] * (e[z] + e[z + 6]))
        for z in range(32)
    ]
    return jnp.concatenate([out[2 * m + p] for p in range(2) for m in range(16)], axis=0)


def back_project(blurred, back_ref, total):
    total[...] = jnp.zeros_like(total)

    def step(pair, carry):
        rows = []
        for x in blurred(pair):
            halves = [split(side) for side in x]
            high = [h for h, _ in halves]
            low = [l for _, l in halves]
            rows.append(jnp.concatenate(high + low + high, axis=1))
        total[...] += dot(jnp.concatenate(rows, axis=0), back_ref[pair])
        return carry

    lax.fori_loop(0, 4, step, 0, unroll=True)


def finish_back(total, out_ref, own_ref, outs):
    for q in range(4):
        own_ref[q] = total[q * 256 : q * 256 + 256, :LAT]
    halo = jnp.concatenate([total[q * 256 : q * 256 + 256, LAT:] for q in range(4)], axis=1)
    to_messages(halo, out_ref, outs)


def cover_kernel(taps_ref, obs_ref, back_ref, out_ref, own_ref, *rest):
    outs, total = rest[:8], rest[8]

    def blurred(pair):
        for q in range(4):
            sides = []
            for i in range(2):
                taps = [taps_ref[0, 2 * pair + i, k] for k in range(RAD + 1)]
                sides.append(depth_blur((obs_ref[2 * pair + i, q] > 0.0).astype(F32), taps))
            yield sides

    back_project(blurred, back_ref, total)
    finish_back(total, out_ref, own_ref, outs)


def cover(taps, obs, back, leave):
    whole = pl.BlockSpec(memory_space=pltpu.VMEM)
    return pl.pallas_call(
        cover_kernel,
        in_specs=[pl.BlockSpec(memory_space=pltpu.SMEM)] + [whole] * 3,
        out_specs=[whole] * 9,
        out_shape=[jax.ShapeDtypeStruct((4, 256, LAT), F32)] + MESSAGES,
        scratch_shapes=[pltpu.VMEM((1024, EXT), F32)],
        compiler_params=params(20),
        cost_estimate=pl.CostEstimate(flops=6 << 30, bytes_accessed=8 << 20, transcendentals=0),
        name="cover",
    )(taps, obs, back, leave)


def sweep_kernel(taps_ref, obs_ref, fore_ref, back_ref, enter_ref, leave_ref, cur_ref, *refs):
    parts, beside, own_ref, outs = refs[:8], refs[8:-11], refs[-11], refs[-10:-2]
    total, ext = refs[-2:]
    for message, out in zip(beside, outs, strict=False):
        rows = message.shape[0]
        out[rows : 2 * rows, :] = message[...]

    def put(rows, at, x):
        high, low = split(x)
        for i, half in enumerate((high, low, high)):
            ext[rows, i * EXT + at : i * EXT + at + x.shape[1]] = half

    for q in range(4):
        put(slice(q * 256, q * 256 + 256), 0, cur_ref[q])
    for p, halo in enumerate(from_messages(parts, enter_ref)):
        for q in range(4):
            start = q * 256 + p * 128
            put(slice(start, start + 128), LAT, halo[:, q * HALO_PAD : (q + 1) * HALO_PAD])

    def blurred(pair):
        across = dot(ext[...], fore_ref[pair])
        for q in range(4):
            sides = []
            for i in range(2):
                w = 2 * pair + i
                taps = [taps_ref[0, w, k] for k in range(RAD + 1)]
                blur = depth_blur(across[q * 256 : q * 256 + 256, i * LAT : i * LAT + LAT], taps)
                near = pl.reciprocal(blur, approx=True)
                near = near * (2.0 - blur * near)
                sides.append(depth_blur(obs_ref[w, q] * near, taps))
            yield sides

    back_project(blurred, back_ref, total)
    finish_back(total, leave_ref, own_ref, outs)


def sweep(taps, obs, weights, enter, leave, cur, parts, beside=()):
    messages = [jax.ShapeDtypeStruct((m.shape[0] * (2 if beside else 1), 128), F32) for m in MESSAGES]
    whole = pl.BlockSpec(memory_space=pltpu.VMEM)
    return pl.pallas_call(
        sweep_kernel,
        in_specs=[pl.BlockSpec(memory_space=pltpu.SMEM)] + [whole] * (14 + len(beside)),
        out_specs=[whole] * 9,
        out_shape=[jax.ShapeDtypeStruct((4, 256, LAT), F32)] + messages,
        scratch_shapes=[pltpu.VMEM((1024, EXT), F32), pltpu.VMEM((1024, 3 * EXT), BF16)],
        compiler_params=params(26),
        cost_estimate=pl.CostEstimate(flops=12 << 30, bytes_accessed=12 << 20, transcendentals=0),
        name="sweep",
    )(taps, obs, *weights, enter, leave, cur, *parts, *beside)


def update_kernel(pick_ref, add_ref, cur_ref, cover_ref, total_ref, *refs):
    parts, cur_out, below_out, outs = refs[:8], refs[8], refs[9], refs[10:18]
    behind = [part.at[pl.ds(m.shape[0], m.shape[0])] for part, m in zip(parts, MESSAGES, strict=True)]
    total = add_messages(parts, add_ref, total_ref)
    cover = add_messages(behind, add_ref, cover_ref)
    for p in range(2):
        rows = slice(p * 128, p * 128 + 128)
        for q in range(4):
            lanes = slice(q * LAT, q * LAT + LAT)
            below = 1.0 + cover[p][:, lanes]
            below_out[q, rows, :] = below
            cur_out[q, rows, :] = cur_ref[q, rows, :] * (1.0 + total[p][:, lanes]) / below
    to_messages(quads(cur_out), pick_ref, outs)


def update(pick, add, cur, cover, total, parts):
    whole = pl.BlockSpec(memory_space=pltpu.VMEM)
    return pl.pallas_call(
        update_kernel,
        in_specs=[whole] * 13,
        out_specs=[whole] * 10,
        out_shape=[jax.ShapeDtypeStruct((4, 256, LAT), F32)] * 2 + MESSAGES,
        compiler_params=params(16),
        name="update",
    )(pick, add, cur, cover, total, *parts)


def last_kernel(add_ref, cur_ref, below_ref, total_ref, *refs):
    totals, out_ref, rows_ref = refs[:8], refs[8], refs[9]
    total = add_messages(totals, add_ref, total_ref)
    for p in range(2):
        rows = slice(p * 128, p * 128 + 128)
        for q in range(4):
            mine = total[p][:, q * LAT : q * LAT + LAT]
            done = cur_ref[q, rows, :] * (1.0 + mine) / below_ref[q, rows, :]
            for m in range(16):
                rows_ref[pl.ds(m * 8 + p * 4 + q, 8, stride=128), :] = done[m * 8 : m * 8 + 8]
    done = rows_ref[...].reshape(32, 32, 128)
    for v in range(4):
        out_ref[:, v] = done


def last_update(add, cur, below, total):
    whole = pl.BlockSpec(memory_space=pltpu.VMEM)
    out = pl.pallas_call(
        last_kernel,
        in_specs=[whole] * 12,
        out_specs=whole,
        out_shape=jax.ShapeDtypeStruct((32, 4, 32, 128), F32),
        scratch_shapes=[pltpu.VMEM((1024, 128), F32)],
        compiler_params=params(14),
        name="last_update",
    )(add, cur, below, *total)
    return out.reshape(128, 32, 128)


def place_kernel(got_ref, out_ref, side_ref):
    got = got_ref.reshape(4096, 128)
    for k in range(4):
        y, z = row_place(pl.program_id(0) * 4 + k)
        for tx in range(2):
            rows = turn([got[pl.ds(y * 1024 + column_place(c) * 128 + z * 32 + tx, 16, stride=2), :] for c in range(8)])
            side = side_ref.at[k * 2 + tx]
            for s in range(8):
                side[pl.ds(s, 16, stride=8), :] = rows[s]
            lanes = slice(tx * 128, tx * 128 + 128)
            out_ref[:, :, 0, k * 8 : k * 8 + 8, lanes] = side[...].reshape(8, 2, 8, 128)


def place_output(got):
    out = pl.pallas_call(
        place_kernel,
        grid=(4,),
        in_specs=[pl.BlockSpec((4, 8, 4, 32, 128), lambda y: (0, 0, 0, 0, 0))],
        out_specs=pl.BlockSpec((8, 2, 1, 32, 256), lambda y: (0, 0, y, 0, 0)),
        out_shape=jax.ShapeDtypeStruct((8, 2, 4, 32, 256), F32),
        scratch_shapes=[pltpu.VMEM((8, 128, 128), F32)],
        compiler_params=params(20),
        name="place_output",
    )(got.reshape(4, 8, 4, 32, 128))
    return out.reshape(8, 256, 256)


def gather_parts(parts):
    return [lax.ppermute(x, ALL, towards(-er, -ec)) for x, (er, ec) in zip(parts, DIRS, strict=True)]


def reduce_parts(parts):
    return [lax.ppermute(x, ALL, towards(er, ec)) for x, (er, ec) in zip(parts, DIRS, strict=True)]


def on_device(estimate, tiles, tile_block, tile_view, tile_slot, widths):
    block, view = lax.axis_index("block"), lax.axis_index("view")
    y, x, core = block // 8, block // 2 % 4, block % 2
    outward = jnp.where(y % 2 == 0, y * 3 + view - 1, y * 3 + 3 - view)
    r = jnp.where(view == 0, 15 - y, outward)
    c = jnp.where(core == 0, x, 7 - x)
    slot = tile_slot[0]
    deep = tile_block[0, :, 0] * 4 + slot // 4
    place = tile_view[0] * 512 + (slot % 4) * 128 + (deep % 16) * 8 + deep // 16
    place = jnp.where(jnp.arange(128) // 32 == block % 4, jnp.tile(place.astype(F32), 4), 0.0)
    own_widths = jnp.pad(widths.reshape(1, 6), ((1, 6), (0, 122)))
    meta = jnp.where(jnp.arange(8)[:, None] == 0, place[None, :], own_widths)
    send = small_message(view.reshape(1), estimate, meta)
    order, send = lax.optimization_barrier((view.reshape(1), send))
    small = lax.all_to_all(send, ALL, split_axis=0, concat_axis=0, tiled=True)
    send = tile_message(order, tiles[0])
    send, small = lax.optimization_barrier((send, small))
    got = lax.all_to_all(send, ALL, split_axis=0, concat_axis=0, tiled=True)

    add = (LANE_OWN[:, None] == np.arange(4 * LAT)[None, :]).astype(BF16)
    pick = (np.arange(4 * LAT)[:, None] == LANE_OWN[None, :]).astype(BF16)
    wrap_r = ((r + ER < 0) | (r + ER >= PR)).astype(jnp.int32) * ER
    wrap_c = ((c + EC < 0) | (c + EC >= PC)).astype(jnp.int32) * EC
    ty, tx = LANE_Q // 2 - wrap_r, LANE_Q % 2 - wrap_c
    inside = (LANE_Q >= 0) & (ty >= 0) & (ty < 2) & (tx >= 0) & (tx < 2)
    target = jnp.where(inside, (ty * 2 + tx) * HALO_PAD + LANE_HALO, -1)
    enter = (target[:, None] == jnp.arange(4 * HALO_PAD)[None, :]).astype(BF16)
    leave = (jnp.arange(4 * HALO_PAD)[:, None] == target[None, :]).astype(BF16)

    cur, *sent = begin(small, pick)
    parts = gather_parts(sent)
    spread = small[0:4, 9, 0:6].reshape(4, 3, 2).transpose(1, 0, 2).reshape(3, 8, 1)
    steps = jnp.arange(RAD + 1).astype(F32)
    raw = jnp.exp(-steps * steps / (2.0 * spread * spread))
    taps = raw / (2.0 * jnp.sum(raw, axis=2, keepdims=True) - raw[:, :, 0:1])
    weights = make_weights(taps)
    got, weights, taps = lax.optimization_barrier((got, weights, taps))
    obs = observe(got, small)
    obs, corners = lax.optimization_barrier((obs, parts[4:]))
    covered, *beside = cover(taps, obs, weights[1], leave)
    parts = parts[:4] + list(corners)
    own, *sent = sweep(taps, obs, weights, enter, leave, cur, parts, beside)
    cur, below, *sent = update(pick, add, cur, covered, own, reduce_parts(sent))
    parts = gather_parts(sent)
    own, *sent = sweep(taps, obs, weights, enter, leave, cur, parts)
    total = [own] + reduce_parts(sent)
    out = last_update(add, cur, below, total)
    out = lax.all_to_all(out, ALL, split_axis=0, concat_axis=0, tiled=True)
    return place_output(out)


def solution(mesh):
    placed = (
        P("block", None, None),
        P("view", "block", None, None, None),
        P("view", "block", None),
        P("view", "block"),
        P("view", "block"),
        P(None, "view"),
    )
    return jax.shard_map(
        on_device, mesh=mesh, in_specs=placed, out_specs=P("block", None, None), check_vma=False
    )
```

```python
import jax
import jax.numpy as jnp
import numpy as np
from jax import lax
from jax.experimental import pallas as pl
from jax.experimental.pallas import tpu as pltpu
from jax.sharding import PartitionSpec as P

RAD = 3
ITERS = 2
ALL = ("block", "view")
PR, PC = 16, 8
SR, SC = 8, 16
LAT = SR * SC
HALO_PAD = 256
EXT = LAT + HALO_PAD
F32, BF16 = jnp.float32, jnp.bfloat16

DIRS = [(0, -1), (0, 1), (-1, 0), (1, 0), (-1, -1), (-1, 1), (1, -1), (1, 1)]


def part_range(step, size):
    if step < 0:
        return list(range(-RAD, 0))
    if step > 0:
        return list(range(size, size + RAD))
    return list(range(size))


PARTS = [[(dr, dc) for dr in part_range(er, SR) for dc in part_range(ec, SC)] for er, ec in DIRS]
SIZES = [len(part) for part in PARTS]
HALO_AT = [sum(SIZES[:n]) for n in range(8)]
EXT_POS = [(s, j) for s in range(SR) for j in range(SC)] + [pos for part in PARTS for pos in part]
EXT_POS = EXT_POS + [(1000, 1000)] * (EXT - len(EXT_POS))


def row_place(r):
    y, k = r // 3, r % 3
    turned = y % 2
    z = 1 + k + turned * (2 - 2 * k)
    home = r // 12
    return y + home * (15 - r - y), z - home * z


def column_place(c):
    core = c // 4
    return (c % 4 + core * (3 - 2 * (c % 4))) * 2 + core


def device_of(r, c):
    y, z = row_place(r % PR)
    return (y * 8 + column_place(c % PC)) * 4 + z


def towards(er, ec):
    return [(device_of(r, c), device_of(r + er, c + ec)) for r in range(PR) for c in range(PC)]


def lane_table():
    main = [[-1] * 128 for _ in range(4)]
    aux = [[[-1] * 128 for _ in range(6)] for _ in range(2)]
    for n in range(8):
        for lane in range(4 * SIZES[n]):
            if n < 4 and lane < 128:
                main[n][lane] = (n, lane)
            else:
                for p in range(2):
                    if n < 4:
                        aux[p][n - 2][p * 64 + lane - 128] = (n, lane)
                    else:
                        aux[p][n - 2][p * 36 + lane] = (n, lane)
    return [x for row in main for x in row] + [x for kind in aux for row in kind for x in row]


LANES = lane_table()
LANE_N = np.array([0 if x == -1 else x[0] for x in LANES])
LANE_Q = np.array([-100 if x == -1 else x[1] // SIZES[x[0]] for x in LANES])
LANE_HALO = np.array([0 if x == -1 else HALO_AT[x[0]] + x[1] % SIZES[x[0]] for x in LANES])
LANE_OWN = np.array(
    [
        -1
        if x == -1
        else (x[1] // SIZES[x[0]]) * LAT
        + (PARTS[x[0]][x[1] % SIZES[x[0]]][0] % SR) * SC
        + PARTS[x[0]][x[1] % SIZES[x[0]]][1] % SC
        for x in LANES
    ]
)
ER = np.array([d[0] for d in DIRS])[LANE_N]
EC = np.array([d[1] for d in DIRS])[LANE_N]
N_MAIN, N_AUX = 512, 768


def params(mib):
    return pltpu.CompilerParams(vmem_limit_bytes=mib << 20)


def turn(rows):
    chunk = lax.broadcasted_iota(jnp.int32, rows[0].shape, 1) // SC
    for k in (4, 2, 1):
        low = (chunk & k) == 0
        after = list(rows)
        for a in range(8):
            if a & k == 0:
                x, y = rows[a], rows[a | k]
                after[a] = jnp.where(low, x, pltpu.roll(y, SC * k, 1))
                after[a | k] = jnp.where(low, pltpu.roll(x, 128 - SC * k, 1), y)
        rows = after
    return rows


def split(x):
    high = x.astype(BF16)
    return high, (x - high.astype(F32)).astype(BF16)


def dot(a, b):
    return jnp.dot(a, b, preferred_element_type=F32)


def send_small_kernel(view_ref, left_ref, right_ref, meta_ref, out_ref):
    left, right = left_ref.reshape(128, 128), right_ref.reshape(128, 128)
    rows = []
    for s in range(8):
        at = pl.ds(s, 16, stride=8)
        rows.append(jnp.concatenate([left[at, :], right[at, :]], axis=0))
    rows = turn(rows)
    for c in range(8):
        out_ref[0, column_place(c), 0:32, :] = rows[c]
        out_ref[0, column_place(c), 32:40, :] = meta_ref[...]


def patch_row(y, z):
    return jnp.where(z == 0, 15 - y, 3 * y + z - 1 + (y % 2) * (4 - 2 * z))


def small_message(view, estimate, meta):
    estimate = estimate.reshape(8, 2, 16, 8, 256)
    out = pl.pallas_call(
        send_small_kernel,
        grid_spec=pltpu.PrefetchScalarGridSpec(
            num_scalar_prefetch=1,
            grid=(4,),
            in_specs=[
                pl.BlockSpec((8, 2, 1, 8, 128), lambda y, v: (0, 0, patch_row(y, v[0]), 0, 0)),
                pl.BlockSpec((8, 2, 1, 8, 128), lambda y, v: (0, 0, patch_row(y, v[0]), 0, 1)),
                pl.BlockSpec((8, 128), lambda y, v: (0, 0)),
            ],
            out_specs=pl.BlockSpec((1, 8, 40, 128), lambda y, v: (y, 0, 0, 0)),
        ),
        out_shape=jax.ShapeDtypeStruct((4, 8, 40, 128), F32),
        compiler_params=params(56),
        name="small_message",
    )(view, estimate, estimate, meta)
    return out.reshape(32, 40, 128)


def send_tiles_kernel(view_ref, tiles_ref, out_ref):
    tiles = tiles_ref.reshape(2048, 128)
    for k in range(4):
        y, z = row_place(pl.program_id(0) * 4 + k)
        for p in range(2):
            rows = turn([tiles[pl.ds(p * 32 + k * 8 + s, 32, stride=64), :] for s in range(8)])
            for c in range(8):
                out_ref[y, column_place(c), z, p * 32 : p * 32 + 32, :] = rows[c]


def tile_message(view, tiles):
    out = pl.pallas_call(
        send_tiles_kernel,
        grid_spec=pltpu.PrefetchScalarGridSpec(
            num_scalar_prefetch=1,
            grid=(4,),
            in_specs=[pl.BlockSpec((32, 2, 32, 128), lambda y, v: (0, 0, y, 0))],
            out_specs=pl.BlockSpec((4, 8, 4, 64, 128), lambda y, v: (0, 0, 0, 0, 0)),
        ),
        out_shape=jax.ShapeDtypeStruct((4, 8, 4, 64, 128), F32),
        compiler_params=params(56),
        cost_estimate=pl.CostEstimate(flops=1 << 20, bytes_accessed=24 << 20, transcendentals=0),
        name="tile_message",
    )(view, tiles)
    return out.reshape(128, 64, 128)


def stacked(x):
    return jnp.concatenate(split(x), axis=0)


def dot_halves(x, table):
    out = dot(x, table)
    rows = out.shape[0] // 2
    return out[:rows] + out[rows:]


def aux_at(p):
    return slice(N_MAIN + p * N_AUX, N_MAIN + (p + 1) * N_AUX)


def to_messages(x, table_ref, outs):
    main = dot_halves(stacked(x), table_ref[:, :N_MAIN])
    aux = dot_halves(stacked(x[:128]), table_ref[:, aux_at(0)]) + dot_halves(stacked(x[128:]), table_ref[:, aux_at(1)])
    put_messages(main, aux, outs)


def from_messages(parts, table_ref):
    main = jnp.concatenate([parts[n][0:256, :] for n in range(4)], axis=1)
    aux = jnp.concatenate([parts[n][256:384, :] for n in (2, 3)] + [parts[n][0:128, :] for n in range(4, 8)], axis=1)
    main = dot_halves(stacked(main), table_ref[:N_MAIN, :])
    aux = stacked(aux)
    return [main[p * 128 : p * 128 + 128] + dot_halves(aux, table_ref[aux_at(p), :]) for p in range(2)]


def put_messages(main, aux, outs):
    for n in range(4):
        outs[n][0:256, :] = main[:, n * 128 : n * 128 + 128]
        if n >= 2:
            outs[n][256:384, :] = aux[:, (n - 2) * 128 : (n - 2) * 128 + 128]
    for n in range(4, 8):
        outs[n][0:128, :] = aux[:, (n - 2) * 128 : (n - 2) * 128 + 128]


MESSAGES = [jax.ShapeDtypeStruct((rows, 128), F32) for rows in (256, 256, 384, 384, 128, 128, 128, 128)]


def add_messages(parts, table_ref, base):
    out = []
    for p, term in enumerate(from_messages(parts, table_ref)):
        out.append(term + jnp.concatenate([base[q, p * 128 : p * 128 + 128, :] for q in range(4)], axis=1))
    return out


def quads(x):
    return jnp.concatenate([x[q] for q in range(4)], axis=1)


def begin_kernel(got_ref, pick_ref, cur_ref, *outs):
    got = got_ref.reshape(32 * 40, 128)
    for q in range(4):
        for p in range(2):
            for m in range(16):
                row = (m // 4) * 40 + (q % 2) * 16 + (2 * (m % 4) + p) * 2 + q // 2
                at = p * 128 + m * 8
                cur_ref[q, at : at + 8, :] = got[pl.ds(row, 8, stride=160), :]
    to_messages(quads(cur_ref), pick_ref, outs)


def begin(got, pick):
    return pl.pallas_call(
        begin_kernel,
        grid=(1,),
        in_specs=[
            pl.BlockSpec((32, 40, 128), lambda i: (0, 0, 0)),
            pl.BlockSpec((512, N_MAIN + 2 * N_AUX), lambda i: (0, 0)),
        ],
        out_specs=[pl.BlockSpec((4, 256, 128), lambda i: (0, 0, 0))]
        + [pl.BlockSpec(m.shape, lambda i: (0, 0)) for m in MESSAGES],
        out_shape=[jax.ShapeDtypeStruct((4, 256, 128), F32)] + MESSAGES,
        compiler_params=params(16),
        name="begin",
    )(got, pick)


def weight_kernel(taps_ref, er_ref, ec_ref, ert_ref, ect_ref, fore_ref, back_ref):
    def from_taps(apart, axis, w):
        far = jnp.abs(apart)
        out = jnp.zeros(apart.shape, F32)
        for k in range(RAD + 1):
            out = jnp.where(far == k, taps_ref[axis, w, k], out)
        return out

    lanes = lax.broadcasted_iota(jnp.int32, (EXT, LAT), 1)
    down, across = er_ref[...] - lanes // SC, ec_ref[...] - lanes % SC
    rows = lax.broadcasted_iota(jnp.int32, (LAT, EXT), 0)
    down_t, across_t = ert_ref[...] - rows // SC, ect_ref[...] - rows % SC
    for w in range(8):
        pair, at = w // 2, slice((w % 2) * LAT, (w % 2) * LAT + LAT)
        high, low = split(from_taps(down, 1, w) * from_taps(across, 2, w))
        for i, x in enumerate((high, high, low)):
            fore_ref[pair, i * EXT : i * EXT + EXT, at] = x
        high, low = split(from_taps(down_t, 1, w) * from_taps(across_t, 2, w))
        for i, x in enumerate((high, high, low)):
            start = i * 2 * LAT + (w % 2) * LAT
            back_ref[pair, start : start + LAT, :] = x


def make_weights(taps):
    ext = np.array(EXT_POS, np.int32)
    tall = [np.broadcast_to(ext[:, i][:, None], (EXT, LAT)) for i in range(2)]
    wide = [np.broadcast_to(ext[:, i][None, :], (LAT, EXT)) for i in range(2)]
    whole = pl.BlockSpec(memory_space=pltpu.VMEM)
    return pl.pallas_call(
        weight_kernel,
        in_specs=[pl.BlockSpec(memory_space=pltpu.SMEM)] + [whole] * 4,
        out_specs=[whole] * 2,
        out_shape=[
            jax.ShapeDtypeStruct((4, 3 * EXT, 2 * LAT), BF16),
            jax.ShapeDtypeStruct((4, 6 * LAT, EXT), BF16),
        ],
        compiler_params=params(20),
        name="make_weights",
    )(taps, *tall, *wide)


def observe_kernel(got_ref, place_ref, obs_ref):
    sides = []
    for p in range(2):
        sides.append(got_ref[:, 0, p * 32 : p * 32 + 32, :].reshape(1024, 128))
    high, low = split(jnp.concatenate(sides, axis=1))
    place = jnp.concatenate([place_ref[0, i : i + 1, :] for i in range(8)], axis=1)
    for half in range(4):
        rows = lax.broadcasted_iota(jnp.int32, (256, 1024), 0) + half * 256
        hot = (rows.astype(F32) == place).astype(F32)
        counts = jnp.sum(hot, axis=1, keepdims=True)
        hot = hot.astype(BF16)
        mean = (dot(hot, high) + dot(hot, low)) / jnp.maximum(counts, 1.0)
        for i in range(2):
            for p in range(2):
                obs_ref[half // 2, (half % 2) * 2 + i, p * 128 : p * 128 + 128, :] = mean[
                    i * 128 : i * 128 + 128, p * 128 : p * 128 + 128
                ]


def observe(got, places):
    got = got.reshape(32, 4, 64, 128)
    return pl.pallas_call(
        observe_kernel,
        grid=(4,),
        in_specs=[
            pl.BlockSpec((32, 1, 64, 128), lambda g: (0, g, 0, 0)),
            pl.BlockSpec((1, 8, 128), lambda g: (g, 0, 0)),
        ],
        out_specs=pl.BlockSpec((2, 4, 256, 128), lambda g: (g, 0, 0, 0)),
        out_shape=jax.ShapeDtypeStruct((8, 4, 256, 128), F32),
        compiler_params=params(20),
        cost_estimate=pl.CostEstimate(flops=4 << 30, bytes_accessed=8 << 20, transcendentals=0),
        name="observe",
    )(got, places)


def depth_blur(x, taps):
    rows = [None] * 32
    for p in range(2):
        for m in range(16):
            rows[2 * m + p] = x[p * 128 + m * 8 : p * 128 + m * 8 + 8]
    layer = lax.broadcasted_iota(jnp.int32, rows[0].shape, 0)
    before = [jnp.where(layer == 0, 0.0, pltpu.roll(rows[32 - k], 1, 0)) for k in (3, 2, 1)]
    after = [jnp.where(layer == 7, 0.0, pltpu.roll(rows[k], 7, 0)) for k in (0, 1, 2)]
    e = before + rows + after
    out = [
        taps[0] * e[z + 3]
        + taps[1] * (e[z + 2] + e[z + 4])
        + (taps[2] * (e[z + 1] + e[z + 5]) + taps[3] * (e[z] + e[z + 6]))
        for z in range(32)
    ]
    return jnp.concatenate([out[2 * m + p] for p in range(2) for m in range(16)], axis=0)


def back_project(blurred, back_ref, total):
    def step(pair):
        rows = []
        for x in blurred(pair):
            halves = [split(side) for side in x]
            high = [h for h, _ in halves]
            low = [l for _, l in halves]
            rows.append(jnp.concatenate(high + low + high, axis=1))
        return jnp.concatenate(rows, axis=0)

    sides = [step(pair) for pair in range(4)]
    total[...] = dot(jnp.concatenate(sides, axis=1), back_ref[...].reshape(4 * 6 * LAT, EXT))


def finish_back(total, out_ref, own_ref, outs):
    for q in range(4):
        own_ref[q] = total[q * 256 : q * 256 + 256, :LAT]
    halo = jnp.concatenate([total[q * 256 : q * 256 + 256, LAT:] for q in range(4)], axis=1)
    to_messages(halo, out_ref, outs)


def cover_kernel(taps_ref, obs_ref, back_ref, out_ref, own_ref, *rest):
    outs, total = rest[:8], rest[8]

    def blurred(pair):
        for q in range(4):
            sides = []
            for i in range(2):
                taps = [taps_ref[0, 2 * pair + i, k] for k in range(RAD + 1)]
                sides.append(depth_blur((obs_ref[2 * pair + i, q] > 0.0).astype(F32), taps))
            yield sides

    back_project(blurred, back_ref, total)
    finish_back(total, out_ref, own_ref, outs)


def cover(taps, obs, back, leave):
    whole = pl.BlockSpec(memory_space=pltpu.VMEM)
    return pl.pallas_call(
        cover_kernel,
        in_specs=[pl.BlockSpec(memory_space=pltpu.SMEM)] + [whole] * 3,
        out_specs=[whole] * 9,
        out_shape=[jax.ShapeDtypeStruct((4, 256, LAT), F32)] + MESSAGES,
        scratch_shapes=[pltpu.VMEM((1024, EXT), F32)],
        compiler_params=params(20),
        cost_estimate=pl.CostEstimate(flops=6 << 30, bytes_accessed=8 << 20, transcendentals=0),
        name="cover",
    )(taps, obs, back, leave)


def sweep_kernel(taps_ref, obs_ref, fore_ref, back_ref, enter_ref, leave_ref, cur_ref, *refs):
    parts, beside, own_ref, outs = refs[:8], refs[8:-11], refs[-11], refs[-10:-2]
    total, ext = refs[-2:]
    for message, out in zip(beside, outs, strict=False):
        rows = message.shape[0]
        out[rows : 2 * rows, :] = message[...]

    def put(rows, at, x):
        high, low = split(x)
        for i, half in enumerate((high, low, high)):
            ext[rows, i * EXT + at : i * EXT + at + x.shape[1]] = half

    for q in range(4):
        put(slice(q * 256, q * 256 + 256), 0, cur_ref[q])
    for p, halo in enumerate(from_messages(parts, enter_ref)):
        for q in range(4):
            start = q * 256 + p * 128
            put(slice(start, start + 128), LAT, halo[:, q * HALO_PAD : (q + 1) * HALO_PAD])

    def blurred(pair):
        across = dot(ext[...], fore_ref[pair])
        for q in range(4):
            sides = []
            for i in range(2):
                w = 2 * pair + i
                taps = [taps_ref[0, w, k] for k in range(RAD + 1)]
                blur = depth_blur(across[q * 256 : q * 256 + 256, i * LAT : i * LAT + LAT], taps)
                near = pl.reciprocal(blur, approx=True)
                near = near * (2.0 - blur * near)
                sides.append(depth_blur(obs_ref[w, q] * near, taps))
            yield sides

    back_project(blurred, back_ref, total)
    finish_back(total, leave_ref, own_ref, outs)


def sweep(taps, obs, weights, enter, leave, cur, parts, beside=()):
    messages = [jax.ShapeDtypeStruct((m.shape[0] * (2 if beside else 1), 128), F32) for m in MESSAGES]
    whole = pl.BlockSpec(memory_space=pltpu.VMEM)
    return pl.pallas_call(
        sweep_kernel,
        in_specs=[pl.BlockSpec(memory_space=pltpu.SMEM)] + [whole] * (14 + len(beside)),
        out_specs=[whole] * 9,
        out_shape=[jax.ShapeDtypeStruct((4, 256, LAT), F32)] + messages,
        scratch_shapes=[pltpu.VMEM((1024, EXT), F32), pltpu.VMEM((1024, 3 * EXT), BF16)],
        compiler_params=params(26),
        cost_estimate=pl.CostEstimate(flops=12 << 30, bytes_accessed=12 << 20, transcendentals=0),
        name="sweep",
    )(taps, obs, *weights, enter, leave, cur, *parts, *beside)


def update_kernel(pick_ref, add_ref, cur_ref, cover_ref, total_ref, *refs):
    parts, cur_out, below_out, outs = refs[:8], refs[8], refs[9], refs[10:18]
    behind = [part.at[pl.ds(m.shape[0], m.shape[0])] for part, m in zip(parts, MESSAGES, strict=True)]
    total = add_messages(parts, add_ref, total_ref)
    cover = add_messages(behind, add_ref, cover_ref)
    for p in range(2):
        rows = slice(p * 128, p * 128 + 128)
        for q in range(4):
            lanes = slice(q * LAT, q * LAT + LAT)
            below = 1.0 + cover[p][:, lanes]
            below_out[q, rows, :] = below
            cur_out[q, rows, :] = cur_ref[q, rows, :] * (1.0 + total[p][:, lanes]) / below
    to_messages(quads(cur_out), pick_ref, outs)


def update(pick, add, cur, cover, total, parts):
    whole = pl.BlockSpec(memory_space=pltpu.VMEM)
    return pl.pallas_call(
        update_kernel,
        in_specs=[whole] * 13,
        out_specs=[whole] * 10,
        out_shape=[jax.ShapeDtypeStruct((4, 256, LAT), F32)] * 2 + MESSAGES,
        compiler_params=params(16),
        name="update",
    )(pick, add, cur, cover, total, *parts)


def last_kernel(add_ref, cur_ref, below_ref, total_ref, *refs):
    totals, out_ref, rows_ref = refs[:8], refs[8], refs[9]
    total = add_messages(totals, add_ref, total_ref)
    for p in range(2):
        rows = slice(p * 128, p * 128 + 128)
        for q in range(4):
            mine = total[p][:, q * LAT : q * LAT + LAT]
            done = cur_ref[q, rows, :] * (1.0 + mine) / below_ref[q, rows, :]
            for m in range(16):
                rows_ref[pl.ds(m * 8 + p * 4 + q, 8, stride=128), :] = done[m * 8 : m * 8 + 8]
    done = rows_ref[...].reshape(32, 32, 128)
    for v in range(4):
        out_ref[:, v] = done


def last_update(add, cur, below, total):
    whole = pl.BlockSpec(memory_space=pltpu.VMEM)
    out = pl.pallas_call(
        last_kernel,
        in_specs=[whole] * 12,
        out_specs=whole,
        out_shape=jax.ShapeDtypeStruct((32, 4, 32, 128), F32),
        scratch_shapes=[pltpu.VMEM((1024, 128), F32)],
        compiler_params=params(14),
        name="last_update",
    )(add, cur, below, *total)
    return out.reshape(128, 32, 128)


def place_kernel(got_ref, out_ref, side_ref):
    got = got_ref.reshape(4096, 128)
    for k in range(4):
        y, z = row_place(pl.program_id(0) * 4 + k)
        for tx in range(2):
            rows = turn([got[pl.ds(y * 1024 + column_place(c) * 128 + z * 32 + tx, 16, stride=2), :] for c in range(8)])
            side = side_ref.at[k * 2 + tx]
            for s in range(8):
                side[pl.ds(s, 16, stride=8), :] = rows[s]
            lanes = slice(tx * 128, tx * 128 + 128)
            out_ref[:, :, 0, k * 8 : k * 8 + 8, lanes] = side[...].reshape(8, 2, 8, 128)


def place_output(got):
    out = pl.pallas_call(
        place_kernel,
        grid=(4,),
        in_specs=[pl.BlockSpec((4, 8, 4, 32, 128), lambda y: (0, 0, 0, 0, 0))],
        out_specs=pl.BlockSpec((8, 2, 1, 32, 256), lambda y: (0, 0, y, 0, 0)),
        out_shape=jax.ShapeDtypeStruct((8, 2, 4, 32, 256), F32),
        scratch_shapes=[pltpu.VMEM((8, 128, 128), F32)],
        compiler_params=params(20),
        name="place_output",
    )(got.reshape(4, 8, 4, 32, 128))
    return out.reshape(8, 256, 256)


def gather_parts(parts):
    return [lax.ppermute(x, ALL, towards(-er, -ec)) for x, (er, ec) in zip(parts, DIRS, strict=True)]


def reduce_parts(parts):
    return [lax.ppermute(x, ALL, towards(er, ec)) for x, (er, ec) in zip(parts, DIRS, strict=True)]


def from_views(x, view):
    others = [lax.ppermute(x, "view", [((i + k) % 4, i) for i in range(4)]) for k in range(1, 4)]
    ring = jnp.stack([x] + others)
    return lax.dynamic_slice_in_dim(jnp.concatenate([ring, ring]), (4 - view) % 4, 4, 0)


def on_device(estimate, tiles, tile_block, tile_view, tile_slot, widths):
    block, view = lax.axis_index("block"), lax.axis_index("view")
    y, x, core = block // 8, block // 2 % 4, block % 2
    r = patch_row(y, view)
    c = jnp.where(core == 0, x, 7 - x)
    slot = tile_slot[0]
    deep = tile_block[0, :, 0] * 4 + slot // 4
    place = tile_view[0] * 512 + (slot % 4) * 128 + (deep % 16) * 8 + deep // 16
    place = jnp.where(jnp.arange(128) // 32 == block % 4, jnp.tile(place.astype(F32), 4), 0.0)
    meta = jnp.broadcast_to(place[None], (8, 128))
    own_widths = jnp.pad(widths.reshape(1, 6), ((0, 7), (0, 122)))
    all_widths = from_views(own_widths, view)[:, 0, 0:6]
    send = small_message(view.reshape(1), estimate, meta)
    order, send = lax.optimization_barrier((view.reshape(1), send))
    small = lax.all_to_all(send, "block", split_axis=0, concat_axis=0, tiled=True)
    send = tile_message(order, tiles[0])
    send, small = lax.optimization_barrier((send, small))
    got = lax.all_to_all(send, ALL, split_axis=0, concat_axis=0, tiled=True)

    add = (LANE_OWN[:, None] == np.arange(4 * LAT)[None, :]).astype(BF16)
    pick = (np.arange(4 * LAT)[:, None] == LANE_OWN[None, :]).astype(BF16)
    wrap_r = ((r + ER < 0) | (r + ER >= PR)).astype(jnp.int32) * ER
    wrap_c = ((c + EC < 0) | (c + EC >= PC)).astype(jnp.int32) * EC
    ty, tx = LANE_Q // 2 - wrap_r, LANE_Q % 2 - wrap_c
    inside = (LANE_Q >= 0) & (ty >= 0) & (ty < 2) & (tx >= 0) & (tx < 2)
    target = jnp.where(inside, (ty * 2 + tx) * HALO_PAD + LANE_HALO, -1)
    enter = (target[:, None] == jnp.arange(4 * HALO_PAD)[None, :]).astype(BF16)
    leave = (jnp.arange(4 * HALO_PAD)[:, None] == target[None, :]).astype(BF16)

    cur, *sent = begin(small, pick)
    parts = gather_parts(sent)
    places = from_views(small[:, 32, :].reshape(8, 4, 128).sum(1), view)
    spread = all_widths.reshape(4, 3, 2).transpose(1, 0, 2).reshape(3, 8, 1)
    steps = jnp.arange(RAD + 1).astype(F32)
    raw = jnp.exp(-steps * steps / (2.0 * spread * spread))
    taps = raw / (2.0 * jnp.sum(raw, axis=2, keepdims=True) - raw[:, :, 0:1])
    weights = make_weights(taps)
    got, weights, taps, places = lax.optimization_barrier((got, weights, taps, places))
    obs = observe(got, places)
    obs, corners = lax.optimization_barrier((obs, parts[4:]))
    covered, *beside = cover(taps, obs, weights[1], leave)
    parts = parts[:4] + list(corners)
    own, *sent = sweep(taps, obs, weights, enter, leave, cur, parts, beside)
    cur, below, *sent = update(pick, add, cur, covered, own, reduce_parts(sent))
    parts = gather_parts(sent)
    own, *sent = sweep(taps, obs, weights, enter, leave, cur, parts)
    total = [own] + reduce_parts(sent)
    out = last_update(add, cur, below, total)
    out = lax.all_to_all(out, ALL, split_axis=0, concat_axis=0, tiled=True)
    return place_output(out)


def solution(mesh):
    placed = (
        P("block", None, None),
        P("view", "block", None, None, None),
        P("view", "block", None),
        P("view", "block"),
        P("view", "block"),
        P(None, "view"),
    )
    return jax.shard_map(
        on_device, mesh=mesh, in_specs=placed, out_specs=P("block", None, None), check_vma=False
    )
```

```python
import jax
import jax.numpy as jnp
import numpy as np
from jax import lax
from jax.experimental import pallas as pl
from jax.experimental.pallas import tpu as pltpu
from jax.sharding import PartitionSpec as P

RAD = 3
ITERS = 2
ALL = ("block", "view")
PR, PC = 16, 8
SR, SC = 8, 16
LAT = SR * SC
HALO_PAD = 256
EXT = LAT + HALO_PAD
F32, BF16 = jnp.float32, jnp.bfloat16

DIRS = [(0, -1), (0, 1), (-1, 0), (1, 0), (-1, -1), (-1, 1), (1, -1), (1, 1)]


def part_range(step, size):
    if step < 0:
        return list(range(-RAD, 0))
    if step > 0:
        return list(range(size, size + RAD))
    return list(range(size))


PARTS = [[(dr, dc) for dr in part_range(er, SR) for dc in part_range(ec, SC)] for er, ec in DIRS]
SIZES = [len(part) for part in PARTS]
HALO_AT = [sum(SIZES[:n]) for n in range(8)]
EXT_POS = [(s, j) for s in range(SR) for j in range(SC)] + [pos for part in PARTS for pos in part]
EXT_POS = EXT_POS + [(1000, 1000)] * (EXT - len(EXT_POS))


def row_place(r):
    y, k = r // 3, r % 3
    turned = y % 2
    z = 1 + k + turned * (2 - 2 * k)
    home = r // 12
    return y + home * (15 - r - y), z - home * z


def column_place(c):
    core = c // 4
    return (c % 4 + core * (3 - 2 * (c % 4))) * 2 + core


def device_of(r, c):
    y, z = row_place(r % PR)
    return (y * 8 + column_place(c % PC)) * 4 + z


def towards(er, ec):
    return [(device_of(r, c), device_of(r + er, c + ec)) for r in range(PR) for c in range(PC)]


def lane_table():
    main = [[-1] * 128 for _ in range(4)]
    aux = [[[-1] * 128 for _ in range(6)] for _ in range(2)]
    for n in range(8):
        for lane in range(4 * SIZES[n]):
            if n < 4 and lane < 128:
                main[n][lane] = (n, lane)
            else:
                for p in range(2):
                    if n < 4:
                        aux[p][n - 2][p * 64 + lane - 128] = (n, lane)
                    else:
                        aux[p][n - 2][p * 36 + lane] = (n, lane)
    return [x for row in main for x in row] + [x for kind in aux for row in kind for x in row]


LANES = lane_table()
LANE_N = np.array([0 if x == -1 else x[0] for x in LANES])
LANE_Q = np.array([-100 if x == -1 else x[1] // SIZES[x[0]] for x in LANES])
LANE_HALO = np.array([0 if x == -1 else HALO_AT[x[0]] + x[1] % SIZES[x[0]] for x in LANES])
LANE_OWN = np.array(
    [
        -1
        if x == -1
        else (x[1] // SIZES[x[0]]) * LAT
        + (PARTS[x[0]][x[1] % SIZES[x[0]]][0] % SR) * SC
        + PARTS[x[0]][x[1] % SIZES[x[0]]][1] % SC
        for x in LANES
    ]
)
ER = np.array([d[0] for d in DIRS])[LANE_N]
EC = np.array([d[1] for d in DIRS])[LANE_N]
N_MAIN, N_AUX = 512, 768


def params(mib):
    return pltpu.CompilerParams(vmem_limit_bytes=mib << 20)


def turn(rows):
    chunk = lax.broadcasted_iota(jnp.int32, rows[0].shape, 1) // SC
    for k in (4, 2, 1):
        low = (chunk & k) == 0
        after = list(rows)
        for a in range(8):
            if a & k == 0:
                x, y = rows[a], rows[a | k]
                after[a] = jnp.where(low, x, pltpu.roll(y, SC * k, 1))
                after[a | k] = jnp.where(low, pltpu.roll(x, 128 - SC * k, 1), y)
        rows = after
    return rows


def split(x):
    high = x.astype(BF16)
    return high, (x - high.astype(F32)).astype(BF16)


def dot(a, b):
    return jnp.dot(a, b, preferred_element_type=F32)


def send_small_kernel(view_ref, left_ref, right_ref, meta_ref, out_ref):
    left, right = left_ref.reshape(128, 128), right_ref.reshape(128, 128)
    rows = []
    for s in range(8):
        at = pl.ds(s, 16, stride=8)
        rows.append(jnp.concatenate([left[at, :], right[at, :]], axis=0))
    rows = turn(rows)
    for c in range(8):
        out_ref[0, column_place(c), 0:32, :] = rows[c]
        out_ref[0, column_place(c), 32:40, :] = meta_ref[...]


def patch_row(y, z):
    return jnp.where(z == 0, 15 - y, 3 * y + z - 1 + (y % 2) * (4 - 2 * z))


def small_message(view, estimate, meta):
    estimate = estimate.reshape(8, 2, 16, 8, 256)
    out = pl.pallas_call(
        send_small_kernel,
        grid_spec=pltpu.PrefetchScalarGridSpec(
            num_scalar_prefetch=1,
            grid=(4,),
            in_specs=[
                pl.BlockSpec((8, 2, 1, 8, 128), lambda y, v: (0, 0, patch_row(y, v[0]), 0, 0)),
                pl.BlockSpec((8, 2, 1, 8, 128), lambda y, v: (0, 0, patch_row(y, v[0]), 0, 1)),
                pl.BlockSpec((8, 128), lambda y, v: (0, 0)),
            ],
            out_specs=pl.BlockSpec((1, 8, 40, 128), lambda y, v: (y, 0, 0, 0)),
        ),
        out_shape=jax.ShapeDtypeStruct((4, 8, 40, 128), F32),
        compiler_params=params(56),
        name="small_message",
    )(view, estimate, estimate, meta)
    return out.reshape(32, 40, 128)


def send_tiles_kernel(view_ref, tiles_ref, out_ref):
    tiles = tiles_ref.reshape(2048, 128)
    for k in range(4):
        y, z = row_place(pl.program_id(0) * 4 + k)
        for p in range(2):
            rows = turn([tiles[pl.ds(p * 32 + k * 8 + s, 32, stride=64), :] for s in range(8)])
            for c in range(8):
                out_ref[y, column_place(c), z, p * 32 : p * 32 + 32, :] = rows[c]


def tile_message(view, tiles):
    out = pl.pallas_call(
        send_tiles_kernel,
        grid_spec=pltpu.PrefetchScalarGridSpec(
            num_scalar_prefetch=1,
            grid=(4,),
            in_specs=[pl.BlockSpec((32, 2, 32, 128), lambda y, v: (0, 0, y, 0))],
            out_specs=pl.BlockSpec((4, 8, 4, 64, 128), lambda y, v: (0, 0, 0, 0, 0)),
        ),
        out_shape=jax.ShapeDtypeStruct((4, 8, 4, 64, 128), F32),
        compiler_params=params(56),
        cost_estimate=pl.CostEstimate(flops=1 << 20, bytes_accessed=24 << 20, transcendentals=0),
        name="tile_message",
    )(view, tiles)
    return out.reshape(128, 64, 128)


def stacked(x):
    return jnp.concatenate(split(x), axis=0)


def dot_halves(x, table):
    out = dot(x, table)
    rows = out.shape[0] // 2
    return out[:rows] + out[rows:]


def aux_at(p):
    return slice(N_MAIN + p * N_AUX, N_MAIN + (p + 1) * N_AUX)


def to_messages(x, table_ref, outs):
    main = dot_halves(stacked(x), table_ref[:, :N_MAIN])
    aux = dot_halves(stacked(x[:128]), table_ref[:, aux_at(0)]) + dot_halves(stacked(x[128:]), table_ref[:, aux_at(1)])
    put_messages(main, aux, outs)


def from_messages(parts, table_ref):
    main = jnp.concatenate([parts[n][0:256, :] for n in range(4)], axis=1)
    aux = jnp.concatenate([parts[n][256:384, :] for n in (2, 3)] + [parts[n][0:128, :] for n in range(4, 8)], axis=1)
    main = dot_halves(stacked(main), table_ref[:N_MAIN, :])
    aux = stacked(aux)
    return [main[p * 128 : p * 128 + 128] + dot_halves(aux, table_ref[aux_at(p), :]) for p in range(2)]


def put_messages(main, aux, outs):
    for n in range(4):
        outs[n][0:256, :] = main[:, n * 128 : n * 128 + 128]
        if n >= 2:
            outs[n][256:384, :] = aux[:, (n - 2) * 128 : (n - 2) * 128 + 128]
    for n in range(4, 8):
        outs[n][0:128, :] = aux[:, (n - 2) * 128 : (n - 2) * 128 + 128]


MESSAGES = [jax.ShapeDtypeStruct((rows, 128), F32) for rows in (256, 256, 384, 384, 128, 128, 128, 128)]


def add_messages(parts, table_ref, base):
    out = []
    for p, term in enumerate(from_messages(parts, table_ref)):
        out.append(term + jnp.concatenate([base[q, p * 128 : p * 128 + 128, :] for q in range(4)], axis=1))
    return out


def quads(x):
    return jnp.concatenate([x[q] for q in range(4)], axis=1)


def begin_kernel(got_ref, pick_ref, cur_ref, *outs):
    got = got_ref.reshape(32 * 40, 128)
    for q in range(4):
        for p in range(2):
            for m in range(16):
                row = (m // 4) * 40 + (q % 2) * 16 + (2 * (m % 4) + p) * 2 + q // 2
                at = p * 128 + m * 8
                cur_ref[q, at : at + 8, :] = got[pl.ds(row, 8, stride=160), :]
    to_messages(quads(cur_ref), pick_ref, outs)


def begin(got, pick):
    return pl.pallas_call(
        begin_kernel,
        grid=(1,),
        in_specs=[
            pl.BlockSpec((32, 40, 128), lambda i: (0, 0, 0)),
            pl.BlockSpec((512, N_MAIN + 2 * N_AUX), lambda i: (0, 0)),
        ],
        out_specs=[pl.BlockSpec((4, 256, 128), lambda i: (0, 0, 0))]
        + [pl.BlockSpec(m.shape, lambda i: (0, 0)) for m in MESSAGES],
        out_shape=[jax.ShapeDtypeStruct((4, 256, 128), F32)] + MESSAGES,
        compiler_params=params(16),
        name="begin",
    )(got, pick)


def weight_kernel(taps_ref, er_ref, ec_ref, ert_ref, ect_ref, fore_ref, back_ref):
    def from_taps(apart, axis, w):
        far = jnp.abs(apart)
        out = jnp.zeros(apart.shape, F32)
        for k in range(RAD + 1):
            out = jnp.where(far == k, taps_ref[axis, w, k], out)
        return out

    lanes = lax.broadcasted_iota(jnp.int32, (EXT, LAT), 1)
    down, across = er_ref[...] - lanes // SC, ec_ref[...] - lanes % SC
    rows = lax.broadcasted_iota(jnp.int32, (LAT, EXT), 0)
    down_t, across_t = ert_ref[...] - rows // SC, ect_ref[...] - rows % SC
    for w in range(8):
        pair, at = w // 2, slice((w % 2) * LAT, (w % 2) * LAT + LAT)
        high, low = split(from_taps(down, 1, w) * from_taps(across, 2, w))
        for i, x in enumerate((high, high, low)):
            fore_ref[pair, i * EXT : i * EXT + EXT, at] = x
        high, low = split(from_taps(down_t, 1, w) * from_taps(across_t, 2, w))
        for i, x in enumerate((high, high, low)):
            start = i * 2 * LAT + (w % 2) * LAT
            back_ref[pair, start : start + LAT, :] = x


def make_weights(taps):
    ext = np.array(EXT_POS, np.int32)
    tall = [np.broadcast_to(ext[:, i][:, None], (EXT, LAT)) for i in range(2)]
    wide = [np.broadcast_to(ext[:, i][None, :], (LAT, EXT)) for i in range(2)]
    whole = pl.BlockSpec(memory_space=pltpu.VMEM)
    return pl.pallas_call(
        weight_kernel,
        in_specs=[pl.BlockSpec(memory_space=pltpu.SMEM)] + [whole] * 4,
        out_specs=[whole] * 2,
        out_shape=[
            jax.ShapeDtypeStruct((4, 3 * EXT, 2 * LAT), BF16),
            jax.ShapeDtypeStruct((4, 6 * LAT, EXT), BF16),
        ],
        compiler_params=params(20),
        name="make_weights",
    )(taps, *tall, *wide)


def observe_kernel(got_ref, place_ref, obs_ref):
    sides = []
    for p in range(2):
        sides.append(got_ref[:, 0, p * 32 : p * 32 + 32, :].reshape(1024, 128))
    high, low = split(jnp.concatenate(sides, axis=1))
    place = jnp.concatenate([place_ref[0, i : i + 1, :] for i in range(8)], axis=1)
    for half in range(4):
        rows = lax.broadcasted_iota(jnp.int32, (256, 1024), 0) + half * 256
        hot = (rows.astype(F32) == place).astype(F32)
        counts = jnp.sum(hot, axis=1, keepdims=True)
        hot = hot.astype(BF16)
        mean = (dot(hot, high) + dot(hot, low)) / jnp.maximum(counts, 1.0)
        for i in range(2):
            for p in range(2):
                obs_ref[half // 2, (half % 2) * 2 + i, p * 128 : p * 128 + 128, :] = mean[
                    i * 128 : i * 128 + 128, p * 128 : p * 128 + 128
                ]


def observe(got, places):
    got = got.reshape(32, 4, 64, 128)
    return pl.pallas_call(
        observe_kernel,
        grid=(4,),
        in_specs=[
            pl.BlockSpec((32, 1, 64, 128), lambda g: (0, g, 0, 0)),
            pl.BlockSpec((1, 8, 128), lambda g: (g, 0, 0)),
        ],
        out_specs=pl.BlockSpec((2, 4, 256, 128), lambda g: (g, 0, 0, 0)),
        out_shape=jax.ShapeDtypeStruct((8, 4, 256, 128), F32),
        compiler_params=params(20),
        cost_estimate=pl.CostEstimate(flops=4 << 30, bytes_accessed=8 << 20, transcendentals=0),
        name="observe",
    )(got, places)


def depth_blur(x, taps):
    rows = [None] * 32
    for p in range(2):
        for m in range(16):
            rows[2 * m + p] = x[p * 128 + m * 8 : p * 128 + m * 8 + 8]
    layer = lax.broadcasted_iota(jnp.int32, rows[0].shape, 0)
    before = [jnp.where(layer == 0, 0.0, pltpu.roll(rows[32 - k], 1, 0)) for k in (3, 2, 1)]
    after = [jnp.where(layer == 7, 0.0, pltpu.roll(rows[k], 7, 0)) for k in (0, 1, 2)]
    e = before + rows + after
    out = [
        taps[0] * e[z + 3]
        + taps[1] * (e[z + 2] + e[z + 4])
        + (taps[2] * (e[z + 1] + e[z + 5]) + taps[3] * (e[z] + e[z + 6]))
        for z in range(32)
    ]
    return jnp.concatenate([out[2 * m + p] for p in range(2) for m in range(16)], axis=0)


def back_project(blurred, back_ref, total):
    def step(pair):
        rows = []
        for x in blurred(pair):
            halves = [split(side) for side in x]
            high = [h for h, _ in halves]
            low = [l for _, l in halves]
            rows.append(jnp.concatenate(high + low + high, axis=1))
        return jnp.concatenate(rows, axis=0)

    sides = [step(pair) for pair in range(4)]
    total[...] = dot(jnp.concatenate(sides, axis=1), back_ref[...].reshape(4 * 6 * LAT, EXT))


def finish_back(total, out_ref, own_ref, outs):
    for q in range(4):
        own_ref[q] = total[q * 256 : q * 256 + 256, :LAT]
    halo = jnp.concatenate([total[q * 256 : q * 256 + 256, LAT:] for q in range(4)], axis=1)
    to_messages(halo, out_ref, outs)


def cover_kernel(taps_ref, obs_ref, back_ref, out_ref, own_ref, *rest):
    outs, total = rest[:8], rest[8]

    def blurred(pair):
        for q in range(4):
            sides = []
            for i in range(2):
                taps = [taps_ref[0, 2 * pair + i, k] for k in range(RAD + 1)]
                sides.append(depth_blur((obs_ref[2 * pair + i, q] > 0.0).astype(F32), taps))
            yield sides

    back_project(blurred, back_ref, total)
    finish_back(total, out_ref, own_ref, outs)


def cover(taps, obs, back, leave):
    whole = pl.BlockSpec(memory_space=pltpu.VMEM)
    return pl.pallas_call(
        cover_kernel,
        in_specs=[pl.BlockSpec(memory_space=pltpu.SMEM)] + [whole] * 3,
        out_specs=[whole] * 9,
        out_shape=[jax.ShapeDtypeStruct((4, 256, LAT), F32)] + MESSAGES,
        scratch_shapes=[pltpu.VMEM((1024, EXT), F32)],
        compiler_params=params(20),
        cost_estimate=pl.CostEstimate(flops=6 << 30, bytes_accessed=8 << 20, transcendentals=0),
        name="cover",
    )(taps, obs, back, leave)


def sweep_kernel(taps_ref, obs_ref, fore_ref, back_ref, enter_ref, leave_ref, cur_ref, *refs):
    parts, beside, own_ref, outs = refs[:8], refs[8:-11], refs[-11], refs[-10:-2]
    total, ext = refs[-2:]
    for message, out in zip(beside, outs, strict=False):
        rows = message.shape[0]
        out[rows : 2 * rows, :] = message[...]

    def put(rows, at, x):
        high, low = split(x)
        for i, half in enumerate((high, low, high)):
            ext[rows, i * EXT + at : i * EXT + at + x.shape[1]] = half

    for q in range(4):
        put(slice(q * 256, q * 256 + 256), 0, cur_ref[q])
    for p, halo in enumerate(from_messages(parts, enter_ref)):
        for q in range(4):
            start = q * 256 + p * 128
            put(slice(start, start + 128), LAT, halo[:, q * HALO_PAD : (q + 1) * HALO_PAD])

    def blurred(pair):
        across = dot(ext[...], fore_ref[pair])
        for q in range(4):
            sides = []
            for i in range(2):
                w = 2 * pair + i
                taps = [taps_ref[0, w, k] for k in range(RAD + 1)]
                blur = depth_blur(across[q * 256 : q * 256 + 256, i * LAT : i * LAT + LAT], taps)
                near = pl.reciprocal(blur, approx=True)
                near = near * (2.0 - blur * near)
                sides.append(depth_blur(obs_ref[w, q] * near, taps))
            yield sides

    back_project(blurred, back_ref, total)
    finish_back(total, leave_ref, own_ref, outs)


def sweep(taps, obs, weights, enter, leave, cur, parts, beside=()):
    messages = [jax.ShapeDtypeStruct((m.shape[0] * (2 if beside else 1), 128), F32) for m in MESSAGES]
    whole = pl.BlockSpec(memory_space=pltpu.VMEM)
    return pl.pallas_call(
        sweep_kernel,
        in_specs=[pl.BlockSpec(memory_space=pltpu.SMEM)] + [whole] * (14 + len(beside)),
        out_specs=[whole] * 9,
        out_shape=[jax.ShapeDtypeStruct((4, 256, LAT), F32)] + messages,
        scratch_shapes=[pltpu.VMEM((1024, EXT), F32), pltpu.VMEM((1024, 3 * EXT), BF16)],
        compiler_params=params(26),
        cost_estimate=pl.CostEstimate(flops=12 << 30, bytes_accessed=12 << 20, transcendentals=0),
        name="sweep",
    )(taps, obs, *weights, enter, leave, cur, *parts, *beside)


def update_kernel(pick_ref, add_ref, cur_ref, cover_ref, total_ref, *refs):
    parts, cur_out, below_out, outs = refs[:8], refs[8], refs[9], refs[10:18]
    behind = [part.at[pl.ds(m.shape[0], m.shape[0])] for part, m in zip(parts, MESSAGES, strict=True)]
    total = add_messages(parts, add_ref, total_ref)
    cover = add_messages(behind, add_ref, cover_ref)
    for p in range(2):
        rows = slice(p * 128, p * 128 + 128)
        for q in range(4):
            lanes = slice(q * LAT, q * LAT + LAT)
            below = 1.0 + cover[p][:, lanes]
            below_out[q, rows, :] = below
            cur_out[q, rows, :] = cur_ref[q, rows, :] * (1.0 + total[p][:, lanes]) / below
    to_messages(quads(cur_out), pick_ref, outs)


def update(pick, add, cur, cover, total, parts):
    whole = pl.BlockSpec(memory_space=pltpu.VMEM)
    return pl.pallas_call(
        update_kernel,
        in_specs=[whole] * 13,
        out_specs=[whole] * 10,
        out_shape=[jax.ShapeDtypeStruct((4, 256, LAT), F32)] * 2 + MESSAGES,
        compiler_params=params(16),
        name="update",
    )(pick, add, cur, cover, total, *parts)


def last_kernel(add_ref, cur_ref, below_ref, total_ref, *refs):
    totals, out_ref, rows_ref = refs[:8], refs[8], refs[9]
    total = add_messages(totals, add_ref, total_ref)
    for p in range(2):
        rows = slice(p * 128, p * 128 + 128)
        for q in range(4):
            mine = total[p][:, q * LAT : q * LAT + LAT]
            done = cur_ref[q, rows, :] * (1.0 + mine) / below_ref[q, rows, :]
            for m in range(16):
                rows_ref[pl.ds(m * 8 + p * 4 + q, 8, stride=128), :] = done[m * 8 : m * 8 + 8]
    done = rows_ref[...].reshape(32, 32, 128)
    for v in range(4):
        out_ref[:, v] = done


def last_update(add, cur, below, total):
    whole = pl.BlockSpec(memory_space=pltpu.VMEM)
    out = pl.pallas_call(
        last_kernel,
        in_specs=[whole] * 12,
        out_specs=whole,
        out_shape=jax.ShapeDtypeStruct((32, 4, 32, 128), F32),
        scratch_shapes=[pltpu.VMEM((1024, 128), F32)],
        compiler_params=params(14),
        name="last_update",
    )(add, cur, below, *total)
    return out.reshape(128, 32, 128)


def place_kernel(got_ref, out_ref, side_ref):
    got = got_ref.reshape(4096, 128)
    for k in range(4):
        y, z = row_place(pl.program_id(0) * 4 + k)
        for tx in range(2):
            rows = turn([got[pl.ds(y * 1024 + column_place(c) * 128 + z * 32 + tx, 16, stride=2), :] for c in range(8)])
            side = side_ref.at[k * 2 + tx]
            for s in range(8):
                side[pl.ds(s, 16, stride=8), :] = rows[s]
            lanes = slice(tx * 128, tx * 128 + 128)
            out_ref[:, :, 0, k * 8 : k * 8 + 8, lanes] = side[...].reshape(8, 2, 8, 128)


def place_output(got):
    out = pl.pallas_call(
        place_kernel,
        grid=(4,),
        in_specs=[pl.BlockSpec((4, 8, 4, 32, 128), lambda y: (0, 0, 0, 0, 0))],
        out_specs=pl.BlockSpec((8, 2, 1, 32, 256), lambda y: (0, 0, y, 0, 0)),
        out_shape=jax.ShapeDtypeStruct((8, 2, 4, 32, 256), F32),
        scratch_shapes=[pltpu.VMEM((8, 128, 128), F32)],
        compiler_params=params(20),
        name="place_output",
    )(got.reshape(4, 8, 4, 32, 128))
    return out.reshape(8, 256, 256)


def gather_parts(parts):
    return [lax.ppermute(x, ALL, towards(-er, -ec)) for x, (er, ec) in zip(parts, DIRS, strict=True)]


def reduce_parts(parts):
    return [lax.ppermute(x, ALL, towards(er, ec)) for x, (er, ec) in zip(parts, DIRS, strict=True)]


def from_views(x, view):
    others = [lax.ppermute(x, "view", [((i + k) % 4, i) for i in range(4)]) for k in range(1, 4)]
    ring = jnp.stack([x] + others)
    return lax.dynamic_slice_in_dim(jnp.concatenate([ring, ring]), (4 - view) % 4, 4, 0)


def on_device(estimate, tiles, tile_block, tile_view, tile_slot, widths):
    block, view = lax.axis_index("block"), lax.axis_index("view")
    y, x, core = block // 8, block // 2 % 4, block % 2
    r = patch_row(y, view)
    c = jnp.where(core == 0, x, 7 - x)
    slot = tile_slot[0]
    deep = tile_block[0, :, 0] * 4 + slot // 4
    place = tile_view[0] * 512 + (slot % 4) * 128 + (deep % 16) * 8 + deep // 16
    place = jnp.where(jnp.arange(128) // 32 == block % 4, jnp.tile(place.astype(F32), 4), 0.0)
    own_widths = jnp.pad(widths.reshape(1, 6), ((1, 6), (0, 122)))
    meta = jnp.where(jnp.arange(8)[:, None] == 0, place[None, :], own_widths)
    metas = from_views(meta, view)
    all_widths = metas[:, 1, 0:6]
    meta = jnp.concatenate([metas[:, 0, :], jnp.zeros((4, 128), F32)])
    send = small_message(view.reshape(1), estimate, meta)
    order, send = lax.optimization_barrier((view.reshape(1), send))
    small = lax.all_to_all(send, "block", split_axis=0, concat_axis=0, tiled=True)
    send = tile_message(order, tiles[0])
    send, small, r = lax.optimization_barrier((send, small, r))
    got = lax.all_to_all(send, ALL, split_axis=0, concat_axis=0, tiled=True)

    add = (LANE_OWN[:, None] == np.arange(4 * LAT)[None, :]).astype(BF16)
    pick = (np.arange(4 * LAT)[:, None] == LANE_OWN[None, :]).astype(BF16)
    wrap_r = ((r + ER < 0) | (r + ER >= PR)).astype(jnp.int32) * ER
    wrap_c = ((c + EC < 0) | (c + EC >= PC)).astype(jnp.int32) * EC
    ty, tx = LANE_Q // 2 - wrap_r, LANE_Q % 2 - wrap_c
    inside = (LANE_Q >= 0) & (ty >= 0) & (ty < 2) & (tx >= 0) & (tx < 2)
    target = jnp.where(inside, (ty * 2 + tx) * HALO_PAD + LANE_HALO, -1)
    enter = (target[:, None] == jnp.arange(4 * HALO_PAD)[None, :]).astype(BF16)
    leave = (jnp.arange(4 * HALO_PAD)[:, None] == target[None, :]).astype(BF16)

    cur, *sent = begin(small, pick)
    parts = gather_parts(sent)
    places = small[:, 32:36, :].reshape(8, 4, 4, 128).sum(1).transpose(1, 0, 2)
    spread = all_widths.reshape(4, 3, 2).transpose(1, 0, 2).reshape(3, 8, 1)
    steps = jnp.arange(RAD + 1).astype(F32)
    raw = jnp.exp(-steps * steps / (2.0 * spread * spread))
    taps = raw / (2.0 * jnp.sum(raw, axis=2, keepdims=True) - raw[:, :, 0:1])
    weights = make_weights(taps)
    got, weights, taps, places = lax.optimization_barrier((got, weights, taps, places))
    obs = observe(got, places)
    obs, corners = lax.optimization_barrier((obs, parts[4:]))
    covered, *beside = cover(taps, obs, weights[1], leave)
    parts = parts[:4] + list(corners)
    own, *sent = sweep(taps, obs, weights, enter, leave, cur, parts, beside)
    cur, below, *sent = update(pick, add, cur, covered, own, reduce_parts(sent))
    parts = gather_parts(sent)
    own, *sent = sweep(taps, obs, weights, enter, leave, cur, parts)
    total = [own] + reduce_parts(sent)
    out = last_update(add, cur, below, total)
    out = lax.all_to_all(out, ALL, split_axis=0, concat_axis=0, tiled=True)
    return place_output(out)


def solution(mesh):
    placed = (
        P("block", None, None),
        P("view", "block", None, None, None),
        P("view", "block", None),
        P("view", "block"),
        P("view", "block"),
        P(None, "view"),
    )
    return jax.shard_map(
        on_device, mesh=mesh, in_specs=placed, out_specs=P("block", None, None), check_vma=False
    )
```

```python
import jax
import jax.numpy as jnp
import numpy as np
from jax import lax
from jax.experimental import pallas as pl
from jax.experimental.pallas import tpu as pltpu
from jax.sharding import PartitionSpec as P

RAD = 3
ITERS = 2
ALL = ("block", "view")
PR, PC = 16, 8
SR, SC = 8, 16
LAT = SR * SC
HALO_PAD = 256
EXT = LAT + HALO_PAD
F32, BF16 = jnp.float32, jnp.bfloat16

DIRS = [(0, -1), (0, 1), (-1, 0), (1, 0), (-1, -1), (-1, 1), (1, -1), (1, 1)]


def part_range(step, size):
    if step < 0:
        return list(range(-RAD, 0))
    if step > 0:
        return list(range(size, size + RAD))
    return list(range(size))


PARTS = [[(dr, dc) for dr in part_range(er, SR) for dc in part_range(ec, SC)] for er, ec in DIRS]
SIZES = [len(part) for part in PARTS]
HALO_AT = [sum(SIZES[:n]) for n in range(8)]
EXT_POS = [(s, j) for s in range(SR) for j in range(SC)] + [pos for part in PARTS for pos in part]
EXT_POS = EXT_POS + [(1000, 1000)] * (EXT - len(EXT_POS))


def row_place(r):
    y, k = r // 3, r % 3
    turned = y % 2
    z = 1 + k + turned * (2 - 2 * k)
    home = r // 12
    return y + home * (15 - r - y), z - home * z


def column_place(c):
    core = c // 4
    return (c % 4 + core * (3 - 2 * (c % 4))) * 2 + core


def device_of(r, c):
    y, z = row_place(r % PR)
    return (y * 8 + column_place(c % PC)) * 4 + z


def towards(er, ec):
    return [(device_of(r, c), device_of(r + er, c + ec)) for r in range(PR) for c in range(PC)]


def lane_table():
    main = [[-1] * 128 for _ in range(4)]
    aux = [[[-1] * 128 for _ in range(6)] for _ in range(2)]
    for n in range(8):
        for lane in range(4 * SIZES[n]):
            if n < 4 and lane < 128:
                main[n][lane] = (n, lane)
            else:
                for p in range(2):
                    if n < 4:
                        aux[p][n - 2][p * 64 + lane - 128] = (n, lane)
                    else:
                        aux[p][n - 2][p * 36 + lane] = (n, lane)
    return [x for row in main for x in row] + [x for kind in aux for row in kind for x in row]


LANES = lane_table()
LANE_N = np.array([0 if x == -1 else x[0] for x in LANES])
LANE_Q = np.array([-100 if x == -1 else x[1] // SIZES[x[0]] for x in LANES])
LANE_HALO = np.array([0 if x == -1 else HALO_AT[x[0]] + x[1] % SIZES[x[0]] for x in LANES])
LANE_OWN = np.array(
    [
        -1
        if x == -1
        else (x[1] // SIZES[x[0]]) * LAT
        + (PARTS[x[0]][x[1] % SIZES[x[0]]][0] % SR) * SC
        + PARTS[x[0]][x[1] % SIZES[x[0]]][1] % SC
        for x in LANES
    ]
)
ER = np.array([d[0] for d in DIRS])[LANE_N]
EC = np.array([d[1] for d in DIRS])[LANE_N]
N_MAIN, N_AUX = 512, 768


def params(mib):
    return pltpu.CompilerParams(vmem_limit_bytes=mib << 20)


def turn(rows):
    chunk = lax.broadcasted_iota(jnp.int32, rows[0].shape, 1) // SC
    for k in (4, 2, 1):
        low = (chunk & k) == 0
        after = list(rows)
        for a in range(8):
            if a & k == 0:
                x, y = rows[a], rows[a | k]
                after[a] = jnp.where(low, x, pltpu.roll(y, SC * k, 1))
                after[a | k] = jnp.where(low, pltpu.roll(x, 128 - SC * k, 1), y)
        rows = after
    return rows


def split(x):
    high = x.astype(BF16)
    return high, (x - high.astype(F32)).astype(BF16)


def dot(a, b):
    return jnp.dot(a, b, preferred_element_type=F32)


def send_small_kernel(view_ref, left_ref, right_ref, meta_ref, out_ref):
    left, right = left_ref.reshape(128, 128), right_ref.reshape(128, 128)
    for k in range(4):
        y, z = row_place(pl.program_id(0) * 4 + k)
        rows = []
        for s in range(8):
            at = pl.ds(k * 8 + s, 4, stride=32)
            rows.append(jnp.concatenate([left[at, :], right[at, :]], axis=0))
        rows = turn(rows)
        for c in range(8):
            out_ref[y, column_place(c), z, 0:8, :] = rows[c]
            out_ref[y, column_place(c), z, 8:16, :] = meta_ref[...]


def small_message(view, estimate, meta):
    estimate = estimate.reshape(8, 2, 4, 32, 256)
    out = pl.pallas_call(
        send_small_kernel,
        grid_spec=pltpu.PrefetchScalarGridSpec(
            num_scalar_prefetch=1,
            grid=(4,),
            in_specs=[
                pl.BlockSpec((2, 2, 1, 32, 128), lambda y, v: (v[0], 0, y, 0, 0)),
                pl.BlockSpec((2, 2, 1, 32, 128), lambda y, v: (v[0], 0, y, 0, 1)),
                pl.BlockSpec((8, 128), lambda y, v: (0, 0)),
            ],
            out_specs=pl.BlockSpec((4, 8, 4, 16, 128), lambda y, v: (0, 0, 0, 0, 0)),
        ),
        out_shape=jax.ShapeDtypeStruct((4, 8, 4, 16, 128), F32),
        compiler_params=params(56),
        name="small_message",
    )(view, estimate, estimate, meta)
    return out.reshape(128, 16, 128)


def send_tiles_kernel(view_ref, tiles_ref, out_ref):
    tiles = tiles_ref.reshape(2048, 128)
    for k in range(4):
        y, z = row_place(pl.program_id(0) * 4 + k)
        for p in range(2):
            rows = turn([tiles[pl.ds(p * 32 + k * 8 + s, 32, stride=64), :] for s in range(8)])
            for c in range(8):
                out_ref[y, column_place(c), z, p * 32 : p * 32 + 32, :] = rows[c]


def tile_message(view, tiles):
    out = pl.pallas_call(
        send_tiles_kernel,
        grid_spec=pltpu.PrefetchScalarGridSpec(
            num_scalar_prefetch=1,
            grid=(4,),
            in_specs=[pl.BlockSpec((32, 2, 32, 128), lambda y, v: (0, 0, y, 0))],
            out_specs=pl.BlockSpec((4, 8, 4, 64, 128), lambda y, v: (0, 0, 0, 0, 0)),
        ),
        out_shape=jax.ShapeDtypeStruct((4, 8, 4, 64, 128), F32),
        compiler_params=params(56),
        cost_estimate=pl.CostEstimate(flops=1 << 20, bytes_accessed=24 << 20, transcendentals=0),
        name="tile_message",
    )(view, tiles)
    return out.reshape(128, 64, 128)


def stacked(x):
    return jnp.concatenate(split(x), axis=0)


def dot_halves(x, table):
    out = dot(x, table)
    rows = out.shape[0] // 2
    return out[:rows] + out[rows:]


def aux_at(p):
    return slice(N_MAIN + p * N_AUX, N_MAIN + (p + 1) * N_AUX)


def to_messages(x, table_ref, outs):
    main = dot_halves(stacked(x), table_ref[:, :N_MAIN])
    aux = dot_halves(stacked(x[:128]), table_ref[:, aux_at(0)]) + dot_halves(stacked(x[128:]), table_ref[:, aux_at(1)])
    put_messages(main, aux, outs)


def from_messages(parts, table_ref):
    main = jnp.concatenate([parts[n][0:256, :] for n in range(4)], axis=1)
    aux = jnp.concatenate([parts[n][256:384, :] for n in (2, 3)] + [parts[n][0:128, :] for n in range(4, 8)], axis=1)
    main = dot_halves(stacked(main), table_ref[:N_MAIN, :])
    aux = stacked(aux)
    return [main[p * 128 : p * 128 + 128] + dot_halves(aux, table_ref[aux_at(p), :]) for p in range(2)]


def put_messages(main, aux, outs):
    for n in range(4):
        outs[n][0:256, :] = main[:, n * 128 : n * 128 + 128]
        if n >= 2:
            outs[n][256:384, :] = aux[:, (n - 2) * 128 : (n - 2) * 128 + 128]
    for n in range(4, 8):
        outs[n][0:128, :] = aux[:, (n - 2) * 128 : (n - 2) * 128 + 128]


MESSAGES = [jax.ShapeDtypeStruct((rows, 128), F32) for rows in (256, 256, 384, 384, 128, 128, 128, 128)]


def add_messages(parts, table_ref, base):
    out = []
    for p, term in enumerate(from_messages(parts, table_ref)):
        out.append(term + jnp.concatenate([base[q, p * 128 : p * 128 + 128, :] for q in range(4)], axis=1))
    return out


def quads(x):
    return jnp.concatenate([x[q] for q in range(4)], axis=1)


def begin_kernel(got_ref, pick_ref, cur_ref, *outs):
    got = got_ref.reshape(128 * 16, 128)
    for q in range(4):
        for p in range(2):
            row = (q % 2) * 4 + p * 2 + q // 2
            for m in range(16):
                at = p * 128 + m * 8
                cur_ref[q, at : at + 8, :] = got[pl.ds(m * 16 + row, 8, stride=256), :]
    to_messages(quads(cur_ref), pick_ref, outs)


def begin(got, pick):
    return pl.pallas_call(
        begin_kernel,
        grid=(1,),
        in_specs=[
            pl.BlockSpec((128, 16, 128), lambda i: (0, 0, 0)),
            pl.BlockSpec((512, N_MAIN + 2 * N_AUX), lambda i: (0, 0)),
        ],
        out_specs=[pl.BlockSpec((4, 256, 128), lambda i: (0, 0, 0))]
        + [pl.BlockSpec(m.shape, lambda i: (0, 0)) for m in MESSAGES],
        out_shape=[jax.ShapeDtypeStruct((4, 256, 128), F32)] + MESSAGES,
        compiler_params=params(16),
        name="begin",
    )(got, pick)


def weight_kernel(taps_ref, er_ref, ec_ref, ert_ref, ect_ref, fore_ref, back_ref):
    def from_taps(apart, axis, w):
        far = jnp.abs(apart)
        out = jnp.zeros(apart.shape, F32)
        for k in range(RAD + 1):
            out = jnp.where(far == k, taps_ref[axis, w, k], out)
        return out

    lanes = lax.broadcasted_iota(jnp.int32, (EXT, LAT), 1)
    down, across = er_ref[...] - lanes // SC, ec_ref[...] - lanes % SC
    rows = lax.broadcasted_iota(jnp.int32, (LAT, EXT), 0)
    down_t, across_t = ert_ref[...] - rows // SC, ect_ref[...] - rows % SC
    for w in range(8):
        pair, at = w // 2, slice((w % 2) * LAT, (w % 2) * LAT + LAT)
        high, low = split(from_taps(down, 1, w) * from_taps(across, 2, w))
        for i, x in enumerate((high, high, low)):
            fore_ref[pair, i * EXT : i * EXT + EXT, at] = x
        high, low = split(from_taps(down_t, 1, w) * from_taps(across_t, 2, w))
        for i, x in enumerate((high, high, low)):
            start = i * 2 * LAT + (w % 2) * LAT
            back_ref[pair, start : start + LAT, :] = x


def make_weights(taps):
    ext = np.array(EXT_POS, np.int32)
    tall = [np.broadcast_to(ext[:, i][:, None], (EXT, LAT)) for i in range(2)]
    wide = [np.broadcast_to(ext[:, i][None, :], (LAT, EXT)) for i in range(2)]
    whole = pl.BlockSpec(memory_space=pltpu.VMEM)
    return pl.pallas_call(
        weight_kernel,
        in_specs=[pl.BlockSpec(memory_space=pltpu.SMEM)] + [whole] * 4,
        out_specs=[whole] * 2,
        out_shape=[
            jax.ShapeDtypeStruct((4, 3 * EXT, 2 * LAT), BF16),
            jax.ShapeDtypeStruct((4, 6 * LAT, EXT), BF16),
        ],
        compiler_params=params(20),
        name="make_weights",
    )(taps, *tall, *wide)


def observe_kernel(got_ref, meta_ref, obs_ref):
    sides = []
    for p in range(2):
        sides.append(got_ref[:, 0, p * 32 : p * 32 + 32, :].reshape(1024, 128))
    high, low = split(jnp.concatenate(sides, axis=1))
    lanes = []
    for i in range(0, 32, 4):
        lanes.append(sum(meta_ref[i + k, 0, 0:1, :] for k in range(1, 4)) + meta_ref[i, 0, 0:1, :])
    place = jnp.concatenate(lanes, axis=1)
    for half in range(4):
        rows = lax.broadcasted_iota(jnp.int32, (256, 1024), 0) + half * 256
        hot = (rows.astype(F32) == place).astype(F32)
        counts = jnp.sum(hot, axis=1, keepdims=True)
        hot = hot.astype(BF16)
        mean = (dot(hot, high) + dot(hot, low)) / jnp.maximum(counts, 1.0)
        for i in range(2):
            for p in range(2):
                obs_ref[half // 2, (half % 2) * 2 + i, p * 128 : p * 128 + 128, :] = mean[
                    i * 128 : i * 128 + 128, p * 128 : p * 128 + 128
                ]


def observe(got, small):
    got = got.reshape(32, 4, 64, 128)
    small = small.reshape(32, 4, 16, 128)
    return pl.pallas_call(
        observe_kernel,
        grid=(4,),
        in_specs=[
            pl.BlockSpec((32, 1, 64, 128), lambda g: (0, g, 0, 0)),
            pl.BlockSpec((32, 1, 8, 128), lambda g: (0, g, 1, 0)),
        ],
        out_specs=pl.BlockSpec((2, 4, 256, 128), lambda g: (g, 0, 0, 0)),
        out_shape=jax.ShapeDtypeStruct((8, 4, 256, 128), F32),
        compiler_params=params(20),
        cost_estimate=pl.CostEstimate(flops=4 << 30, bytes_accessed=8 << 20, transcendentals=0),
        name="observe",
    )(got, small)


def depth_blur(x, taps):
    rows = [None] * 32
    for p in range(2):
        for m in range(16):
            rows[2 * m + p] = x[p * 128 + m * 8 : p * 128 + m * 8 + 8]
    layer = lax.broadcasted_iota(jnp.int32, rows[0].shape, 0)
    before = [jnp.where(layer == 0, 0.0, pltpu.roll(rows[32 - k], 1, 0)) for k in (3, 2, 1)]
    after = [jnp.where(layer == 7, 0.0, pltpu.roll(rows[k], 7, 0)) for k in (0, 1, 2)]
    e = before + rows + after
    out = [
        taps[0] * e[z + 3]
        + taps[1] * (e[z + 2] + e[z + 4])
        + (taps[2] * (e[z + 1] + e[z + 5]) + taps[3] * (e[z] + e[z + 6]))
        for z in range(32)
    ]
    return jnp.concatenate([out[2 * m + p] for p in range(2) for m in range(16)], axis=0)


def back_project(blurred, back_ref, total):
    def step(pair):
        rows = []
        for x in blurred(pair):
            halves = [split(side) for side in x]
            high = [h for h, _ in halves]
            low = [l for _, l in halves]
            rows.append(jnp.concatenate(high + low + high, axis=1))
        return jnp.concatenate(rows, axis=0)

    sides = [step(pair) for pair in range(4)]
    total[...] = dot(jnp.concatenate(sides, axis=1), back_ref[...].reshape(4 * 6 * LAT, EXT))


def finish_back(total, out_ref, own_ref, outs):
    for q in range(4):
        own_ref[q] = total[q * 256 : q * 256 + 256, :LAT]
    halo = jnp.concatenate([total[q * 256 : q * 256 + 256, LAT:] for q in range(4)], axis=1)
    to_messages(halo, out_ref, outs)


def cover_kernel(taps_ref, obs_ref, back_ref, out_ref, own_ref, *rest):
    outs, total = rest[:8], rest[8]

    def blurred(pair):
        for q in range(4):
            sides = []
            for i in range(2):
                taps = [taps_ref[0, 2 * pair + i, k] for k in range(RAD + 1)]
                sides.append(depth_blur((obs_ref[2 * pair + i, q] > 0.0).astype(F32), taps))
            yield sides

    back_project(blurred, back_ref, total)
    finish_back(total, out_ref, own_ref, outs)


def cover(taps, obs, back, leave):
    whole = pl.BlockSpec(memory_space=pltpu.VMEM)
    return pl.pallas_call(
        cover_kernel,
        in_specs=[pl.BlockSpec(memory_space=pltpu.SMEM)] + [whole] * 3,
        out_specs=[whole] * 9,
        out_shape=[jax.ShapeDtypeStruct((4, 256, LAT), F32)] + MESSAGES,
        scratch_shapes=[pltpu.VMEM((1024, EXT), F32)],
        compiler_params=params(20),
        cost_estimate=pl.CostEstimate(flops=6 << 30, bytes_accessed=8 << 20, transcendentals=0),
        name="cover",
    )(taps, obs, back, leave)


def sweep_kernel(taps_ref, obs_ref, fore_ref, back_ref, enter_ref, leave_ref, cur_ref, *refs):
    parts, beside, own_ref, outs = refs[:8], refs[8:-11], refs[-11], refs[-10:-2]
    total, ext = refs[-2:]
    for message, out in zip(beside, outs, strict=False):
        rows = message.shape[0]
        out[rows : 2 * rows, :] = message[...]

    def put(rows, at, x):
        high, low = split(x)
        for i, half in enumerate((high, low, high)):
            ext[rows, i * EXT + at : i * EXT + at + x.shape[1]] = half

    for q in range(4):
        put(slice(q * 256, q * 256 + 256), 0, cur_ref[q])
    for p, halo in enumerate(from_messages(parts, enter_ref)):
        for q in range(4):
            start = q * 256 + p * 128
            put(slice(start, start + 128), LAT, halo[:, q * HALO_PAD : (q + 1) * HALO_PAD])

    def blurred(pair):
        across = dot(ext[...], fore_ref[pair])
        for q in range(4):
            sides = []
            for i in range(2):
                w = 2 * pair + i
                taps = [taps_ref[0, w, k] for k in range(RAD + 1)]
                blur = depth_blur(across[q * 256 : q * 256 + 256, i * LAT : i * LAT + LAT], taps)
                near = pl.reciprocal(blur, approx=True)
                near = near * (2.0 - blur * near)
                sides.append(depth_blur(obs_ref[w, q] * near, taps))
            yield sides

    back_project(blurred, back_ref, total)
    finish_back(total, leave_ref, own_ref, outs)


def sweep(taps, obs, weights, enter, leave, cur, parts, beside=()):
    messages = [jax.ShapeDtypeStruct((m.shape[0] * (2 if beside else 1), 128), F32) for m in MESSAGES]
    whole = pl.BlockSpec(memory_space=pltpu.VMEM)
    return pl.pallas_call(
        sweep_kernel,
        in_specs=[pl.BlockSpec(memory_space=pltpu.SMEM)] + [whole] * (14 + len(beside)),
        out_specs=[whole] * 9,
        out_shape=[jax.ShapeDtypeStruct((4, 256, LAT), F32)] + messages,
        scratch_shapes=[pltpu.VMEM((1024, EXT), F32), pltpu.VMEM((1024, 3 * EXT), BF16)],
        compiler_params=params(26),
        cost_estimate=pl.CostEstimate(flops=12 << 30, bytes_accessed=12 << 20, transcendentals=0),
        name="sweep",
    )(taps, obs, *weights, enter, leave, cur, *parts, *beside)


def update_kernel(pick_ref, add_ref, cur_ref, cover_ref, total_ref, *refs):
    parts, cur_out, below_out, outs = refs[:8], refs[8], refs[9], refs[10:18]
    behind = [part.at[pl.ds(m.shape[0], m.shape[0])] for part, m in zip(parts, MESSAGES, strict=True)]
    total = add_messages(parts, add_ref, total_ref)
    cover = add_messages(behind, add_ref, cover_ref)
    for p in range(2):
        rows = slice(p * 128, p * 128 + 128)
        for q in range(4):
            lanes = slice(q * LAT, q * LAT + LAT)
            below = 1.0 + cover[p][:, lanes]
            below_out[q, rows, :] = below
            cur_out[q, rows, :] = cur_ref[q, rows, :] * (1.0 + total[p][:, lanes]) / below
    to_messages(quads(cur_out), pick_ref, outs)


def update(pick, add, cur, cover, total, parts):
    whole = pl.BlockSpec(memory_space=pltpu.VMEM)
    return pl.pallas_call(
        update_kernel,
        in_specs=[whole] * 13,
        out_specs=[whole] * 10,
        out_shape=[jax.ShapeDtypeStruct((4, 256, LAT), F32)] * 2 + MESSAGES,
        compiler_params=params(16),
        name="update",
    )(pick, add, cur, cover, total, *parts)


def last_kernel(add_ref, cur_ref, below_ref, total_ref, *refs):
    totals, out_ref, rows_ref = refs[:8], refs[8], refs[9]
    total = add_messages(totals, add_ref, total_ref)
    for p in range(2):
        rows = slice(p * 128, p * 128 + 128)
        for q in range(4):
            mine = total[p][:, q * LAT : q * LAT + LAT]
            done = cur_ref[q, rows, :] * (1.0 + mine) / below_ref[q, rows, :]
            for m in range(16):
                rows_ref[pl.ds(m * 8 + p * 4 + q, 8, stride=128), :] = done[m * 8 : m * 8 + 8]
    done = rows_ref[...].reshape(32, 32, 128)
    for v in range(4):
        out_ref[:, v] = done


def last_update(add, cur, below, total):
    whole = pl.BlockSpec(memory_space=pltpu.VMEM)
    out = pl.pallas_call(
        last_kernel,
        in_specs=[whole] * 12,
        out_specs=whole,
        out_shape=jax.ShapeDtypeStruct((32, 4, 32, 128), F32),
        scratch_shapes=[pltpu.VMEM((1024, 128), F32)],
        compiler_params=params(14),
        name="last_update",
    )(add, cur, below, *total)
    return out.reshape(128, 32, 128)


def place_kernel(got_ref, out_ref, side_ref):
    got = got_ref.reshape(4096, 128)
    for k in range(4):
        y, z = row_place(pl.program_id(0) * 4 + k)
        for tx in range(2):
            rows = turn([got[pl.ds(y * 1024 + column_place(c) * 128 + z * 32 + tx, 16, stride=2), :] for c in range(8)])
            side = side_ref.at[k * 2 + tx]
            for s in range(8):
                side[pl.ds(s, 16, stride=8), :] = rows[s]
            lanes = slice(tx * 128, tx * 128 + 128)
            out_ref[:, :, 0, k * 8 : k * 8 + 8, lanes] = side[...].reshape(8, 2, 8, 128)


def place_output(got):
    out = pl.pallas_call(
        place_kernel,
        grid=(4,),
        in_specs=[pl.BlockSpec((4, 8, 4, 32, 128), lambda y: (0, 0, 0, 0, 0))],
        out_specs=pl.BlockSpec((8, 2, 1, 32, 256), lambda y: (0, 0, y, 0, 0)),
        out_shape=jax.ShapeDtypeStruct((8, 2, 4, 32, 256), F32),
        scratch_shapes=[pltpu.VMEM((8, 128, 128), F32)],
        compiler_params=params(20),
        name="place_output",
    )(got.reshape(4, 8, 4, 32, 128))
    return out.reshape(8, 256, 256)


def gather_parts(parts):
    return [lax.ppermute(x, ALL, towards(-er, -ec)) for x, (er, ec) in zip(parts, DIRS, strict=True)]


def reduce_parts(parts):
    return [lax.ppermute(x, ALL, towards(er, ec)) for x, (er, ec) in zip(parts, DIRS, strict=True)]


def on_device(estimate, tiles, tile_block, tile_view, tile_slot, widths):
    block, view = lax.axis_index("block"), lax.axis_index("view")
    y, x, core = block // 8, block // 2 % 4, block % 2
    outward = jnp.where(y % 2 == 0, y * 3 + view - 1, y * 3 + 3 - view)
    r = jnp.where(view == 0, 15 - y, outward)
    c = jnp.where(core == 0, x, 7 - x)
    slot = tile_slot[0]
    deep = tile_block[0, :, 0] * 4 + slot // 4
    place = tile_view[0] * 512 + (slot % 4) * 128 + (deep % 16) * 8 + deep // 16
    place = jnp.where(jnp.arange(128) // 32 == block % 4, jnp.tile(place.astype(F32), 4), 0.0)
    own_widths = jnp.pad(widths.reshape(1, 6), ((1, 6), (0, 122)))
    meta = jnp.where(jnp.arange(8)[:, None] == 0, place[None, :], own_widths)
    send = small_message(view.reshape(1), estimate, meta)
    order, send = lax.optimization_barrier((view.reshape(1), send))
    small = lax.all_to_all(send, ALL, split_axis=0, concat_axis=0, tiled=True)
    send = tile_message(order, tiles[0])
    send, small = lax.optimization_barrier((send, small))
    got = lax.all_to_all(send, ALL, split_axis=0, concat_axis=0, tiled=True)

    add = (LANE_OWN[:, None] == np.arange(4 * LAT)[None, :]).astype(BF16)
    pick = (np.arange(4 * LAT)[:, None] == LANE_OWN[None, :]).astype(BF16)
    wrap_r = ((r + ER < 0) | (r + ER >= PR)).astype(jnp.int32) * ER
    wrap_c = ((c + EC < 0) | (c + EC >= PC)).astype(jnp.int32) * EC
    ty, tx = LANE_Q // 2 - wrap_r, LANE_Q % 2 - wrap_c
    inside = (LANE_Q >= 0) & (ty >= 0) & (ty < 2) & (tx >= 0) & (tx < 2)
    target = jnp.where(inside, (ty * 2 + tx) * HALO_PAD + LANE_HALO, -1)
    enter = (target[:, None] == jnp.arange(4 * HALO_PAD)[None, :]).astype(BF16)
    leave = (jnp.arange(4 * HALO_PAD)[:, None] == target[None, :]).astype(BF16)

    cur, *sent = begin(small, pick)
    parts = gather_parts(sent)
    spread = small[0:4, 9, 0:6].reshape(4, 3, 2).transpose(1, 0, 2).reshape(3, 8, 1)
    steps = jnp.arange(RAD + 1).astype(F32)
    raw = jnp.exp(-steps * steps / (2.0 * spread * spread))
    taps = raw / (2.0 * jnp.sum(raw, axis=2, keepdims=True) - raw[:, :, 0:1])
    weights = make_weights(taps)
    got, weights, taps = lax.optimization_barrier((got, weights, taps))
    obs = observe(got, small)
    obs, corners = lax.optimization_barrier((obs, parts[4:]))
    covered, *beside = cover(taps, obs, weights[1], leave)
    parts = parts[:4] + list(corners)
    own, *sent = sweep(taps, obs, weights, enter, leave, cur, parts, beside)
    cur, below, *sent = update(pick, add, cur, covered, own, reduce_parts(sent))
    parts = gather_parts(sent)
    own, *sent = sweep(taps, obs, weights, enter, leave, cur, parts)
    total = [own] + reduce_parts(sent)
    out = last_update(add, cur, below, total)
    out = lax.all_to_all(out, ALL, split_axis=0, concat_axis=0, tiled=True)
    return place_output(out)


def solution(mesh):
    placed = (
        P("block", None, None),
        P("view", "block", None, None, None),
        P("view", "block", None),
        P("view", "block"),
        P("view", "block"),
        P(None, "view"),
    )
    return jax.shard_map(
        on_device, mesh=mesh, in_specs=placed, out_specs=P("block", None, None), check_vma=False
    )
```

```python
import jax
import jax.numpy as jnp
import numpy as np
from jax import lax
from jax.experimental import pallas as pl
from jax.experimental.pallas import tpu as pltpu
from jax.sharding import PartitionSpec as P

RAD = 3
ITERS = 2
ALL = ("block", "view")
PR, PC = 16, 8
SR, SC = 8, 16
LAT = SR * SC
HALO_PAD = 256
EXT = LAT + HALO_PAD
F32, BF16 = jnp.float32, jnp.bfloat16

DIRS = [(0, -1), (0, 1), (-1, 0), (1, 0), (-1, -1), (-1, 1), (1, -1), (1, 1)]


def part_range(step, size):
    if step < 0:
        return list(range(-RAD, 0))
    if step > 0:
        return list(range(size, size + RAD))
    return list(range(size))


PARTS = [[(dr, dc) for dr in part_range(er, SR) for dc in part_range(ec, SC)] for er, ec in DIRS]
SIZES = [len(part) for part in PARTS]
HALO_AT = [sum(SIZES[:n]) for n in range(8)]
EXT_POS = [(s, j) for s in range(SR) for j in range(SC)] + [pos for part in PARTS for pos in part]
EXT_POS = EXT_POS + [(1000, 1000)] * (EXT - len(EXT_POS))


def row_place(r):
    y, k = r // 3, r % 3
    turned = y % 2
    z = 1 + k + turned * (2 - 2 * k)
    home = r // 12
    return y + home * (15 - r - y), z - home * z


def column_place(c):
    core = c // 4
    return (c % 4 + core * (3 - 2 * (c % 4))) * 2 + core


def device_of(r, c):
    y, z = row_place(r % PR)
    return (y * 8 + column_place(c % PC)) * 4 + z


def towards(er, ec):
    return [(device_of(r, c), device_of(r + er, c + ec)) for r in range(PR) for c in range(PC)]


def lane_table():
    main = [[-1] * 128 for _ in range(4)]
    aux = [[[-1] * 128 for _ in range(6)] for _ in range(2)]
    for n in range(8):
        for lane in range(4 * SIZES[n]):
            if n < 4 and lane < 128:
                main[n][lane] = (n, lane)
            else:
                for p in range(2):
                    if n < 4:
                        aux[p][n - 2][p * 64 + lane - 128] = (n, lane)
                    else:
                        aux[p][n - 2][p * 36 + lane] = (n, lane)
    return [x for row in main for x in row] + [x for kind in aux for row in kind for x in row]


LANES = lane_table()
LANE_N = np.array([0 if x == -1 else x[0] for x in LANES])
LANE_Q = np.array([-100 if x == -1 else x[1] // SIZES[x[0]] for x in LANES])
LANE_HALO = np.array([0 if x == -1 else HALO_AT[x[0]] + x[1] % SIZES[x[0]] for x in LANES])
LANE_OWN = np.array(
    [
        -1
        if x == -1
        else (x[1] // SIZES[x[0]]) * LAT
        + (PARTS[x[0]][x[1] % SIZES[x[0]]][0] % SR) * SC
        + PARTS[x[0]][x[1] % SIZES[x[0]]][1] % SC
        for x in LANES
    ]
)
ER = np.array([d[0] for d in DIRS])[LANE_N]
EC = np.array([d[1] for d in DIRS])[LANE_N]
N_MAIN, N_AUX = 512, 768


def params(mib):
    return pltpu.CompilerParams(vmem_limit_bytes=mib << 20)


def turn(rows):
    chunk = lax.broadcasted_iota(jnp.int32, rows[0].shape, 1) // SC
    for k in (4, 2, 1):
        low = (chunk & k) == 0
        after = list(rows)
        for a in range(8):
            if a & k == 0:
                x, y = rows[a], rows[a | k]
                after[a] = jnp.where(low, x, pltpu.roll(y, SC * k, 1))
                after[a | k] = jnp.where(low, pltpu.roll(x, 128 - SC * k, 1), y)
        rows = after
    return rows


def split(x):
    high = x.astype(BF16)
    return high, (x - high.astype(F32)).astype(BF16)


def dot(a, b):
    return jnp.dot(a, b, preferred_element_type=F32)


def send_small_kernel(at_ref, left_ref, right_ref, block_ref, tile_view_ref, slot_ref, widths_ref, out_ref, meta_ref):
    slot = slot_ref[...]
    deep = block_ref[...] * 4 + slot // 4
    place = (tile_view_ref[...] * 512 + (slot % 4) * 128 + (deep % 16) * 8 + deep // 16).astype(F32)
    meta_ref[...] = jnp.zeros_like(meta_ref)
    for k in range(4):
        meta_ref[0:1, k * 32 : k * 32 + 32] = jnp.where(at_ref[1] == k, place, 0.0)
    meta_ref[1:4, 0:2] = widths_ref[...]
    left, right = left_ref.reshape(128, 128), right_ref.reshape(128, 128)
    for k in range(4):
        y, z = row_place(pl.program_id(0) * 4 + k)
        rows = []
        for s in range(8):
            at = pl.ds(k * 8 + s, 4, stride=32)
            rows.append(jnp.concatenate([left[at, :], right[at, :]], axis=0))
        rows = turn(rows)
        for c in range(8):
            out_ref[y, column_place(c), z, 0:8, :] = rows[c]
            out_ref[y, column_place(c), z, 8:16, :] = meta_ref[...]


def small_message(at, estimate, tile_block, tile_view, tile_slot, widths):
    estimate = estimate.reshape(8, 2, 4, 32, 256)
    out = pl.pallas_call(
        send_small_kernel,
        grid_spec=pltpu.PrefetchScalarGridSpec(
            num_scalar_prefetch=1,
            grid=(4,),
            in_specs=[
                pl.BlockSpec((2, 2, 1, 32, 128), lambda y, v: (v[0], 0, y, 0, 0)),
                pl.BlockSpec((2, 2, 1, 32, 128), lambda y, v: (v[0], 0, y, 0, 1)),
                pl.BlockSpec((1, 32), lambda y, v: (0, 0)),
                pl.BlockSpec((1, 32), lambda y, v: (0, 0)),
                pl.BlockSpec((1, 32), lambda y, v: (0, 0)),
                pl.BlockSpec((3, 2), lambda y, v: (0, 0)),
            ],
            out_specs=pl.BlockSpec((4, 8, 4, 16, 128), lambda y, v: (0, 0, 0, 0, 0)),
            scratch_shapes=[pltpu.VMEM((8, 128), F32)],
        ),
        out_shape=jax.ShapeDtypeStruct((4, 8, 4, 16, 128), F32),
        compiler_params=params(56),
        name="small_message",
    )(at, estimate, estimate, tile_block.reshape(1, 32), tile_view, tile_slot, widths)
    return out.reshape(128, 16, 128)


def send_tiles_kernel(view_ref, tiles_ref, out_ref):
    tiles = tiles_ref.reshape(2048, 128)
    for k in range(4):
        y, z = row_place(pl.program_id(0) * 4 + k)
        for p in range(2):
            rows = turn([tiles[pl.ds(p * 32 + k * 8 + s, 32, stride=64), :] for s in range(8)])
            for c in range(8):
                out_ref[y, column_place(c), z, p * 32 : p * 32 + 32, :] = rows[c]


def tile_message(view, tiles):
    out = pl.pallas_call(
        send_tiles_kernel,
        grid_spec=pltpu.PrefetchScalarGridSpec(
            num_scalar_prefetch=1,
            grid=(4,),
            in_specs=[pl.BlockSpec((32, 2, 32, 128), lambda y, v: (0, 0, y, 0))],
            out_specs=pl.BlockSpec((4, 8, 4, 64, 128), lambda y, v: (0, 0, 0, 0, 0)),
        ),
        out_shape=jax.ShapeDtypeStruct((4, 8, 4, 64, 128), F32),
        compiler_params=params(56),
        cost_estimate=pl.CostEstimate(flops=1 << 20, bytes_accessed=24 << 20, transcendentals=0),
        name="tile_message",
    )(view, tiles)
    return out.reshape(128, 64, 128)


def stacked(x):
    return jnp.concatenate(split(x), axis=0)


def dot_halves(x, table):
    out = dot(x, table)
    rows = out.shape[0] // 2
    return out[:rows] + out[rows:]


def aux_at(p):
    return slice(N_MAIN + p * N_AUX, N_MAIN + (p + 1) * N_AUX)


def to_messages(x, table_ref, outs):
    main = dot_halves(stacked(x), table_ref[:, :N_MAIN])
    aux = dot_halves(stacked(x[:128]), table_ref[:, aux_at(0)]) + dot_halves(stacked(x[128:]), table_ref[:, aux_at(1)])
    put_messages(main, aux, outs)


def from_messages(parts, table_ref):
    main = jnp.concatenate([parts[n][0:256, :] for n in range(4)], axis=1)
    aux = jnp.concatenate([parts[n][256:384, :] for n in (2, 3)] + [parts[n][0:128, :] for n in range(4, 8)], axis=1)
    main = dot_halves(stacked(main), table_ref[:N_MAIN, :])
    aux = stacked(aux)
    return [main[p * 128 : p * 128 + 128] + dot_halves(aux, table_ref[aux_at(p), :]) for p in range(2)]


def put_messages(main, aux, outs):
    for n in range(4):
        outs[n][0:256, :] = main[:, n * 128 : n * 128 + 128]
        if n >= 2:
            outs[n][256:384, :] = aux[:, (n - 2) * 128 : (n - 2) * 128 + 128]
    for n in range(4, 8):
        outs[n][0:128, :] = aux[:, (n - 2) * 128 : (n - 2) * 128 + 128]


MESSAGES = [jax.ShapeDtypeStruct((rows, 128), F32) for rows in (256, 256, 384, 384, 128, 128, 128, 128)]


def add_messages(parts, table_ref, base):
    out = []
    for p, term in enumerate(from_messages(parts, table_ref)):
        out.append(term + jnp.concatenate([base[q, p * 128 : p * 128 + 128, :] for q in range(4)], axis=1))
    return out


def quads(x):
    return jnp.concatenate([x[q] for q in range(4)], axis=1)


def begin_kernel(got_ref, pick_ref, cur_ref, *outs):
    got = got_ref.reshape(128 * 16, 128)
    for q in range(4):
        for p in range(2):
            row = (q % 2) * 4 + p * 2 + q // 2
            for m in range(16):
                at = p * 128 + m * 8
                cur_ref[q, at : at + 8, :] = got[pl.ds(m * 16 + row, 8, stride=256), :]
    to_messages(quads(cur_ref), pick_ref, outs)


def begin(got, pick):
    return pl.pallas_call(
        begin_kernel,
        grid=(1,),
        in_specs=[
            pl.BlockSpec((128, 16, 128), lambda i: (0, 0, 0)),
            pl.BlockSpec((512, N_MAIN + 2 * N_AUX), lambda i: (0, 0)),
        ],
        out_specs=[pl.BlockSpec((4, 256, 128), lambda i: (0, 0, 0))]
        + [pl.BlockSpec(m.shape, lambda i: (0, 0)) for m in MESSAGES],
        out_shape=[jax.ShapeDtypeStruct((4, 256, 128), F32)] + MESSAGES,
        compiler_params=params(16),
        name="begin",
    )(got, pick)


def weight_kernel(taps_ref, er_ref, ec_ref, ert_ref, ect_ref, fore_ref, back_ref):
    def from_taps(apart, axis, w):
        far = jnp.abs(apart)
        out = jnp.zeros(apart.shape, F32)
        for k in range(RAD + 1):
            out = jnp.where(far == k, taps_ref[axis, w, k], out)
        return out

    lanes = lax.broadcasted_iota(jnp.int32, (EXT, LAT), 1)
    down, across = er_ref[...] - lanes // SC, ec_ref[...] - lanes % SC
    rows = lax.broadcasted_iota(jnp.int32, (LAT, EXT), 0)
    down_t, across_t = ert_ref[...] - rows // SC, ect_ref[...] - rows % SC
    for w in range(8):
        pair, at = w // 2, slice((w % 2) * LAT, (w % 2) * LAT + LAT)
        high, low = split(from_taps(down, 1, w) * from_taps(across, 2, w))
        for i, x in enumerate((high, high, low)):
            fore_ref[pair, i * EXT : i * EXT + EXT, at] = x
        high, low = split(from_taps(down_t, 1, w) * from_taps(across_t, 2, w))
        for i, x in enumerate((high, high, low)):
            start = i * 2 * LAT + (w % 2) * LAT
            back_ref[pair, start : start + LAT, :] = x


def make_weights(taps):
    ext = np.array(EXT_POS, np.int32)
    tall = [np.broadcast_to(ext[:, i][:, None], (EXT, LAT)) for i in range(2)]
    wide = [np.broadcast_to(ext[:, i][None, :], (LAT, EXT)) for i in range(2)]
    whole = pl.BlockSpec(memory_space=pltpu.VMEM)
    return pl.pallas_call(
        weight_kernel,
        in_specs=[pl.BlockSpec(memory_space=pltpu.SMEM)] + [whole] * 4,
        out_specs=[whole] * 2,
        out_shape=[
            jax.ShapeDtypeStruct((4, 3 * EXT, 2 * LAT), BF16),
            jax.ShapeDtypeStruct((4, 6 * LAT, EXT), BF16),
        ],
        compiler_params=params(20),
        name="make_weights",
    )(taps, *tall, *wide)


def observe_kernel(got_ref, meta_ref, obs_ref):
    sides = []
    for p in range(2):
        sides.append(got_ref[:, 0, p * 32 : p * 32 + 32, :].reshape(1024, 128))
    high, low = split(jnp.concatenate(sides, axis=1))
    lanes = []
    for i in range(0, 32, 4):
        lanes.append(sum(meta_ref[i + k, 0, 0:1, :] for k in range(1, 4)) + meta_ref[i, 0, 0:1, :])
    place = jnp.concatenate(lanes, axis=1)
    for half in range(4):
        rows = lax.broadcasted_iota(jnp.int32, (256, 1024), 0) + half * 256
        hot = (rows.astype(F32) == place).astype(F32)
        counts = jnp.sum(hot, axis=1, keepdims=True)
        hot = hot.astype(BF16)
        mean = (dot(hot, high) + dot(hot, low)) / jnp.maximum(counts, 1.0)
        for i in range(2):
            for p in range(2):
                obs_ref[half // 2, (half % 2) * 2 + i, p * 128 : p * 128 + 128, :] = mean[
                    i * 128 : i * 128 + 128, p * 128 : p * 128 + 128
                ]


def observe(got, small):
    got = got.reshape(32, 4, 64, 128)
    small = small.reshape(32, 4, 16, 128)
    return pl.pallas_call(
        observe_kernel,
        grid=(4,),
        in_specs=[
            pl.BlockSpec((32, 1, 64, 128), lambda g: (0, g, 0, 0)),
            pl.BlockSpec((32, 1, 8, 128), lambda g: (0, g, 1, 0)),
        ],
        out_specs=pl.BlockSpec((2, 4, 256, 128), lambda g: (g, 0, 0, 0)),
        out_shape=jax.ShapeDtypeStruct((8, 4, 256, 128), F32),
        compiler_params=params(20),
        cost_estimate=pl.CostEstimate(flops=4 << 30, bytes_accessed=8 << 20, transcendentals=0),
        name="observe",
    )(got, small)


def depth_blur(x, taps):
    rows = [None] * 32
    for p in range(2):
        for m in range(16):
            rows[2 * m + p] = x[p * 128 + m * 8 : p * 128 + m * 8 + 8]
    layer = lax.broadcasted_iota(jnp.int32, rows[0].shape, 0)
    before = [jnp.where(layer == 0, 0.0, pltpu.roll(rows[32 - k], 1, 0)) for k in (3, 2, 1)]
    after = [jnp.where(layer == 7, 0.0, pltpu.roll(rows[k], 7, 0)) for k in (0, 1, 2)]
    e = before + rows + after
    out = [
        taps[0] * e[z + 3]
        + taps[1] * (e[z + 2] + e[z + 4])
        + (taps[2] * (e[z + 1] + e[z + 5]) + taps[3] * (e[z] + e[z + 6]))
        for z in range(32)
    ]
    return jnp.concatenate([out[2 * m + p] for p in range(2) for m in range(16)], axis=0)


def back_project(blurred, back_ref, total):
    def step(pair):
        rows = []
        for x in blurred(pair):
            halves = [split(side) for side in x]
            high = [h for h, _ in halves]
            low = [l for _, l in halves]
            rows.append(jnp.concatenate(high + low + high, axis=1))
        return jnp.concatenate(rows, axis=0)

    sides = [step(pair) for pair in range(4)]
    total[...] = dot(jnp.concatenate(sides, axis=1), back_ref[...].reshape(4 * 6 * LAT, EXT))


def finish_back(total, out_ref, own_ref, outs):
    for q in range(4):
        own_ref[q] = total[q * 256 : q * 256 + 256, :LAT]
    halo = jnp.concatenate([total[q * 256 : q * 256 + 256, LAT:] for q in range(4)], axis=1)
    to_messages(halo, out_ref, outs)


def cover_kernel(taps_ref, obs_ref, back_ref, out_ref, own_ref, *rest):
    outs, total = rest[:8], rest[8]

    def blurred(pair):
        for q in range(4):
            sides = []
            for i in range(2):
                taps = [taps_ref[0, 2 * pair + i, k] for k in range(RAD + 1)]
                sides.append(depth_blur((obs_ref[2 * pair + i, q] > 0.0).astype(F32), taps))
            yield sides

    back_project(blurred, back_ref, total)
    finish_back(total, out_ref, own_ref, outs)


def cover(taps, obs, back, leave):
    whole = pl.BlockSpec(memory_space=pltpu.VMEM)
    return pl.pallas_call(
        cover_kernel,
        in_specs=[pl.BlockSpec(memory_space=pltpu.SMEM)] + [whole] * 3,
        out_specs=[whole] * 9,
        out_shape=[jax.ShapeDtypeStruct((4, 256, LAT), F32)] + MESSAGES,
        scratch_shapes=[pltpu.VMEM((1024, EXT), F32)],
        compiler_params=params(20),
        cost_estimate=pl.CostEstimate(flops=6 << 30, bytes_accessed=8 << 20, transcendentals=0),
        name="cover",
    )(taps, obs, back, leave)


def sweep_kernel(taps_ref, obs_ref, fore_ref, back_ref, enter_ref, leave_ref, cur_ref, *refs):
    parts, beside, own_ref, outs = refs[:8], refs[8:-11], refs[-11], refs[-10:-2]
    total, ext = refs[-2:]
    for message, out in zip(beside, outs, strict=False):
        rows = message.shape[0]
        out[rows : 2 * rows, :] = message[...]

    def put(rows, at, x):
        high, low = split(x)
        for i, half in enumerate((high, low, high)):
            ext[rows, i * EXT + at : i * EXT + at + x.shape[1]] = half

    for q in range(4):
        put(slice(q * 256, q * 256 + 256), 0, cur_ref[q])
    for p, halo in enumerate(from_messages(parts, enter_ref)):
        for q in range(4):
            start = q * 256 + p * 128
            put(slice(start, start + 128), LAT, halo[:, q * HALO_PAD : (q + 1) * HALO_PAD])

    def blurred(pair):
        across = dot(ext[...], fore_ref[pair])
        for q in range(4):
            sides = []
            for i in range(2):
                w = 2 * pair + i
                taps = [taps_ref[0, w, k] for k in range(RAD + 1)]
                blur = depth_blur(across[q * 256 : q * 256 + 256, i * LAT : i * LAT + LAT], taps)
                near = pl.reciprocal(blur, approx=True)
                near = near * (2.0 - blur * near)
                sides.append(depth_blur(obs_ref[w, q] * near, taps))
            yield sides

    back_project(blurred, back_ref, total)
    finish_back(total, leave_ref, own_ref, outs)


def sweep(taps, obs, weights, enter, leave, cur, parts, beside=()):
    messages = [jax.ShapeDtypeStruct((m.shape[0] * (2 if beside else 1), 128), F32) for m in MESSAGES]
    whole = pl.BlockSpec(memory_space=pltpu.VMEM)
    return pl.pallas_call(
        sweep_kernel,
        in_specs=[pl.BlockSpec(memory_space=pltpu.SMEM)] + [whole] * (14 + len(beside)),
        out_specs=[whole] * 9,
        out_shape=[jax.ShapeDtypeStruct((4, 256, LAT), F32)] + messages,
        scratch_shapes=[pltpu.VMEM((1024, EXT), F32), pltpu.VMEM((1024, 3 * EXT), BF16)],
        compiler_params=params(26),
        cost_estimate=pl.CostEstimate(flops=12 << 30, bytes_accessed=12 << 20, transcendentals=0),
        name="sweep",
    )(taps, obs, *weights, enter, leave, cur, *parts, *beside)


def update_kernel(pick_ref, add_ref, cur_ref, cover_ref, total_ref, *refs):
    parts, cur_out, below_out, outs = refs[:8], refs[8], refs[9], refs[10:18]
    behind = [part.at[pl.ds(m.shape[0], m.shape[0])] for part, m in zip(parts, MESSAGES, strict=True)]
    total = add_messages(parts, add_ref, total_ref)
    cover = add_messages(behind, add_ref, cover_ref)
    for p in range(2):
        rows = slice(p * 128, p * 128 + 128)
        for q in range(4):
            lanes = slice(q * LAT, q * LAT + LAT)
            below = 1.0 + cover[p][:, lanes]
            below_out[q, rows, :] = below
            cur_out[q, rows, :] = cur_ref[q, rows, :] * (1.0 + total[p][:, lanes]) / below
    to_messages(quads(cur_out), pick_ref, outs)


def update(pick, add, cur, cover, total, parts):
    whole = pl.BlockSpec(memory_space=pltpu.VMEM)
    return pl.pallas_call(
        update_kernel,
        in_specs=[whole] * 13,
        out_specs=[whole] * 10,
        out_shape=[jax.ShapeDtypeStruct((4, 256, LAT), F32)] * 2 + MESSAGES,
        compiler_params=params(16),
        name="update",
    )(pick, add, cur, cover, total, *parts)


def last_kernel(add_ref, cur_ref, below_ref, total_ref, *refs):
    totals, out_ref, rows_ref = refs[:8], refs[8], refs[9]
    total = add_messages(totals, add_ref, total_ref)
    for p in range(2):
        rows = slice(p * 128, p * 128 + 128)
        for q in range(4):
            mine = total[p][:, q * LAT : q * LAT + LAT]
            done = cur_ref[q, rows, :] * (1.0 + mine) / below_ref[q, rows, :]
            for m in range(16):
                rows_ref[pl.ds(m * 8 + p * 4 + q, 8, stride=128), :] = done[m * 8 : m * 8 + 8]
    done = rows_ref[...].reshape(32, 32, 128)
    for v in range(4):
        out_ref[:, v] = done


def last_update(add, cur, below, total):
    whole = pl.BlockSpec(memory_space=pltpu.VMEM)
    out = pl.pallas_call(
        last_kernel,
        in_specs=[whole] * 12,
        out_specs=whole,
        out_shape=jax.ShapeDtypeStruct((32, 4, 32, 128), F32),
        scratch_shapes=[pltpu.VMEM((1024, 128), F32)],
        compiler_params=params(14),
        name="last_update",
    )(add, cur, below, *total)
    return out.reshape(128, 32, 128)


def place_kernel(got_ref, out_ref, side_ref):
    got = got_ref.reshape(4096, 128)
    for k in range(4):
        y, z = row_place(pl.program_id(0) * 4 + k)
        for tx in range(2):
            rows = turn([got[pl.ds(y * 1024 + column_place(c) * 128 + z * 32 + tx, 16, stride=2), :] for c in range(8)])
            side = side_ref.at[k * 2 + tx]
            for s in range(8):
                side[pl.ds(s, 16, stride=8), :] = rows[s]
            lanes = slice(tx * 128, tx * 128 + 128)
            out_ref[:, :, 0, k * 8 : k * 8 + 8, lanes] = side[...].reshape(8, 2, 8, 128)


def place_output(got):
    out = pl.pallas_call(
        place_kernel,
        grid=(4,),
        in_specs=[pl.BlockSpec((4, 8, 4, 32, 128), lambda y: (0, 0, 0, 0, 0))],
        out_specs=pl.BlockSpec((8, 2, 1, 32, 256), lambda y: (0, 0, y, 0, 0)),
        out_shape=jax.ShapeDtypeStruct((8, 2, 4, 32, 256), F32),
        scratch_shapes=[pltpu.VMEM((8, 128, 128), F32)],
        compiler_params=params(20),
        name="place_output",
    )(got.reshape(4, 8, 4, 32, 128))
    return out.reshape(8, 256, 256)


def gather_parts(parts):
    return [lax.ppermute(x, ALL, towards(-er, -ec)) for x, (er, ec) in zip(parts, DIRS, strict=True)]


def reduce_parts(parts):
    return [lax.ppermute(x, ALL, towards(er, ec)) for x, (er, ec) in zip(parts, DIRS, strict=True)]


def on_device(estimate, tiles, tile_block, tile_view, tile_slot, widths):
    block, view = lax.axis_index("block"), lax.axis_index("view")
    y, x, core = block // 8, block // 2 % 4, block % 2
    outward = jnp.where(y % 2 == 0, y * 3 + view - 1, y * 3 + 3 - view)
    r = jnp.where(view == 0, 15 - y, outward)
    c = jnp.where(core == 0, x, 7 - x)
    at = jnp.stack([view, block % 4])
    send = small_message(at, estimate, tile_block, tile_view, tile_slot, widths)
    order, send = lax.optimization_barrier((view.reshape(1), send))
    small = lax.all_to_all(send, ALL, split_axis=0, concat_axis=0, tiled=True)
    send = tile_message(order, tiles[0])
    send, small = lax.optimization_barrier((send, small))
    got = lax.all_to_all(send, ALL, split_axis=0, concat_axis=0, tiled=True)

    add = (LANE_OWN[:, None] == np.arange(4 * LAT)[None, :]).astype(BF16)
    pick = (np.arange(4 * LAT)[:, None] == LANE_OWN[None, :]).astype(BF16)
    wrap_r = ((r + ER < 0) | (r + ER >= PR)).astype(jnp.int32) * ER
    wrap_c = ((c + EC < 0) | (c + EC >= PC)).astype(jnp.int32) * EC
    ty, tx = LANE_Q // 2 - wrap_r, LANE_Q % 2 - wrap_c
    inside = (LANE_Q >= 0) & (ty >= 0) & (ty < 2) & (tx >= 0) & (tx < 2)
    target = jnp.where(inside, (ty * 2 + tx) * HALO_PAD + LANE_HALO, -1)
    enter = (target[:, None] == jnp.arange(4 * HALO_PAD)[None, :]).astype(BF16)
    leave = (jnp.arange(4 * HALO_PAD)[:, None] == target[None, :]).astype(BF16)

    cur, *sent = begin(small, pick)
    parts = gather_parts(sent)
    spread = small[0:4, 9:12, 0:2].transpose(1, 0, 2).reshape(3, 8, 1)
    steps = jnp.arange(RAD + 1).astype(F32)
    raw = jnp.exp(-steps * steps / (2.0 * spread * spread))
    taps = raw / (2.0 * jnp.sum(raw, axis=2, keepdims=True) - raw[:, :, 0:1])
    weights = make_weights(taps)
    got, weights, taps = lax.optimization_barrier((got, weights, taps))
    obs = observe(got, small)
    obs, corners = lax.optimization_barrier((obs, parts[4:]))
    covered, *beside = cover(taps, obs, weights[1], leave)
    parts = parts[:4] + list(corners)
    own, *sent = sweep(taps, obs, weights, enter, leave, cur, parts, beside)
    cur, below, *sent = update(pick, add, cur, covered, own, reduce_parts(sent))
    parts = gather_parts(sent)
    own, *sent = sweep(taps, obs, weights, enter, leave, cur, parts)
    total = [own] + reduce_parts(sent)
    out = last_update(add, cur, below, total)
    out = lax.all_to_all(out, ALL, split_axis=0, concat_axis=0, tiled=True)
    return place_output(out)


def solution(mesh):
    placed = (
        P("block", None, None),
        P("view", "block", None, None, None),
        P("view", "block", None),
        P("view", "block"),
        P("view", "block"),
        P(None, "view"),
    )
    return jax.shard_map(
        on_device, mesh=mesh, in_specs=placed, out_specs=P("block", None, None), check_vma=False
    )
```

```python
import jax
import jax.numpy as jnp
import numpy as np
from jax import lax
from jax.experimental import pallas as pl
from jax.experimental.pallas import tpu as pltpu
from jax.sharding import PartitionSpec as P

RAD = 3
ITERS = 2
ALL = ("block", "view")
PR, PC = 16, 8
SR, SC = 8, 16
LAT = SR * SC
HALO_PAD = 256
EXT = LAT + HALO_PAD
F32, BF16 = jnp.float32, jnp.bfloat16

DIRS = [(0, -1), (0, 1), (-1, 0), (1, 0), (-1, -1), (-1, 1), (1, -1), (1, 1)]


def part_range(step, size):
    if step < 0:
        return list(range(-RAD, 0))
    if step > 0:
        return list(range(size, size + RAD))
    return list(range(size))


PARTS = [[(dr, dc) for dr in part_range(er, SR) for dc in part_range(ec, SC)] for er, ec in DIRS]
SIZES = [len(part) for part in PARTS]
HALO_AT = [sum(SIZES[:n]) for n in range(8)]
EXT_POS = [(s, j) for s in range(SR) for j in range(SC)] + [pos for part in PARTS for pos in part]
EXT_POS = EXT_POS + [(1000, 1000)] * (EXT - len(EXT_POS))


def row_place(r):
    y, k = r // 3, r % 3
    turned = y % 2
    z = 1 + k + turned * (2 - 2 * k)
    home = r // 12
    return y + home * (15 - r - y), z - home * z


def column_place(c):
    core = c // 4
    return (c % 4 + core * (3 - 2 * (c % 4))) * 2 + core


def device_of(r, c):
    y, z = row_place(r % PR)
    return (y * 8 + column_place(c % PC)) * 4 + z


def towards(er, ec):
    return [(device_of(r, c), device_of(r + er, c + ec)) for r in range(PR) for c in range(PC)]


def lane_table():
    main = [[-1] * 128 for _ in range(4)]
    aux = [[[-1] * 128 for _ in range(6)] for _ in range(2)]
    for n in range(8):
        for lane in range(4 * SIZES[n]):
            if n < 4 and lane < 128:
                main[n][lane] = (n, lane)
            else:
                for p in range(2):
                    if n < 4:
                        aux[p][n - 2][p * 64 + lane - 128] = (n, lane)
                    else:
                        aux[p][n - 2][p * 36 + lane] = (n, lane)
    return [x for row in main for x in row] + [x for kind in aux for row in kind for x in row]


LANES = lane_table()
LANE_N = np.array([0 if x == -1 else x[0] for x in LANES])
LANE_Q = np.array([-100 if x == -1 else x[1] // SIZES[x[0]] for x in LANES])
LANE_HALO = np.array([0 if x == -1 else HALO_AT[x[0]] + x[1] % SIZES[x[0]] for x in LANES])
LANE_OWN = np.array(
    [
        -1
        if x == -1
        else (x[1] // SIZES[x[0]]) * LAT
        + (PARTS[x[0]][x[1] % SIZES[x[0]]][0] % SR) * SC
        + PARTS[x[0]][x[1] % SIZES[x[0]]][1] % SC
        for x in LANES
    ]
)
ER = np.array([d[0] for d in DIRS])[LANE_N]
EC = np.array([d[1] for d in DIRS])[LANE_N]
N_MAIN, N_AUX = 512, 768


def params(mib):
    return pltpu.CompilerParams(vmem_limit_bytes=mib << 20)


def turn(rows):
    chunk = lax.broadcasted_iota(jnp.int32, rows[0].shape, 1) // SC
    for k in (4, 2, 1):
        low = (chunk & k) == 0
        after = list(rows)
        for a in range(8):
            if a & k == 0:
                x, y = rows[a], rows[a | k]
                after[a] = jnp.where(low, x, pltpu.roll(y, SC * k, 1))
                after[a | k] = jnp.where(low, pltpu.roll(x, 128 - SC * k, 1), y)
        rows = after
    return rows


def split(x):
    high = x.astype(BF16)
    return high, (x - high.astype(F32)).astype(BF16)


def dot(a, b):
    return jnp.dot(a, b, preferred_element_type=F32)


def send_small_kernel(view_ref, left_ref, right_ref, meta_ref, out_ref):
    left, right = left_ref.reshape(128, 128), right_ref.reshape(128, 128)
    for k in range(4):
        y, z = row_place(pl.program_id(0) * 4 + k)
        rows = []
        for s in range(8):
            at = pl.ds(k * 8 + s, 4, stride=32)
            rows.append(jnp.concatenate([left[at, :], right[at, :]], axis=0))
        rows = turn(rows)
        for c in range(8):
            out_ref[y, column_place(c), z, 0:8, :] = rows[c]
            out_ref[y, column_place(c), z, 8:16, :] = meta_ref[...]


def small_message(view, estimate, meta):
    estimate = estimate.reshape(8, 2, 4, 32, 256)
    out = pl.pallas_call(
        send_small_kernel,
        grid_spec=pltpu.PrefetchScalarGridSpec(
            num_scalar_prefetch=1,
            grid=(4,),
            in_specs=[
                pl.BlockSpec((2, 2, 1, 32, 128), lambda y, v: (v[0], 0, y, 0, 0)),
                pl.BlockSpec((2, 2, 1, 32, 128), lambda y, v: (v[0], 0, y, 0, 1)),
                pl.BlockSpec((8, 128), lambda y, v: (0, 0)),
            ],
            out_specs=pl.BlockSpec((4, 8, 4, 16, 128), lambda y, v: (0, 0, 0, 0, 0)),
        ),
        out_shape=jax.ShapeDtypeStruct((4, 8, 4, 16, 128), F32),
        compiler_params=params(56),
        name="small_message",
    )(view, estimate, estimate, meta)
    return out.reshape(128, 16, 128)


def send_tiles_kernel(view_ref, tiles_ref, out_ref):
    tiles = tiles_ref.reshape(2048, 128)
    for k in range(4):
        y, z = row_place(pl.program_id(0) * 4 + k)
        for p in range(2):
            rows = turn([tiles[pl.ds(p * 32 + k * 8 + s, 32, stride=64), :] for s in range(8)])
            for c in range(8):
                out_ref[y, column_place(c), z, p * 32 : p * 32 + 32, :] = rows[c]


def tile_message(view, tiles):
    out = pl.pallas_call(
        send_tiles_kernel,
        grid_spec=pltpu.PrefetchScalarGridSpec(
            num_scalar_prefetch=1,
            grid=(4,),
            in_specs=[pl.BlockSpec((32, 2, 32, 128), lambda y, v: (0, 0, y, 0))],
            out_specs=pl.BlockSpec((4, 8, 4, 64, 128), lambda y, v: (0, 0, 0, 0, 0)),
        ),
        out_shape=jax.ShapeDtypeStruct((4, 8, 4, 64, 128), F32),
        compiler_params=params(56),
        cost_estimate=pl.CostEstimate(flops=1 << 20, bytes_accessed=24 << 20, transcendentals=0),
        name="tile_message",
    )(view, tiles)
    return out.reshape(128, 64, 128)


def stacked(x):
    return jnp.concatenate(split(x), axis=0)


def dot_halves(x, table):
    out = dot(x, table)
    rows = out.shape[0] // 2
    return out[:rows] + out[rows:]


def aux_at(p):
    return slice(N_MAIN + p * N_AUX, N_MAIN + (p + 1) * N_AUX)


def to_messages(x, table_ref, outs):
    main = dot_halves(stacked(x), table_ref[:, :N_MAIN])
    aux = dot_halves(stacked(x[:128]), table_ref[:, aux_at(0)]) + dot_halves(stacked(x[128:]), table_ref[:, aux_at(1)])
    put_messages(main, aux, outs)


def from_messages(parts, table_ref):
    main = jnp.concatenate([parts[n][0:256, :] for n in range(4)], axis=1)
    aux = jnp.concatenate([parts[n][256:384, :] for n in (2, 3)] + [parts[n][0:128, :] for n in range(4, 8)], axis=1)
    main = dot_halves(stacked(main), table_ref[:N_MAIN, :])
    aux = stacked(aux)
    return [main[p * 128 : p * 128 + 128] + dot_halves(aux, table_ref[aux_at(p), :]) for p in range(2)]


def put_messages(main, aux, outs):
    for n in range(4):
        outs[n][0:256, :] = main[:, n * 128 : n * 128 + 128]
        if n >= 2:
            outs[n][256:384, :] = aux[:, (n - 2) * 128 : (n - 2) * 128 + 128]
    for n in range(4, 8):
        outs[n][0:128, :] = aux[:, (n - 2) * 128 : (n - 2) * 128 + 128]


MESSAGES = [jax.ShapeDtypeStruct((rows, 128), F32) for rows in (256, 256, 384, 384, 128, 128, 128, 128)]


def add_messages(parts, table_ref, base):
    out = []
    for p, term in enumerate(from_messages(parts, table_ref)):
        out.append(term + jnp.concatenate([base[q, p * 128 : p * 128 + 128, :] for q in range(4)], axis=1))
    return out


def quads(x):
    return jnp.concatenate([x[q] for q in range(4)], axis=1)


def begin_kernel(got_ref, pick_ref, cur_ref, *outs):
    got = got_ref.reshape(128 * 16, 128)
    for q in range(4):
        for p in range(2):
            row = (q % 2) * 4 + p * 2 + q // 2
            for m in range(16):
                at = p * 128 + m * 8
                cur_ref[q, at : at + 8, :] = got[pl.ds(m * 16 + row, 8, stride=256), :]
    to_messages(quads(cur_ref), pick_ref, outs)


def begin(got, pick):
    return pl.pallas_call(
        begin_kernel,
        grid=(1,),
        in_specs=[
            pl.BlockSpec((128, 16, 128), lambda i: (0, 0, 0)),
            pl.BlockSpec((512, N_MAIN + 2 * N_AUX), lambda i: (0, 0)),
        ],
        out_specs=[pl.BlockSpec((4, 256, 128), lambda i: (0, 0, 0))]
        + [pl.BlockSpec(m.shape, lambda i: (0, 0)) for m in MESSAGES],
        out_shape=[jax.ShapeDtypeStruct((4, 256, 128), F32)] + MESSAGES,
        compiler_params=params(16),
        name="begin",
    )(got, pick)


def weight_kernel(taps_ref, er_ref, ec_ref, ert_ref, ect_ref, fore_ref, back_ref):
    def from_taps(apart, axis, w):
        far = jnp.abs(apart)
        out = jnp.zeros(apart.shape, F32)
        for k in range(RAD + 1):
            out = jnp.where(far == k, taps_ref[axis, w, k], out)
        return out

    lanes = lax.broadcasted_iota(jnp.int32, (EXT, LAT), 1)
    down, across = er_ref[...] - lanes // SC, ec_ref[...] - lanes % SC
    rows = lax.broadcasted_iota(jnp.int32, (LAT, EXT), 0)
    down_t, across_t = ert_ref[...] - rows // SC, ect_ref[...] - rows % SC
    for w in range(8):
        pair, at = w // 2, slice((w % 2) * LAT, (w % 2) * LAT + LAT)
        high, low = split(from_taps(down, 1, w) * from_taps(across, 2, w))
        for i, x in enumerate((high, high, low)):
            fore_ref[pair, i * EXT : i * EXT + EXT, at] = x
        high, low = split(from_taps(down_t, 1, w) * from_taps(across_t, 2, w))
        for i, x in enumerate((high, high, low)):
            start = i * 2 * LAT + (w % 2) * LAT
            back_ref[pair, start : start + LAT, :] = x


def make_weights(taps):
    ext = np.array(EXT_POS, np.int32)
    tall = [np.broadcast_to(ext[:, i][:, None], (EXT, LAT)) for i in range(2)]
    wide = [np.broadcast_to(ext[:, i][None, :], (LAT, EXT)) for i in range(2)]
    whole = pl.BlockSpec(memory_space=pltpu.VMEM)
    return pl.pallas_call(
        weight_kernel,
        in_specs=[pl.BlockSpec(memory_space=pltpu.SMEM)] + [whole] * 4,
        out_specs=[whole] * 2,
        out_shape=[
            jax.ShapeDtypeStruct((4, 3 * EXT, 2 * LAT), BF16),
            jax.ShapeDtypeStruct((4, 6 * LAT, EXT), BF16),
        ],
        compiler_params=params(20),
        name="make_weights",
    )(taps, *tall, *wide)


def observe_kernel(got_ref, meta_ref, obs_ref):
    sides = []
    for p in range(2):
        sides.append(got_ref[:, 0, p * 32 : p * 32 + 32, :].reshape(1024, 128))
    high, low = split(jnp.concatenate(sides, axis=1))
    lanes = []
    for i in range(0, 32, 4):
        lanes.append(sum(meta_ref[i + k, 0, 0:1, :] for k in range(1, 4)) + meta_ref[i, 0, 0:1, :])
    place = jnp.concatenate(lanes, axis=1)
    for half in range(4):
        rows = lax.broadcasted_iota(jnp.int32, (256, 1024), 0) + half * 256
        hot = (rows.astype(F32) == place).astype(F32)
        counts = jnp.sum(hot, axis=1, keepdims=True)
        hot = hot.astype(BF16)
        mean = (dot(hot, high) + dot(hot, low)) / jnp.maximum(counts, 1.0)
        for i in range(2):
            for p in range(2):
                obs_ref[half // 2, (half % 2) * 2 + i, p * 128 : p * 128 + 128, :] = mean[
                    i * 128 : i * 128 + 128, p * 128 : p * 128 + 128
                ]


def observe(got, small):
    got = got.reshape(32, 4, 64, 128)
    small = small.reshape(32, 4, 16, 128)
    return pl.pallas_call(
        observe_kernel,
        grid=(4,),
        in_specs=[
            pl.BlockSpec((32, 1, 64, 128), lambda g: (0, g, 0, 0)),
            pl.BlockSpec((32, 1, 8, 128), lambda g: (0, g, 1, 0)),
        ],
        out_specs=pl.BlockSpec((2, 4, 256, 128), lambda g: (g, 0, 0, 0)),
        out_shape=jax.ShapeDtypeStruct((8, 4, 256, 128), F32),
        compiler_params=params(20),
        cost_estimate=pl.CostEstimate(flops=4 << 30, bytes_accessed=8 << 20, transcendentals=0),
        name="observe",
    )(got, small)


def depth_blur(x, taps):
    rows = [None] * 32
    for p in range(2):
        for m in range(16):
            rows[2 * m + p] = x[p * 128 + m * 8 : p * 128 + m * 8 + 8]
    layer = lax.broadcasted_iota(jnp.int32, rows[0].shape, 0)
    before = [jnp.where(layer == 0, 0.0, pltpu.roll(rows[32 - k], 1, 0)) for k in (3, 2, 1)]
    after = [jnp.where(layer == 7, 0.0, pltpu.roll(rows[k], 7, 0)) for k in (0, 1, 2)]
    e = before + rows + after
    out = [
        taps[0] * e[z + 3]
        + taps[1] * (e[z + 2] + e[z + 4])
        + (taps[2] * (e[z + 1] + e[z + 5]) + taps[3] * (e[z] + e[z + 6]))
        for z in range(32)
    ]
    return jnp.concatenate([out[2 * m + p] for p in range(2) for m in range(16)], axis=0)


def back_project(blurred, back_ref, total):
    def step(pair):
        rows = []
        for x in blurred(pair):
            halves = [split(side) for side in x]
            high = [h for h, _ in halves]
            low = [l for _, l in halves]
            rows.append(jnp.concatenate(high + low + high, axis=1))
        return jnp.concatenate(rows, axis=0)

    sides = [step(pair) for pair in range(4)]
    total[...] = dot(jnp.concatenate(sides, axis=1), back_ref[...].reshape(4 * 6 * LAT, EXT))


def finish_back(total, out_ref, own_ref, outs):
    for q in range(4):
        own_ref[q] = total[q * 256 : q * 256 + 256, :LAT]
    halo = jnp.concatenate([total[q * 256 : q * 256 + 256, LAT:] for q in range(4)], axis=1)
    to_messages(halo, out_ref, outs)


def cover_kernel(taps_ref, obs_ref, back_ref, out_ref, own_ref, *rest):
    outs, total = rest[:8], rest[8]

    def blurred(pair):
        for q in range(4):
            sides = []
            for i in range(2):
                taps = [taps_ref[0, 2 * pair + i, k] for k in range(RAD + 1)]
                sides.append(depth_blur((obs_ref[2 * pair + i, q] > 0.0).astype(F32), taps))
            yield sides

    back_project(blurred, back_ref, total)
    finish_back(total, out_ref, own_ref, outs)


def cover(taps, obs, back, leave):
    whole = pl.BlockSpec(memory_space=pltpu.VMEM)
    return pl.pallas_call(
        cover_kernel,
        in_specs=[pl.BlockSpec(memory_space=pltpu.SMEM)] + [whole] * 3,
        out_specs=[whole] * 9,
        out_shape=[jax.ShapeDtypeStruct((4, 256, LAT), F32)] + MESSAGES,
        scratch_shapes=[pltpu.VMEM((1024, EXT), F32)],
        compiler_params=params(20),
        cost_estimate=pl.CostEstimate(flops=6 << 30, bytes_accessed=8 << 20, transcendentals=0),
        name="cover",
    )(taps, obs, back, leave)


def sweep_kernel(taps_ref, obs_ref, fore_ref, back_ref, enter_ref, leave_ref, cur_ref, *refs):
    parts, beside, own_ref, outs = refs[:8], refs[8:-11], refs[-11], refs[-10:-2]
    total, ext = refs[-2:]
    for message, out in zip(beside, outs, strict=False):
        rows = message.shape[0]
        out[rows : 2 * rows, :] = message[...]

    def put(rows, at, x):
        high, low = split(x)
        for i, half in enumerate((high, low, high)):
            ext[rows, i * EXT + at : i * EXT + at + x.shape[1]] = half

    for q in range(4):
        put(slice(q * 256, q * 256 + 256), 0, cur_ref[q])
    for p, halo in enumerate(from_messages(parts, enter_ref)):
        for q in range(4):
            start = q * 256 + p * 128
            put(slice(start, start + 128), LAT, halo[:, q * HALO_PAD : (q + 1) * HALO_PAD])

    def blurred(pair):
        across = dot(ext[...], fore_ref[pair])
        for q in range(4):
            sides = []
            for i in range(2):
                w = 2 * pair + i
                taps = [taps_ref[0, w, k] for k in range(RAD + 1)]
                blur = depth_blur(across[q * 256 : q * 256 + 256, i * LAT : i * LAT + LAT], taps)
                near = pl.reciprocal(blur, approx=True)
                near = near * (2.0 - blur * near)
                sides.append(depth_blur(obs_ref[w, q] * near, taps))
            yield sides

    back_project(blurred, back_ref, total)
    finish_back(total, leave_ref, own_ref, outs)


def sweep(taps, obs, weights, enter, leave, cur, parts, beside=()):
    messages = [jax.ShapeDtypeStruct((m.shape[0] * (2 if beside else 1), 128), F32) for m in MESSAGES]
    whole = pl.BlockSpec(memory_space=pltpu.VMEM)
    return pl.pallas_call(
        sweep_kernel,
        in_specs=[pl.BlockSpec(memory_space=pltpu.SMEM)] + [whole] * (14 + len(beside)),
        out_specs=[whole] * 9,
        out_shape=[jax.ShapeDtypeStruct((4, 256, LAT), F32)] + messages,
        scratch_shapes=[pltpu.VMEM((1024, EXT), F32), pltpu.VMEM((1024, 3 * EXT), BF16)],
        compiler_params=params(26),
        cost_estimate=pl.CostEstimate(flops=12 << 30, bytes_accessed=12 << 20, transcendentals=0),
        name="sweep",
    )(taps, obs, *weights, enter, leave, cur, *parts, *beside)


def update_kernel(pick_ref, add_ref, cur_ref, cover_ref, total_ref, *refs):
    parts, cur_out, below_out, outs = refs[:8], refs[8], refs[9], refs[10:18]
    behind = [part.at[pl.ds(m.shape[0], m.shape[0])] for part, m in zip(parts, MESSAGES, strict=True)]
    total = add_messages(parts, add_ref, total_ref)
    cover = add_messages(behind, add_ref, cover_ref)
    for p in range(2):
        rows = slice(p * 128, p * 128 + 128)
        for q in range(4):
            lanes = slice(q * LAT, q * LAT + LAT)
            below = 1.0 + cover[p][:, lanes]
            below_out[q, rows, :] = below
            cur_out[q, rows, :] = cur_ref[q, rows, :] * (1.0 + total[p][:, lanes]) / below
    to_messages(quads(cur_out), pick_ref, outs)


def update(pick, add, cur, cover, total, parts):
    whole = pl.BlockSpec(memory_space=pltpu.VMEM)
    return pl.pallas_call(
        update_kernel,
        in_specs=[whole] * 13,
        out_specs=[whole] * 10,
        out_shape=[jax.ShapeDtypeStruct((4, 256, LAT), F32)] * 2 + MESSAGES,
        compiler_params=params(16),
        name="update",
    )(pick, add, cur, cover, total, *parts)


def last_kernel(add_ref, cur_ref, below_ref, total_ref, *refs):
    totals, out_ref, rows_ref = refs[:8], refs[8], refs[9]
    total = add_messages(totals, add_ref, total_ref)
    for p in range(2):
        rows = slice(p * 128, p * 128 + 128)
        for q in range(4):
            mine = total[p][:, q * LAT : q * LAT + LAT]
            done = cur_ref[q, rows, :] * (1.0 + mine) / below_ref[q, rows, :]
            for m in range(16):
                rows_ref[pl.ds(m * 8 + p * 4 + q, 8, stride=128), :] = done[m * 8 : m * 8 + 8]
    done = rows_ref[...].reshape(32, 32, 128)
    for v in range(4):
        out_ref[:, v] = done


def last_update(add, cur, below, total):
    whole = pl.BlockSpec(memory_space=pltpu.VMEM)
    out = pl.pallas_call(
        last_kernel,
        in_specs=[whole] * 12,
        out_specs=whole,
        out_shape=jax.ShapeDtypeStruct((32, 4, 32, 128), F32),
        scratch_shapes=[pltpu.VMEM((1024, 128), F32)],
        compiler_params=params(14),
        name="last_update",
    )(add, cur, below, *total)
    return out.reshape(128, 32, 128)


def place_kernel(got_ref, out_ref, side_ref):
    got = got_ref.reshape(4096, 128)
    for k in range(4):
        y, z = row_place(pl.program_id(0) * 4 + k)
        for tx in range(2):
            rows = turn([got[pl.ds(y * 1024 + column_place(c) * 128 + z * 32 + tx, 16, stride=2), :] for c in range(8)])
            side = side_ref.at[k * 2 + tx]
            for s in range(8):
                side[pl.ds(s, 16, stride=8), :] = rows[s]
            lanes = slice(tx * 128, tx * 128 + 128)
            out_ref[:, :, 0, k * 8 : k * 8 + 8, lanes] = side[...].reshape(8, 2, 8, 128)


def place_output(got):
    out = pl.pallas_call(
        place_kernel,
        grid=(4,),
        in_specs=[pl.BlockSpec((4, 8, 4, 32, 128), lambda y: (0, 0, 0, 0, 0))],
        out_specs=pl.BlockSpec((8, 2, 1, 32, 256), lambda y: (0, 0, y, 0, 0)),
        out_shape=jax.ShapeDtypeStruct((8, 2, 4, 32, 256), F32),
        scratch_shapes=[pltpu.VMEM((8, 128, 128), F32)],
        compiler_params=params(20),
        name="place_output",
    )(got.reshape(4, 8, 4, 32, 128))
    return out.reshape(8, 256, 256)


def gather_parts(parts):
    return [lax.ppermute(x, ALL, towards(-er, -ec)) for x, (er, ec) in zip(parts, DIRS, strict=True)]


def reduce_parts(parts):
    return [lax.ppermute(x, ALL, towards(er, ec)) for x, (er, ec) in zip(parts, DIRS, strict=True)]


def on_device(estimate, tiles, tile_block, tile_view, tile_slot, widths):
    block, view = lax.axis_index("block"), lax.axis_index("view")
    y, x, core = block // 8, block // 2 % 4, block % 2
    outward = jnp.where(y % 2 == 0, y * 3 + view - 1, y * 3 + 3 - view)
    r = jnp.where(view == 0, 15 - y, outward)
    c = jnp.where(core == 0, x, 7 - x)
    slot = tile_slot[0]
    deep = tile_block[0, :, 0] * 4 + slot // 4
    place = tile_view[0] * 512 + (slot % 4) * 128 + (deep % 16) * 8 + deep // 16
    place = jnp.where(jnp.arange(128) // 32 == block % 4, jnp.tile(place.astype(F32), 4), 0.0)
    own_widths = jnp.pad(widths.reshape(1, 6), ((1, 6), (0, 122)))
    meta = jnp.where(jnp.arange(8)[:, None] == 0, place[None, :], own_widths)
    send = small_message(view.reshape(1), estimate, meta)
    order, send = lax.optimization_barrier((view.reshape(1), send))
    small = lax.all_to_all(send, ALL, split_axis=0, concat_axis=0, tiled=True)
    send = tile_message(order, tiles[0])
    send, small = lax.optimization_barrier((send, small))
    got = lax.all_to_all(send, ALL, split_axis=0, concat_axis=0, tiled=True)

    add = (LANE_OWN[:, None] == np.arange(4 * LAT)[None, :]).astype(BF16)
    pick = (np.arange(4 * LAT)[:, None] == LANE_OWN[None, :]).astype(BF16)
    wrap_r = ((r + ER < 0) | (r + ER >= PR)).astype(jnp.int32) * ER
    wrap_c = ((c + EC < 0) | (c + EC >= PC)).astype(jnp.int32) * EC
    ty, tx = LANE_Q // 2 - wrap_r, LANE_Q % 2 - wrap_c
    inside = (LANE_Q >= 0) & (ty >= 0) & (ty < 2) & (tx >= 0) & (tx < 2)
    target = jnp.where(inside, (ty * 2 + tx) * HALO_PAD + LANE_HALO, -1)
    enter = (target[:, None] == jnp.arange(4 * HALO_PAD)[None, :]).astype(BF16)
    leave = (jnp.arange(4 * HALO_PAD)[:, None] == target[None, :]).astype(BF16)

    cur, *sent = begin(small, pick)
    parts = gather_parts(sent)
    spread = small[0:4, 9, 0:6].reshape(4, 3, 2).transpose(1, 0, 2).reshape(3, 8, 1)
    steps = jnp.arange(RAD + 1).astype(F32)
    raw = jnp.exp(-steps * steps / (2.0 * spread * spread))
    taps = raw / (2.0 * jnp.sum(raw, axis=2, keepdims=True) - raw[:, :, 0:1])
    weights = make_weights(taps)
    got, weights, taps = lax.optimization_barrier((got, weights, taps))
    obs = observe(got, small)
    covered, *beside = cover(taps, obs, weights[1], leave)
    own, *sent = sweep(taps, obs, weights, enter, leave, cur, parts, beside)
    cur, below, *sent = update(pick, add, cur, covered, own, reduce_parts(sent))
    parts = gather_parts(sent)
    own, *sent = sweep(taps, obs, weights, enter, leave, cur, parts)
    total = [own] + reduce_parts(sent)
    out = last_update(add, cur, below, total)
    out = lax.all_to_all(out, ALL, split_axis=0, concat_axis=0, tiled=True)
    return place_output(out)


def solution(mesh):
    placed = (
        P("block", None, None),
        P("view", "block", None, None, None),
        P("view", "block", None),
        P("view", "block"),
        P("view", "block"),
        P(None, "view"),
    )
    return jax.shard_map(
        on_device, mesh=mesh, in_specs=placed, out_specs=P("block", None, None), check_vma=False
    )
```
